32 devices in a mesh: expert: 4 (over z), context: 4 (over x, core), dp: 2 (over y).
Axes of the slice: x: 2, y: 2, z: 4, core: 2. Of those that a mesh axis runs over, the one named last changes fastest.
Arguments:
- tokens: bfloat16 [16, 640, 768], P(('expert', 'dp'), 'context'), may hold values from -6 to 6
- lengths: int32 [16, 4], P(('expert', 'dp')), may hold values from 1 to 160, 577 in all within a row
- route_ids: int32 [16, 640, 2], P(('expert', 'dp'), 'context'), may hold values from 0 to 3, all different within a row; in each aligned block of 160 rows (0 to 159, 160 to 319, ..., all dimensions but the last counted through in order) at most 128 rows name the same one
- keep_mask: int32 [16, 640, 2], P(('expert', 'dp'), 'context'), may hold values 0 or 1
- w_qkv: bfloat16 [768, 2304], P(('expert', 'dp')), may hold values from -0.21875 to 0.21875
- w_attn_out: bfloat16 [768, 768], P(('expert', 'dp')), may hold values from -6 to 6
- w_router: bfloat16 [768, 4], P(('expert', 'dp')), may hold values from -0.375 to 0.375
- norm_gains: bfloat16 [2, 768], P(None, ('expert', 'dp')), may hold values from 0.25 to 1.75
- norm_biases: bfloat16 [2, 768], P(None, ('expert', 'dp')), may hold values from -1 to 1
- w_expert_in: bfloat16 [4, 768, 3072], P('expert'), may hold values from -0.21875 to 0.21875
- w_expert_down: bfloat16 [4, 3072, 768], P('expert'), may hold values from -1 to 1
- cotangent: bfloat16 [16, 640, 768], P(('expert', 'dp'), 'context'), may hold values from -6 to 6
Outputs:
- output: bfloat16 [16, 640, 768], P(('expert', 'dp'), 'context')
- grad_tokens: float32 [16, 640, 768], P(('expert', 'dp'), 'context')
- grad_qkv: float32 [768, 2304], P(('expert', 'dp'))
- grad_attn_out: float32 [768, 768], P(('expert', 'dp'))
- grad_router: float32 [768, 4], P(('expert', 'dp'))
- grad_gains: float32 [2, 768], P(None, ('expert', 'dp'))
- grad_biases: float32 [2, 768], P(None, ('expert', 'dp'))
- grad_expert_in: float32 [4, 768, 3072], P('expert', None, ('context', 'dp'))
- grad_expert_down: float32 [4, 3072, 768], P('expert', ('context', 'dp'))
The draws below stay inside these ranges and needn't reach their ends.
Inputs may be any that keep to these rules, and one draw needn't show every extreme that they name: `route_ids`: each row names two different experts; in each aligned block of 160 rows (one image's block of slots) no expert is named more than 128 times. An image's 4 block lengths sum to 577; the largest is exactly 160.
All inputs are finite; a program needn't handle non-finite values. No bound on the sum of `keep_mask` on one device may be relied on, other than what follows from the above.
Results may differ from the reference program's by a relative error of at most 0.017.
Values may be sent and summed in bfloat16 or wider, within the bound.
A program may use at most 192 MiB of HBM per device.

```python
import math
import jax
import jax.numpy as jnp
import numpy as np
from jax import lax

D = 768
HEADS = 12
HEAD_DIM = 64
FF = 3072
EXPERTS = 4
SEQ = 577
BLK = 160
SLOTS = 640
IMAGES = 16
CAP = 128
N_CONTEXT = 4


def with_ends(array, own_key, smallest, top_value):
    shape = array.shape
    spot = [jax.random.randint(jax.random.fold_in(own_key, axis), (), 0, shape[axis]) for axis in range(len(shape))]
    array = array.at[tuple(spot)].set(smallest)
    longest = shape.index(max(shape))
    spot[longest] = (spot[longest] + 1) % shape[longest]
    return array.at[tuple(spot)].set(top_value)


def steps_of(own_key, extent, shards, smallest, largest):
    factor_of, own = 1.0, jax.random.fold_in(own_key, 6)
    for axis_at, shards_of in shards:
        heights = jnp.exp(jax.random.uniform(jax.random.fold_in(own, axis_at), (shards_of,), jnp.float32, smallest / len(shards), largest / len(shards)))
        factor_of = factor_of * jnp.repeat(heights, extent[axis_at] // shards_of).reshape([-1 if axis == axis_at else 1 for axis in range(len(extent))])
    return factor_of


def profile(count, total, limit, slope):
    loads = [(1 << 20) // math.isqrt(grade ** slope) + 1 for grade in range(2, count + 1)]
    rest, counts = total - limit - (count - 1), [1] * (count - 1)
    while rest > 0:
        free = [i for i in range(count - 1) if counts[i] < limit]
        pool, remaining = sum([loads[i] for i in free]), rest
        for i in free:
            extra = min(limit - counts[i], max(1, remaining * loads[i] // pool), rest)
            counts[i] = counts[i] + extra
            rest = rest - extra
    return np.array([limit] + counts)


def ragged_sizes(own_key, amount, total, limit, slope):
    if amount == 2:
        one = jax.random.randint(own_key, (), max(1, total - limit), min(limit, total - 1) + 1)
        return jnp.stack([one, total - one])
    sizes = jnp.asarray(profile(amount, total, limit, slope), jnp.int32)
    couples = (amount - 1) // 2
    donor, receiver = sizes[1:1 + 2 * couples:2], sizes[2:2 + 2 * couples:2]
    room = jnp.minimum(donor - 1, limit - receiver)
    shifted = jax.random.randint(jax.random.fold_in(own_key, 1), (couples,), 0, 1 << 20) % (room + 1)
    sizes = sizes.at[1:1 + 2 * couples:2].set(donor - shifted).at[2:2 + 2 * couples:2].set(receiver + shifted)
    return sizes[jax.random.permutation(jax.random.fold_in(own_key, 2), amount)]


def shared_out(key, own, number, rows, number_of, top, bound, skew):
    order = jax.random.permutation(key, number_of)
    crowded, ordinary = load_shares(number_of, rows * top, bound, skew, True), load_shares(number_of, rows * top, bound, skew, False)
    places = jnp.arange(number_of)

    def named(sizes, turn):
        used = int((sizes > 0).sum())
        fixed = max(1, used // 4)
        shifted = fixed + (places - fixed + turn * (used - fixed)) % max(1, number_of - fixed)
        return jnp.zeros((number_of,), jnp.int32).at[order[jnp.where(places < fixed, places, shifted)]].set(jnp.asarray(sizes, jnp.int32))

    sizes = jnp.where(number % 4 == 0, named(crowded, number // 4), named(ordinary, number - number // 4 - 1))
    mixed = jax.random.permutation(jax.random.fold_in(own, 3), number_of)
    giver, sink = mixed[0:number_of // 2 * 2:2], mixed[1:number_of // 2 * 2:2]
    margin = jnp.minimum(sizes[giver] - 1, bound - sizes[sink]) // 2
    margin = jnp.where((giver == order[0]) | (sink == order[0]) | (sizes[sink] == 0), 0, jnp.maximum(margin, 0))
    shifted = jax.random.randint(jax.random.fold_in(own, 4), (number_of // 2,), 0, 1 << 20) % (margin + 1)
    sizes = sizes.at[giver].add(-shifted).at[sink].add(shifted)
    items = jnp.searchsorted(jnp.cumsum(sizes), jnp.arange(rows * top), side="right").astype(jnp.int32)
    table = items.reshape(top, rows).T
    table = table[jax.random.permutation(jax.random.fold_in(own, 1), rows)]
    turn = jax.random.randint(jax.random.fold_in(own, 2), (rows, 1), 0, top)
    return jnp.take_along_axis(table, (jnp.arange(top)[None, :] + turn) % top, axis=1)


def load_shares(amount, total, bound, skew, full):
    loads = [(1 << 20) // math.isqrt(rank ** skew) + 1 for rank in range(1, amount + 1)]
    largest = bound if full else min(bound, max(-(-total // amount), total * loads[0] // sum(loads)))
    least = 1 if total - largest >= amount - 1 else 0
    counts, rest = [largest] + [least] * (amount - 1), total - largest - least * (amount - 1)
    while rest > 0:
        candidates = [i for i in range(1, amount) if counts[i] < largest] or [i for i in range(1, amount) if counts[i] < bound]
        mass, remaining = sum([loads[i] for i in candidates]), rest
        for i in candidates:
            extra = min(bound - counts[i], max(1, remaining * loads[i] // mass), rest)
            counts[i] = counts[i] + extra
            rest = rest - extra
    return np.array(counts)


def gaussian(rng, dims, scale, bound, split=(), kind=jnp.bfloat16):
    entries = scale * jax.random.normal(rng, dims, jnp.float32)
    if split:
        entries = entries * steps_of(rng, dims, split, -0.22, 0.18)
    return jnp.clip(entries, -bound, bound).astype(kind)


def setup_inputs(seed: int = 0) -> dict:
    key_list = jax.random.split(jax.random.key(seed), 13)
    tokens = gaussian(key_list[0], (IMAGES, SLOTS, D), 1.0, 6.0, ((0, 8), (1, 4)))
    lengths = jax.vmap(lambda own: ragged_sizes(own, N_CONTEXT, SEQ, BLK, 1))(jax.random.split(key_list[1], IMAGES)).reshape((IMAGES, N_CONTEXT)).astype(jnp.int32)
    route_ids_keys = jax.random.split(jax.random.fold_in(key_list[2], 1), IMAGES * SLOTS // BLK)
    route_ids_turns = jax.random.permutation(jax.random.fold_in(key_list[2], 3), IMAGES * SLOTS // BLK)
    route_ids = jax.vmap(lambda own, number: shared_out(jax.random.fold_in(key_list[2], 2), own, number, BLK, EXPERTS, 2, CAP, 1))(route_ids_keys, route_ids_turns).reshape((IMAGES, SLOTS, 2))
    keep_mask = with_ends((jax.random.randint(key_list[3], (IMAGES, SLOTS, 2), 0, 8) < 7).astype(jnp.int32), jax.random.fold_in(key_list[3], 1), 0, 1)
    w_qkv = gaussian(key_list[4], (D, 3 * D), D ** -0.5, 0.21875, ((0, 8),))
    w_attn_out = gaussian(key_list[5], (D, D), ((SEQ / D) ** 0.5 / 2), 6.0, ((0, 8),))
    w_router = gaussian(key_list[6], (D, EXPERTS), (0.75 / D ** 0.5), 0.375, ((0, 8),))
    norm_gains = jnp.clip(1.0 + 0.15 * jax.random.normal(key_list[7], (2, D), jnp.float32), 0.25, 1.75).astype(jnp.bfloat16)
    norm_biases = gaussian(key_list[8], (2, D), 0.2, 1.0, ((1, 8),))
    w_expert_in = gaussian(key_list[9], (EXPERTS, D, FF), D ** -0.5, 0.21875, ((0, 4),))
    w_expert_down = gaussian(key_list[10], (EXPERTS, FF, D), (EXPERTS / FF ** 0.5), 1.0, ((0, 4),))
    cotangent = gaussian(key_list[11], (IMAGES, SLOTS, D), 1.0, 6.0, ((0, 8), (1, 4)))
    return dict(tokens=tokens, lengths=lengths, route_ids=route_ids, keep_mask=keep_mask, w_qkv=w_qkv, w_attn_out=w_attn_out, w_router=w_router, norm_gains=norm_gains, norm_biases=norm_biases, w_expert_in=w_expert_in, w_expert_down=w_expert_down, cotangent=cotangent)


@jax.custom_vjp
def low(v):
    return lax.optimization_barrier(v.astype(jnp.bfloat16)).astype(jnp.float32)

@jax.custom_vjp
def low_back(v):
    return v

def low_keep(v):
    return (low(v), None)

def low_pass(kept, grad):
    return (grad,)

def back_keep(v):
    return (v, None)

def back_low(kept, grad):
    return (low(grad),)
low.defvjp(low_keep, low_pass)
low_back.defvjp(back_keep, back_low)
epsilon = 1e-06
precise = lax.Precision.HIGHEST

def layer_norm(values, gain, shift):
    centred = values - lax.optimization_barrier(jnp.mean(values, axis=-1, keepdims=True))
    variance = lax.optimization_barrier(jnp.mean(centred * centred, axis=-1, keepdims=True))
    return centred * lax.rsqrt(variance + epsilon) * gain + shift

def slot_ranks(route_ids, n_experts):
    image_count, block_rows, top_count = route_ids.shape
    flat_ids = route_ids.reshape(image_count, block_rows * top_count)
    expert_range = jnp.arange(n_experts, dtype=jnp.int32)
    one_hot = (flat_ids[:, :, None] == expert_range[None, None, :]).astype(jnp.int32)
    earlier = jnp.cumsum(one_hot, axis=1) - one_hot
    return lax.optimization_barrier(jnp.sum(earlier * one_hot, axis=2)).reshape(image_count, block_rows, top_count)

def image_layer(params, image_pack):
    w_qkv, w_attn_out, w_router, norm_gains, norm_biases, w_expert_in, w_expert_down = params
    token_rows, valid_mask, route_ids, keep_wide = image_pack
    model_width = token_rows.shape[1]
    n_experts = w_router.shape[1]
    normed_one = low(layer_norm(token_rows, norm_gains[0], norm_biases[0]))
    projected = low(low_back(jnp.dot(normed_one, w_qkv, precision=precise)))
    query_heads = projected[:, :model_width].reshape(SLOTS, HEADS, HEAD_DIM)
    key_heads = projected[:, model_width:2 * model_width].reshape(SLOTS, HEADS, HEAD_DIM)
    value_heads = projected[:, 2 * model_width:].reshape(SLOTS, HEADS, HEAD_DIM)
    scores = jnp.einsum('qhd,khd->hqk', query_heads, key_heads, precision=precise) * HEAD_DIM ** (-0.5)
    scores = low_back(scores)
    scores = jnp.where(valid_mask[None, None, :] > 0, scores, -1e+30)
    row_max = lax.optimization_barrier(jnp.max(scores, axis=2, keepdims=True))
    exponent = jnp.exp(scores - row_max)
    attn_probs = exponent / lax.optimization_barrier(jnp.sum(exponent, axis=2, keepdims=True))
    attended = jnp.einsum('hqk,khd->qhd', low(attn_probs), value_heads, precision=precise).reshape(SLOTS, model_width)
    attended = low(low_back(attended))
    branch = low_back(jnp.dot(attended, w_attn_out, precision=precise))
    hidden = token_rows + branch
    mixed = low(layer_norm(hidden, norm_gains[1], norm_biases[1]))
    logits = jnp.dot(mixed, w_router, precision=precise)
    router = jax.nn.softmax(logits, axis=-1)
    expert_range = jnp.arange(n_experts, dtype=jnp.int32)
    choose = (route_ids[:, :, None] == expert_range[None, None, :]).astype(jnp.float32)
    live_mask = keep_wide * valid_mask[:, None]
    gate_weights = lax.optimization_barrier(jnp.sum(choose * router[:, None, :], axis=2)) * live_mask
    slot_rank = slot_ranks(route_ids.reshape(N_CONTEXT, BLK, 2), n_experts).reshape(SLOTS, 2)
    block_index = jnp.arange(SLOTS, dtype=jnp.int32) // BLK
    target = (route_ids * N_CONTEXT + block_index[:, None]) * CAP + slot_rank
    copy_zero = low_back(mixed) * live_mask[:, 0:1]
    copy_one = low_back(mixed) * live_mask[:, 1:2]
    buffer = jnp.zeros((n_experts * N_CONTEXT * CAP, model_width), jnp.float32)
    buffer = buffer.at[target[:, 0]].add(copy_zero).at[target[:, 1]].add(copy_one)
    buffer = buffer.reshape(n_experts, N_CONTEXT * CAP, model_width)
    inner_pre = low_back(jnp.einsum('ecd,edf->ecf', buffer, w_expert_in, precision=precise))
    active = low(jax.nn.gelu(inner_pre))
    expert_out = low(low_back(jnp.einsum('ecf,efd->ecd', active, w_expert_down, precision=precise)))
    expert_out = expert_out.reshape(n_experts * N_CONTEXT * CAP, model_width)
    mixture = gate_weights[:, 0:1] * expert_out[target[:, 0]] + gate_weights[:, 1:2] * expert_out[target[:, 1]]
    return valid_mask[:, None] * (hidden + mixture)

def reference(tokens, lengths, route_ids, keep_mask, w_qkv, w_attn_out, w_router, norm_gains, norm_biases, w_expert_in, w_expert_down, cotangent):
    positions = jnp.arange(SLOTS, dtype=jnp.int32)
    block_index = positions // BLK
    valid_mask = ((positions % BLK)[None, :] < lengths[:, block_index]).astype(jnp.float32)
    keep_wide = keep_mask.astype(jnp.float32)
    weight_list = tuple((weight_arg.astype(jnp.float32) for weight_arg in (w_qkv, w_attn_out, w_router, norm_gains, norm_biases, w_expert_in, w_expert_down)))

    def forward(token_rows, *params):

        def per_image(image_pack):
            return jax.checkpoint(image_layer)(params, image_pack)
        return lax.map(per_image, (token_rows, valid_mask, route_ids, keep_wide))
    layer_out, pullback = jax.vjp(forward, tokens.astype(jnp.float32), *weight_list)
    gradients = pullback(cotangent.astype(jnp.float32))
    return (layer_out.astype(jnp.bfloat16), gradients[0], gradients[1], gradients[2], gradients[3], gradients[4], gradients[5], gradients[6], gradients[7])
```

```python
import functools
import itertools
import types

import jax
import jax.numpy as jnp
from jax import lax
from jax.experimental import pallas as pl
from jax.experimental.pallas import tpu as pltpu
from jax.sharding import PartitionSpec as P

HEADS = 12
EPS = 1e-06
F32 = jnp.float32
BF16 = jnp.bfloat16
MESH = pl.DeviceIdType.MESH
NN = (((1,), (0,)), ((), ()))
NT = (((1,), (1,)), ((), ()))
TN = (((0,), (0,)), ((), ()))
VMEM_LIMIT = 60 * 2**20
LOGIT_LANE = 4


def mm(left, right, dims=NN):
    return lax.dot_general(left, right, dims, preferred_element_type=F32)


def lane_of(shape):
    return lax.broadcasted_iota(jnp.int32, shape, 1)


def row_of(shape):
    return lax.broadcasted_iota(jnp.int32, shape, 0)


class Links:
    def __init__(self, send, recv):
        self.send, self.recv, self.ids = send, recv, itertools.count()

    def new(self):
        return next(self.ids)

    def make(self, at, src, dst, device):
        return pltpu.make_async_remote_copy(
            src_ref=src,
            dst_ref=dst,
            send_sem=self.send.at[at],
            recv_sem=self.recv.at[at],
            device_id=device,
            device_id_type=MESH,
        )


def greet(devices):
    barrier = pltpu.get_barrier_semaphore()
    for device in devices:
        pl.semaphore_signal(barrier, inc=1, device_id=device, device_id_type=MESH)
    pl.semaphore_wait(barrier, len(devices))


def normalize(values):
    centred = values - jnp.mean(values, axis=-1, keepdims=True)
    inverse = lax.rsqrt(jnp.mean(centred * centred, axis=-1, keepdims=True) + EPS)
    return centred * inverse, inverse


def normalize_back(grad_out, unit_rows, inverse, gain):
    scaled = grad_out * gain
    centre_term = jnp.mean(scaled, axis=-1, keepdims=True)
    slope_term = jnp.mean(scaled * unit_rows, axis=-1, keepdims=True)
    return inverse * (scaled - centre_term - unit_rows * slope_term)


def to_column(row):
    size = row.shape[1]
    eye = row_of((size, size)) == lane_of((size, size))
    return jnp.sum(jnp.where(eye, row, 0.0), axis=1, keepdims=True)


def to_row(column):
    size = column.shape[0]
    eye = row_of((size, size)) == lane_of((size, size))
    return jnp.sum(jnp.where(eye, column, 0.0), axis=0, keepdims=True)


def key_bias(c, len_ref, image):
    at = row_of((c.S, 1))
    bias = jnp.full((c.S, 1), -1e30, F32)
    for block in range(c.C):
        start = block * c.B
        inside = jnp.logical_and(at >= start, at < start + len_ref[image, block])
        bias = jnp.where(inside, 0.0, bias)
    return bias


def two_heads(pair):
    first = lane_of(pair.shape) < pair.shape[1] // 2
    zero = jnp.zeros_like(pair)
    return jnp.concatenate([jnp.where(first, pair, zero), jnp.where(first, zero, pair)], axis=0)


def one_pair(stacked):
    half = stacked.shape[0] // 2
    first = lane_of((half, stacked.shape[1])) < stacked.shape[1] // 2
    return jnp.where(first, stacked[:half], stacked[half:])


def front_kernel(c, *refs):
    refs = list(refs)
    take = lambda count: [refs.pop(0) for _ in range(count)]
    len_ref, tok_ref, route_ref, keep_ref, cot_ref = take(5)
    if c.gather:
        wqkv_ref, wout_ref, small_ref = take(3)
        w_ref, vec_ref = take(2)
    else:
        w_ref, vec_ref = take(2)
    q_ref, kv_ref, lse_ref, att_ref, hid_ref, mix_ref, meta_ref, router_ref = take(8)
    send_ref, gsend_ref, dyarr_ref = take(3)
    smalls, dysend, norm_ref, ssem, rsem = take(5)
    links = Links(ssem, rsem)
    z, x, y = lax.axis_index("expert"), lax.axis_index("context"), lax.axis_index("dp")
    core = lax.rem(x, 2)
    shard = z * c.Y + y
    core_dev, far_dev, y_dev = (z, x ^ 1, y), (z, x ^ 2, y), (z, x, 1 - y)
    plane = [(lax.div(shard ^ k, c.Y), x, lax.rem(shard ^ k, c.Y)) for k in range(1, c.E * c.Y)]
    experts = [(z ^ k, x, y) for k in range(1, c.E)]
    greet([core_dev, far_dev] + (plane if c.gather else experts))
    ends = []

    def go(at, src, dst, device):
        copy = links.make(at, src, dst, device)
        copy.start()
        ends.append(copy)

    if c.gather:
        small_ids = [links.new() for _ in plane]
        smalls[shard] = small_ref[...]
        for at, device in zip(small_ids, plane):
            go(at, smalls.at[shard], smalls.at[shard], device)

        def rows_of(z_at, y_at):
            return pl.ds(pl.multiple_of((z_at * c.Y + y_at) * c.sh, 32), c.sh)

        own_rows = rows_of(z, y)
        for part in range(3):
            w_ref[part, own_rows, :] = wqkv_ref[:, part * c.D : (part + 1) * c.D]
        w_ref[3, own_rows, :] = wout_ref[...]

        def unit(z_at, y_at):
            return w_ref.at[pl.ds(2 * core, 2), rows_of(z_at, y_at), :]

        def other_unit(z_at, y_at):
            return w_ref.at[pl.ds(2 - 2 * core, 2), rows_of(z_at, y_at), :]

        up = [links.new() for _ in range(c.E)]
        down = [links.new() for _ in range(c.E)]
        y_up = [links.new() for _ in range(c.E)]
        y_down = [links.new() for _ in range(c.E)]
        core_up = [[links.new() for _ in range(c.E)] for _ in range(2)]
        core_down = [[links.new() for _ in range(c.E)] for _ in range(2)]
        above, below = (lax.rem(z + 1, c.E), x, y), (lax.rem(z + c.E - 1, c.E), x, y)

        def copy_of(at, z_at, y_at, device):
            return links.make(at, unit(z_at, y_at), unit(z_at, y_at), device)

        pending = []

        def send_if(condition, at, z_at, y_at, device):
            pl.when(condition)(lambda: copy_of(at, z_at, y_at, device).start())
            pending.append((condition, at, z_at, y_at, device))

        always = z >= 0
        send_if(z < c.E - 1, up[1], z, y, above)
        send_if(z > 0, down[1], z, y, below)
        send_if(always, y_up[0], z, y, y_dev)

    unit_rows = [None] * c.N
    choices = []
    for image in range(c.N):
        rows = slice(image * c.B, (image + 1) * c.B)
        names = route_ref[rows, :]
        live = jnp.where(row_of((c.B, 1)) < len_ref[image, x], 1.0, 0.0)
        kept = keep_ref[rows, :].astype(F32) * live
        first, second = names[:, 0:1], names[:, 1:2]
        lane = lane_of((c.B, 128))
        named = jnp.where(lane == first, kept[:, 0:1], 0.0) + jnp.where(
            lane == second, kept[:, 1:2], 0.0
        )
        earlier = jnp.where(lane_of((c.B, c.B)) < row_of((c.B, c.B)), 1.0, 0.0).astype(BF16)
        rank = mm(earlier, named.astype(BF16))
        rank_first = jnp.sum(jnp.where(lane == first, rank, 0.0), axis=1, keepdims=True)
        rank_second = jnp.sum(jnp.where(lane == second, rank, 0.0), axis=1, keepdims=True)
        slot_first = first * c.cap + rank_first.astype(jnp.int32)
        slot_second = second * c.cap + rank_second.astype(jnp.int32)
        at = lane_of((c.B, c.E * c.cap))
        place = jnp.where(at == slot_first, kept[:, 0:1], 0.0) + jnp.where(
            at == slot_second, kept[:, 1:2], 0.0
        )
        place = place.astype(BF16)
        choices.append((first, second, kept, slot_first, slot_second, place))
        dysend[image] = mm(place, cot_ref[rows, :], TN).astype(BF16).reshape(c.E, c.cap, c.D)
        dyarr_ref[z, image] = dysend[image, z]

    if c.gather:
        for at, device in zip(small_ids, plane):
            other = lax.div(shard, 1)
            links.make(at, smalls.at[other], smalls.at[other], device).wait_recv()
        wide = jnp.concatenate([smalls[k] for k in range(c.E * c.Y)], axis=1).astype(BF16)
        span = c.E * c.Y * 128
        src, dst = row_of((span, c.D)), lane_of((span, c.D))
        inside = lax.rem(src, 128)
        pick = jnp.logical_and(inside < c.sh, lax.div(src, 128) * c.sh + inside == dst)
        vec_ref[...] = mm(wide, jnp.where(pick, 1.0, 0.0).astype(BF16))
    vec = vec_ref[...]
    for image in range(c.N):
        rows = slice(image * c.B, (image + 1) * c.B)
        unit_one, _ = normalize(tok_ref[rows, :].astype(F32))
        norm_ref[rows, :] = (unit_one * vec[0:1] + vec[2:3]).astype(BF16)

    if c.gather:

        def got(at, z_at, y_at):
            copy_of(at, z_at, y_at, core_dev).wait_recv()

        def pass_y(at, z_at, core_at, condition):
            pl.when(condition)(lambda: got(at, z_at, 1 - y))
            send_if(condition, core_at, z_at, 1 - y, core_dev)

        for j in range(1, c.E):
            lower, upper = z >= j, z + j <= c.E - 1
            pl.when(lower)(lambda: got(up[j], z - j, y))
            if j < c.E - 1:
                send_if(jnp.logical_and(lower, z < c.E - 1), up[j + 1], z - j, y, above)
            send_if(lower, y_up[j], z - j, y, y_dev)
            send_if(lower, core_up[0][j], z - j, y, core_dev)
            pl.when(upper)(lambda: got(down[j], z + j, y))
            if j < c.E - 1:
                send_if(jnp.logical_and(upper, z > 0), down[j + 1], z + j, y, below)
            send_if(upper, y_down[j], z + j, y, y_dev)
            send_if(upper, core_down[0][j], z + j, y, core_dev)
            if j == 1:
                pass_y(y_up[0], z, core_up[1][0], always)
            else:
                pass_y(y_up[j - 1], z - j + 1, core_up[1][j - 1], z >= j - 1)
                pass_y(y_down[j - 1], z + j - 1, core_down[1][j - 1], z + j - 1 <= c.E - 1)
        last = c.E - 1
        pass_y(y_up[last], z - last, core_up[1][last], z >= last)
        pass_y(y_down[last], z + last, core_down[1][last], z + last <= c.E - 1)

        def got_core(at, z_at, y_at):
            there = other_unit(z_at, y_at)
            links.make(at, there, there, core_dev).wait_recv()

        for side in range(2):
            y_at = y if side == 0 else 1 - y
            if side:
                got_core(core_up[side][0], z, y_at)
            for j in range(1, c.E):
                pl.when(z >= j)(lambda: got_core(core_up[side][j], z - j, y_at))
                pl.when(z + j <= c.E - 1)(lambda: got_core(core_down[side][j], z + j, y_at))

    normed = norm_ref[...]
    own_at = pl.ds(pl.multiple_of(x * c.B, 32), c.B)
    kv_ids = [[links.new() for _ in range(3)] for _ in range(c.N)]
    keys = mm(normed, w_ref[1]).astype(BF16)
    values = mm(normed, w_ref[2]).astype(BF16)
    for image in range(c.N):
        rows = slice(image * c.B, (image + 1) * c.B)
        kv_ref[image, own_at, 0 : c.D] = keys[rows]
        kv_ref[image, own_at, c.D : 2 * c.D] = values[rows]
        block = kv_ref.at[image, own_at, :]
        go(kv_ids[image][0], block, block, far_dev)
        go(kv_ids[image][1], block, block, core_dev)
    dy_ids = [links.new() for _ in experts]
    for k, (at, device) in enumerate(zip(dy_ids, experts), 1):
        go(at, dysend.at[:, z ^ k], dyarr_ref.at[z], device)
    q_ref[...] = mm(normed, w_ref[0]).astype(BF16)

    block_of = lambda image, who: kv_ref.at[image, pl.ds(pl.multiple_of(who * c.B, 32), c.B), :]

    for image in range(c.N):
        rows = pl.ds(image * c.B, c.B)
        far_block = block_of(image, x ^ 2)
        links.make(kv_ids[image][0], far_block, far_block, far_dev).wait_recv()
        go(kv_ids[image][2], far_block, far_block, core_dev)
        near_block = block_of(image, x ^ 1)
        links.make(kv_ids[image][1], near_block, near_block, core_dev).wait_recv()
        cross_block = block_of(image, x ^ 3)
        links.make(kv_ids[image][2], cross_block, cross_block, core_dev).wait_recv()
        bias = key_bias(c, len_ref, image)

        def pair_step(pair, carry):
            lanes = pl.ds(pl.multiple_of(pair * 128, 128), 128)
            value_lanes = pl.ds(pl.multiple_of(c.D + pair * 128, 128), 128)
            queries = two_heads(q_ref[rows, lanes]) * jnp.asarray(c.scale, BF16)
            scores = mm(kv_ref[image, :, lanes], queries, NT) + bias
            top = jnp.max(scores, axis=0, keepdims=True)
            exponent = jnp.exp(scores - top)
            total = jnp.sum(exponent, axis=0, keepdims=True)
            probs = (exponent * (1.0 / total)).astype(BF16)
            lse_ref[image, pair] = jnp.broadcast_to(top + jnp.log(total), (8, 2 * c.B))
            mixed_values = mm(kv_ref[image, :, value_lanes].T, probs)
            att_ref[rows, lanes] = one_pair(mixed_values.T).astype(BF16)
            return carry

        lax.fori_loop(0, c.D // 128, pair_step, 0)

    branch = mm(att_ref[...], w_ref[3])
    hidden = tok_ref[...].astype(F32) + branch
    hid_ref[...] = hidden
    unit_two, _ = normalize(hidden)
    mixed = (unit_two * vec[1:2] + vec[3:4]).astype(BF16)
    mix_ref[...] = mixed
    pad = jnp.zeros((128 - c.r8, c.D), BF16)
    logits = mm(mixed, jnp.concatenate([vec.astype(BF16), pad], axis=0), NT)
    lane = lane_of((c.N * c.B, 128))
    valid = jnp.logical_and(lane >= LOGIT_LANE, lane < LOGIT_LANE + c.E)
    logits = jnp.where(valid, logits, -1e30)
    weight = jnp.exp(logits - jnp.max(logits, axis=1, keepdims=True))
    router = weight / jnp.sum(weight, axis=1, keepdims=True)
    router_ref[...] = router
    gsend_ref[...] = jnp.zeros_like(gsend_ref)
    lane = lane_of((c.B, 128))
    for image in range(c.N):
        rows = slice(image * c.B, (image + 1) * c.B)
        first, second, kept, slot_first, slot_second, place = choices[image]
        here = router[rows]
        gate_first = kept[:, 0:1] * jnp.sum(
            jnp.where(lane == LOGIT_LANE + first, here, 0.0), axis=1, keepdims=True
        )
        gate_second = kept[:, 1:2] * jnp.sum(
            jnp.where(lane == LOGIT_LANE + second, here, 0.0), axis=1, keepdims=True
        )
        send_ref[image] = mm(place, mixed[rows], TN).astype(BF16).reshape(c.E, c.cap, c.D)
        at = lane_of((c.B, c.cap))
        for expert in range(c.E):
            gates = jnp.where(at == slot_first - expert * c.cap, gate_first, 0.0)
            gates = gates + jnp.where(at == slot_second - expert * c.cap, gate_second, 0.0)
            gsend_ref[expert, image : image + 1, :] = jnp.sum(gates, axis=0, keepdims=True)
        columns = (
            slot_first.astype(F32),
            slot_second.astype(F32),
            kept[:, 0:1],
            kept[:, 1:2],
            gate_first,
            gate_second,
            first.astype(F32),
            second.astype(F32),
        )
        meta = jnp.zeros((c.B, 128), F32)
        for index, column in enumerate(columns):
            meta = jnp.where(lane == index, column, meta)
        meta_ref[rows, :] = meta

    for k, (at, device) in enumerate(zip(dy_ids, experts), 1):
        links.make(at, dyarr_ref.at[z ^ k], dyarr_ref.at[z ^ k], device).wait_recv()
    for copy in ends:
        copy.wait_send()
    if c.gather:
        for condition, at, z_at, y_at, device in pending:
            pl.when(condition)(lambda: copy_of(at, z_at, y_at, device).wait_send())


def spec(space):
    return pl.BlockSpec(memory_space=space)


def run_front(c, lengths, tok, route, keep, cot, weights):
    shape = jax.ShapeDtypeStruct
    made = [shape((4, c.D, c.D), BF16), shape((c.r8, c.D), F32)] if c.gather else []
    made += [
        shape((c.T, c.D), BF16),
        shape((c.N, c.S, 2 * c.D), BF16),
        shape((c.N, c.D // 128, 8, 2 * c.B), F32),
        shape((c.T, c.D), BF16),
        shape((c.T, c.D), F32),
        shape((c.T, c.D), BF16),
        shape((c.T, 128), F32),
        shape((c.T, 128), F32),
        shape((c.N, c.E, c.cap, c.D), BF16),
        shape((c.E, 8, c.cap), F32),
        shape((c.E, c.N, c.cap, c.D), BF16),
    ]
    count = 96 if c.gather else 2 * c.E + 16
    out = pl.pallas_call(
        functools.partial(front_kernel, c),
        out_shape=made,
        in_specs=[spec(pltpu.SMEM)] + [spec(pltpu.VMEM)] * (4 + len(weights)),
        out_specs=[spec(pltpu.VMEM)] * len(made),
        scratch_shapes=[
            pltpu.VMEM((c.E * c.Y, c.r8, 128), F32),
            pltpu.VMEM((c.N, c.E, c.cap, c.D), BF16),
            pltpu.VMEM((c.T, c.D), BF16),
            pltpu.SemaphoreType.DMA((count,)),
            pltpu.SemaphoreType.DMA((count,)),
        ],
        compiler_params=pltpu.CompilerParams(
            collective_id=0, has_side_effects=True, vmem_limit_bytes=VMEM_LIMIT
        ),
        name="front",
    )(lengths, tok, route, keep, cot, *weights)
    return out if c.gather else list(weights) + list(out)


def gelu_both(pre):
    inner = 0.7978845608028654 * (pre + 0.044715 * pre * pre * pre)
    bend = jnp.tanh(inner)
    half = 0.5 * (1.0 + bend)
    slope = 0.7978845608028654 * (1.0 + 0.134145 * pre * pre)
    return pre * half, half + 0.5 * pre * (1.0 - bend * bend) * slope


def expert_kernel(
    c,
    send_ref,
    gsend_ref,
    dyarr_ref,
    win_hbm,
    wdown_hbm,
    xback_ref,
    gback_ref,
    yloc_ref,
    grad_ref,
    win,
    wdown,
    arr,
    garr,
    act_all,
    dpre_all,
    dout_all,
    dxs,
    dgs,
    turned,
    wsem,
    ssem,
    rsem,
):
    links = Links(ssem, rsem)
    z, x, y = lax.axis_index("expert"), lax.axis_index("context"), lax.axis_index("dp")
    experts = [(z ^ k, x, y) for k in range(1, c.E)]
    load_in = pltpu.make_async_copy(win_hbm, win, wsem.at[0])
    load_down = pltpu.make_async_copy(wdown_hbm, wdown, wsem.at[1])
    load_in.start()
    load_down.start()
    greet(experts)
    ids = [[links.new() for _ in range(4)] for _ in range(c.E)]
    ends = []

    def go(at, src, dst, device):
        copy = links.make(at, src, dst, device)
        copy.start()
        ends.append(copy)

    for k in range(1, c.E):
        go(ids[k][0], send_ref.at[:, z ^ k], arr.at[z], experts[k - 1])
        go(ids[k][1], gsend_ref.at[z ^ k], garr.at[z], experts[k - 1])
    for image in range(c.N):
        arr[z, image] = send_ref[image, z]
    garr[z] = gsend_ref[z]
    load_in.wait()
    load_down.wait()
    dgs[...] = jnp.zeros_like(dgs)
    group = c.E // c.chunks
    height = group * c.N * c.cap
    for g in range(c.chunks):
        slab = lax.div(z, group) ^ g
        for k in range(g * group, (g + 1) * group):
            if k:
                there = z ^ k
                links.make(ids[k][0], arr.at[there], arr.at[there], experts[k - 1]).wait_recv()
                links.make(ids[k][1], garr.at[there], garr.at[there], experts[k - 1]).wait_recv()
        start = pl.multiple_of(slab * height, 32)
        rows = pl.ds(start, height)
        for member in range(group):
            source = slab * group + member
            for image in range(c.N):
                gates = to_column(garr[source, image : image + 1, :])
                offset = (member * c.N + image) * c.cap
                part = pl.ds(pl.multiple_of(start + offset, 16), c.cap)
                dout_all[part, :] = (gates * dyarr_ref[source, image].astype(F32)).astype(BF16)
        inputs = arr[pl.ds(slab * group, group)].reshape(height, c.D)
        douts = dout_all[rows, :]

        def ff_step(step, carry):
            lanes = pl.ds(pl.multiple_of(step * c.FB, 128), c.FB)
            pre = mm(inputs, win[:, lanes])
            act, slope = gelu_both(pre)
            act_all[rows, lanes] = act.astype(BF16)
            dact = mm(douts, wdown[lanes, :], NT)
            dpre_all[rows, lanes] = (dact * slope).astype(BF16)
            return carry

        lax.fori_loop(0, c.FF // c.FB, ff_step, 0)
        dx = mm(dpre_all[rows, :], win[...], NT).astype(BF16)
        dxs[pl.ds(slab * group, group)] = dx.reshape(group, c.N, c.cap, c.D)
        made = mm(act_all[rows, :], wdown[...]).astype(BF16)
        yloc_ref[pl.ds(slab * group, group)] = made.reshape(group, c.N, c.cap, c.D)
        for member in range(group):
            source = slab * group + member
            for image in range(c.N):
                offset = (member * c.N + image) * c.cap
                dots = made[offset : offset + c.cap].astype(F32) * dyarr_ref[source, image].astype(
                    F32
                )
                dgs[source, image : image + 1, :] = to_row(jnp.sum(dots, axis=1, keepdims=True))
        for k in range(g * group, (g + 1) * group):
            if k:
                there = z ^ k
                go(ids[k][2], dxs.at[there], xback_ref.at[:, z], experts[k - 1])
                go(ids[k][3], dgs.at[there], gback_ref.at[z], experts[k - 1])
    for image in range(c.N):
        xback_ref[image, z] = dxs[z, image]
    gback_ref[z] = dgs[z]

    total = c.E * c.N * c.cap
    turned[0] = arr[...].reshape(total, c.D).T
    turned[1] = dout_all[...].T

    def grad_step(step, carry):
        lanes = pl.ds(pl.multiple_of(step * c.FB, 128), c.FB)
        grad_ref[0, :, lanes] = mm(turned[0], dpre_all[:, lanes]).astype(BF16)
        grad_ref[1, :, lanes] = mm(turned[1], act_all[:, lanes]).astype(BF16)
        return carry

    lax.fori_loop(0, c.FF // c.FB, grad_step, 0)
    for k in range(1, c.E):
        there = z ^ k
        links.make(ids[k][2], xback_ref.at[:, there], xback_ref.at[:, there], experts[k - 1]).wait_recv()
        links.make(ids[k][3], gback_ref.at[there], gback_ref.at[there], experts[k - 1]).wait_recv()
    for copy in ends:
        copy.wait_send()


def run_experts(c, send, gsend, dyarr, w_in, w_down):
    shape = jax.ShapeDtypeStruct
    total = c.E * c.N * c.cap
    count = 4 * c.E
    return pl.pallas_call(
        functools.partial(expert_kernel, c),
        out_shape=[
            shape((c.N, c.E, c.cap, c.D), BF16),
            shape((c.E, 8, c.cap), F32),
            shape((c.E, c.N, c.cap, c.D), BF16),
            shape((2, c.D, c.FF), BF16),
        ],
        in_specs=[spec(pltpu.VMEM)] * 3 + [spec(pl.ANY)] * 2,
        out_specs=[spec(pltpu.VMEM)] * 4,
        scratch_shapes=[
            pltpu.VMEM((c.D, c.FF), BF16),
            pltpu.VMEM((c.FF, c.D), BF16),
            pltpu.VMEM((c.E, c.N, c.cap, c.D), BF16),
            pltpu.VMEM((c.E, 8, c.cap), F32),
            pltpu.VMEM((total, c.FF), BF16),
            pltpu.VMEM((total, c.FF), BF16),
            pltpu.VMEM((total, c.D), BF16),
            pltpu.VMEM((c.E, c.N, c.cap, c.D), BF16),
            pltpu.VMEM((c.E, 8, c.cap), F32),
            pltpu.VMEM((2, c.D, total), BF16),
            pltpu.SemaphoreType.DMA((2,)),
            pltpu.SemaphoreType.DMA((count,)),
            pltpu.SemaphoreType.DMA((count,)),
        ],
        compiler_params=pltpu.CompilerParams(
            collective_id=1, has_side_effects=True, vmem_limit_bytes=VMEM_LIMIT
        ),
        name="experts",
    )(send, gsend, dyarr, w_in, w_down)


def back_plain(c, tok, cot, lengths, weights, vec, q, kv, lse, att, hid, mix, meta, router, xback, gback, yloc, grads):
    precise = lax.Precision.HIGHEST
    rank = lax.axis_index("context")
    own = lax.dynamic_slice_in_dim(lengths, rank, 1, 1)
    live = (jnp.arange(c.B, dtype=jnp.int32)[None, :] < own).astype(F32).reshape(c.T, 1)
    slots = meta[:, 0:2].astype(jnp.int32)
    kept, gates, names = meta[:, 2:4], meta[:, 4:6], meta[:, 6:8].astype(jnp.int32)
    image = jnp.repeat(jnp.arange(c.N, dtype=jnp.int32), c.B)[:, None]
    spots = image * (c.E * c.cap) + slots
    made = lax.all_to_all(yloc, "expert", split_axis=0, concat_axis=0, tiled=True)
    made = made.transpose(1, 0, 2, 3).reshape(c.N * c.E * c.cap, c.D)
    rows = made[spots].astype(F32)
    dy = cot.astype(F32) * live
    out = (live * (hid + jnp.sum(gates[:, :, None] * rows, axis=1))).astype(BF16)
    copies = xback.reshape(c.N * c.E * c.cap, c.D)[spots].astype(F32)
    dgate = gback[:, : c.N].transpose(1, 0, 2).reshape(-1)[spots] * kept
    d_mixed = jnp.sum(copies * kept[:, :, None], axis=1)
    probs = router[:, LOGIT_LANE : LOGIT_LANE + c.E]
    choose = (names[:, :, None] == jnp.arange(c.E)).astype(F32)
    d_router = jnp.sum(choose * dgate[:, :, None], axis=1)
    d_logits = probs * (d_router - jnp.sum(probs * d_router, axis=1, keepdims=True))
    w_router = vec[LOGIT_LANE : LOGIT_LANE + c.E]
    d_mixed = d_mixed + jnp.dot(d_logits, w_router, precision=precise)
    g_router = jnp.einsum("rd,re->de", mix.astype(F32), d_logits, precision=precise)
    unit_two, inverse_two = normalize(hid)
    gains_two, biases_two = jnp.sum(d_mixed * unit_two, axis=0), jnp.sum(d_mixed, axis=0)
    d_hidden = dy + normalize_back(d_mixed, unit_two, inverse_two, vec[1])
    d_branch = d_hidden.astype(BF16)
    g_out = mm(att, d_branch, TN)
    d_att = mm(d_branch, weights[3], NT).astype(BF16)
    hd = c.D // HEADS
    qh = q.reshape(c.N, c.B, HEADS, hd)
    kh = kv[:, :, : c.D].reshape(c.N, c.S, HEADS, hd)
    vh = kv[:, :, c.D :].reshape(c.N, c.S, HEADS, hd)
    dh = d_att.reshape(c.N, c.B, HEADS, hd)
    ein = functools.partial(jnp.einsum, preferred_element_type=F32)
    at = jnp.arange(c.S, dtype=jnp.int32)
    key_live = at[None, :] % c.B < lengths[:, at // c.B]
    scores = jnp.where(key_live[:, None, None, :], ein("iqhd,ikhd->ihqk", qh, kh) * c.scale, -1e30)
    total = lse[:, :, 0, :].reshape(c.N, c.D // 128, 2, c.B).reshape(c.N, HEADS, c.B, 1)
    p = jnp.exp(scores - total)
    dp = ein("iqhd,ikhd->ihqk", dh, vh)
    ds = (p * (dp - jnp.sum(p * dp, axis=-1, keepdims=True))).astype(BF16)
    dq = ein("ihqk,ikhd->iqhd", ds, kh) * c.scale
    dk = ein("ihqk,iqhd->ikhd", ds, qh) * c.scale
    dv = ein("ihqk,iqhd->ikhd", p.astype(BF16), dh)
    terms = jnp.concatenate([dk.reshape(c.N, c.S, c.D), dv.reshape(c.N, c.S, c.D)], axis=2)
    summed = lax.psum_scatter(terms.astype(BF16), "context", scatter_dimension=1, tiled=True)
    d_proj = jnp.concatenate(
        [dq.reshape(c.T, c.D).astype(BF16), summed.reshape(c.T, 2 * c.D).astype(BF16)], axis=1
    )
    unit_one, inverse_one = normalize(tok.astype(F32))
    normed = (unit_one * vec[0] + vec[2]).astype(BF16)
    g_qkv = mm(normed, d_proj, TN)
    qkv = jnp.concatenate([weights[0], weights[1], weights[2]], axis=1)
    d_normed = mm(d_proj, qkv, NT)
    gains_one, biases_one = jnp.sum(d_normed * unit_one, axis=0), jnp.sum(d_normed, axis=0)
    g_tok = d_hidden + normalize_back(d_normed, unit_one, inverse_one, vec[0])
    both = ("expert", "dp")
    dense = [
        lax.psum_scatter(g_qkv, both, scatter_dimension=0, tiled=True),
        lax.psum_scatter(g_out, both, scatter_dimension=0, tiled=True),
        lax.psum_scatter(g_router, both, scatter_dimension=0, tiled=True),
        lax.psum_scatter(jnp.stack([gains_one, gains_two]), both, scatter_dimension=1, tiled=True),
        lax.psum_scatter(jnp.stack([biases_one, biases_two]), both, scatter_dimension=1, tiled=True),
    ]
    dense = [part.astype(F32) for part in lax.psum([p.astype(BF16) for p in dense], "context")]
    sums = lax.psum_scatter(grads, ("context", "dp"), scatter_dimension=2, tiled=True).astype(F32)
    shape = (c.N, c.B, c.D)
    return (
        out.reshape(shape),
        g_tok.reshape(shape),
        *dense,
        sums[0][None],
        sums[1].T[None],
    )


def pack_small(c, w_router, norm_gains, norm_biases):
    rows = jnp.concatenate([norm_gains, norm_biases, w_router.T], axis=0).astype(F32)
    return jnp.pad(rows, ((0, c.r8 - rows.shape[0]), (0, 128 - rows.shape[1])))


def per_device(
    mesh_shape,
    tokens,
    lengths,
    route_ids,
    keep_mask,
    w_qkv,
    w_attn_out,
    w_router,
    norm_gains,
    norm_biases,
    w_expert_in,
    w_expert_down,
    cotangent,
):
    images, block, width = tokens.shape
    experts = mesh_shape["expert"] * w_expert_in.shape[0]
    c = types.SimpleNamespace(
        E=experts,
        Y=mesh_shape["dp"],
        C=mesh_shape["context"],
        N=images,
        B=block,
        D=width,
        T=images * block,
        S=mesh_shape["context"] * block,
        FF=w_expert_in.shape[2],
        FB=512,
        cap=max(2, 16 * block // (5 * experts)),
        sh=w_qkv.shape[0],
        r8=-(-(LOGIT_LANE + experts) // 8) * 8,
        scale=(width // HEADS) ** -0.5,
        chunks=4,
    )
    c.gather = c.sh % 32 == 0
    tok = tokens.reshape(c.T, width)
    cot = cotangent.reshape(c.T, width)
    route = route_ids.reshape(c.T, 2)
    keep = keep_mask.reshape(c.T, 2)
    both = ("expert", "dp")
    if c.gather:
        given = (w_qkv, w_attn_out, pack_small(c, w_router, norm_gains, norm_biases))
    else:
        qkv = lax.all_gather(w_qkv, both, axis=0, tiled=True)
        out = lax.all_gather(w_attn_out, both, axis=0, tiled=True)
        small = pack_small(c, w_router, norm_gains, norm_biases)[:, : c.sh]
        vec = lax.all_gather(small, both, axis=1, tiled=True)
        stacked = jnp.concatenate([qkv, out], axis=1).reshape(width, 4, width).transpose(1, 0, 2)
        given = (stacked, vec)
    front = run_front(c, lengths, tok, route, keep, cot, given)
    weights, vec, q, kv, lse, att, hid, mix, meta, router, send, gsend, dyarr = front
    back = run_experts(c, send, gsend, dyarr, w_expert_in[0], w_expert_down[0])
    return back_plain(
        c, tok, cot, lengths, weights, vec, q, kv, lse, att, hid, mix, meta, router, *back
    )


def solution(mesh):
    rows = P(("expert", "dp"), "context", None)
    shard = P(("expert", "dp"), None)
    column = P(None, ("expert", "dp"))
    expert = P("expert", None, None)
    return jax.shard_map(
        functools.partial(per_device, dict(mesh.shape)),
        mesh=mesh,
        in_specs=(rows, shard, rows, rows, shard, shard, shard, column, column, expert, expert, rows),
        out_specs=(
            rows,
            rows,
            shard,
            shard,
            shard,
            column,
            column,
            P("expert", None, ("context", "dp")),
            P("expert", ("context", "dp"), None),
        ),
        check_vma=False,
    )
```

```python
import functools
import itertools
import types

import jax
import jax.numpy as jnp
from jax import lax
from jax.experimental import pallas as pl
from jax.experimental.pallas import tpu as pltpu
from jax.sharding import PartitionSpec as P

HEADS = 12
EPS = 1e-06
F32 = jnp.float32
BF16 = jnp.bfloat16
MESH = pl.DeviceIdType.MESH
NN = (((1,), (0,)), ((), ()))
NT = (((1,), (1,)), ((), ()))
TN = (((0,), (0,)), ((), ()))
VMEM_LIMIT = 60 * 2**20
LOGIT_LANE = 4


def mm(left, right, dims=NN):
    return lax.dot_general(left, right, dims, preferred_element_type=F32)


def lane_of(shape):
    return lax.broadcasted_iota(jnp.int32, shape, 1)


def row_of(shape):
    return lax.broadcasted_iota(jnp.int32, shape, 0)


class Links:
    def __init__(self, send, recv):
        self.send, self.recv, self.ids = send, recv, itertools.count()

    def new(self):
        return next(self.ids)

    def make(self, at, src, dst, device):
        return pltpu.make_async_remote_copy(
            src_ref=src,
            dst_ref=dst,
            send_sem=self.send.at[at],
            recv_sem=self.recv.at[at],
            device_id=device,
            device_id_type=MESH,
        )


def greet(devices):
    barrier = pltpu.get_barrier_semaphore()
    for device in devices:
        pl.semaphore_signal(barrier, inc=1, device_id=device, device_id_type=MESH)
    pl.semaphore_wait(barrier, len(devices))


def normalize(values):
    centred = values - jnp.mean(values, axis=-1, keepdims=True)
    inverse = lax.rsqrt(jnp.mean(centred * centred, axis=-1, keepdims=True) + EPS)
    return centred * inverse, inverse


def normalize_back(grad_out, unit_rows, inverse, gain):
    scaled = grad_out * gain
    centre_term = jnp.mean(scaled, axis=-1, keepdims=True)
    slope_term = jnp.mean(scaled * unit_rows, axis=-1, keepdims=True)
    return inverse * (scaled - centre_term - unit_rows * slope_term)


def to_column(row):
    size = row.shape[1]
    eye = row_of((size, size)) == lane_of((size, size))
    return jnp.sum(jnp.where(eye, row, 0.0), axis=1, keepdims=True)


def to_row(column):
    size = column.shape[0]
    eye = row_of((size, size)) == lane_of((size, size))
    return jnp.sum(jnp.where(eye, column, 0.0), axis=0, keepdims=True)


def key_bias(c, len_ref, image):
    at = row_of((c.S, 1))
    bias = jnp.full((c.S, 1), -1e30, F32)
    for block in range(c.C):
        start = block * c.B
        inside = jnp.logical_and(at >= start, at < start + len_ref[image, block])
        bias = jnp.where(inside, 0.0, bias)
    return bias


def two_heads(pair):
    first = lane_of(pair.shape) < pair.shape[1] // 2
    zero = jnp.zeros_like(pair)
    return jnp.concatenate([jnp.where(first, pair, zero), jnp.where(first, zero, pair)], axis=0)


def one_pair(stacked):
    half = stacked.shape[0] // 2
    first = lane_of((half, stacked.shape[1])) < stacked.shape[1] // 2
    return jnp.where(first, stacked[:half], stacked[half:])


def front_kernel(c, *refs):
    refs = list(refs)
    take = lambda count: [refs.pop(0) for _ in range(count)]
    len_ref, tok_ref, route_ref, keep_ref, cot_ref = take(5)
    if c.gather:
        wqkv_ref, wout_ref, small_ref = take(3)
        w_ref, vec_ref = take(2)
    else:
        w_ref, vec_ref = take(2)
    q_ref, kv_ref, lse_ref, att_ref, hid_ref, mix_ref, meta_ref, router_ref = take(8)
    send_ref, gsend_ref, dyarr_ref = take(3)
    smalls, dysend, norm_ref, ssem, rsem = take(5)
    links = Links(ssem, rsem)
    z, x, y = lax.axis_index("expert"), lax.axis_index("context"), lax.axis_index("dp")
    core = lax.rem(x, 2)
    shard = z * c.Y + y
    core_dev, far_dev, y_dev = (z, x ^ 1, y), (z, x ^ 2, y), (z, x, 1 - y)
    plane = [(lax.div(shard ^ k, c.Y), x, lax.rem(shard ^ k, c.Y)) for k in range(1, c.E * c.Y)]
    experts = [(z ^ k, x, y) for k in range(1, c.E)]
    greet([core_dev, far_dev] + (plane if c.gather else experts))
    ends = []

    def go(at, src, dst, device):
        copy = links.make(at, src, dst, device)
        copy.start()
        ends.append(copy)

    if c.gather:
        small_ids = [links.new() for _ in plane]
        smalls[shard] = small_ref[...]
        for at, device in zip(small_ids, plane):
            go(at, smalls.at[shard], smalls.at[shard], device)

        def rows_of(z_at, y_at):
            return pl.ds(pl.multiple_of((z_at * c.Y + y_at) * c.sh, 32), c.sh)

        own_rows = rows_of(z, y)
        for part in range(3):
            w_ref[part, own_rows, :] = wqkv_ref[:, part * c.D : (part + 1) * c.D]
        w_ref[3, own_rows, :] = wout_ref[...]

        def unit(z_at, y_at):
            return w_ref.at[pl.ds(2 * core, 2), rows_of(z_at, y_at), :]

        def other_unit(z_at, y_at):
            return w_ref.at[pl.ds(2 - 2 * core, 2), rows_of(z_at, y_at), :]

        up = [links.new() for _ in range(c.E)]
        down = [links.new() for _ in range(c.E)]
        y_up = [links.new() for _ in range(c.E)]
        y_down = [links.new() for _ in range(c.E)]
        core_up = [[links.new() for _ in range(c.E)] for _ in range(2)]
        core_down = [[links.new() for _ in range(c.E)] for _ in range(2)]
        above, below = (lax.rem(z + 1, c.E), x, y), (lax.rem(z + c.E - 1, c.E), x, y)

        def copy_of(at, z_at, y_at, device):
            return links.make(at, unit(z_at, y_at), unit(z_at, y_at), device)

        pending = []

        def send_if(condition, at, z_at, y_at, device):
            pl.when(condition)(lambda: copy_of(at, z_at, y_at, device).start())
            pending.append((condition, at, z_at, y_at, device))

        always = z >= 0
        send_if(z < c.E - 1, up[1], z, y, above)
        send_if(z > 0, down[1], z, y, below)
        send_if(always, y_up[0], z, y, y_dev)

    unit_rows = [None] * c.N
    choices = []
    for image in range(c.N):
        rows = slice(image * c.B, (image + 1) * c.B)
        names = route_ref[rows, :]
        live = jnp.where(row_of((c.B, 1)) < len_ref[image, x], 1.0, 0.0)
        kept = keep_ref[rows, :].astype(F32) * live
        first, second = names[:, 0:1], names[:, 1:2]
        lane = lane_of((c.B, 128))
        named = jnp.where(lane == first, kept[:, 0:1], 0.0) + jnp.where(
            lane == second, kept[:, 1:2], 0.0
        )
        earlier = jnp.where(lane_of((c.B, c.B)) < row_of((c.B, c.B)), 1.0, 0.0).astype(BF16)
        rank = mm(earlier, named.astype(BF16))
        rank_first = jnp.sum(jnp.where(lane == first, rank, 0.0), axis=1, keepdims=True)
        rank_second = jnp.sum(jnp.where(lane == second, rank, 0.0), axis=1, keepdims=True)
        slot_first = first * c.cap + rank_first.astype(jnp.int32)
        slot_second = second * c.cap + rank_second.astype(jnp.int32)
        at = lane_of((c.B, c.E * c.cap))
        place = jnp.where(at == slot_first, kept[:, 0:1], 0.0) + jnp.where(
            at == slot_second, kept[:, 1:2], 0.0
        )
        place = place.astype(BF16)
        choices.append((first, second, kept, slot_first, slot_second, place))
        dysend[image] = mm(place, cot_ref[rows, :], TN).astype(BF16).reshape(c.E, c.cap, c.D)
        dyarr_ref[z, image] = dysend[image, z]

    if c.gather:
        for at, device in zip(small_ids, plane):
            other = lax.div(shard, 1)
            links.make(at, smalls.at[other], smalls.at[other], device).wait_recv()
        wide = jnp.concatenate([smalls[k] for k in range(c.E * c.Y)], axis=1).astype(BF16)
        span = c.E * c.Y * 128
        src, dst = row_of((span, c.D)), lane_of((span, c.D))
        inside = lax.rem(src, 128)
        pick = jnp.logical_and(inside < c.sh, lax.div(src, 128) * c.sh + inside == dst)
        vec_ref[...] = mm(wide, jnp.where(pick, 1.0, 0.0).astype(BF16))
    vec = vec_ref[...]
    for image in range(c.N):
        rows = slice(image * c.B, (image + 1) * c.B)
        unit_one, _ = normalize(tok_ref[rows, :].astype(F32))
        norm_ref[rows, :] = (unit_one * vec[0:1] + vec[2:3]).astype(BF16)

    if c.gather:

        def got(at, z_at, y_at):
            copy_of(at, z_at, y_at, core_dev).wait_recv()

        def pass_y(at, z_at, core_at, condition):
            pl.when(condition)(lambda: got(at, z_at, 1 - y))
            send_if(condition, core_at, z_at, 1 - y, core_dev)

        for j in range(1, c.E):
            lower, upper = z >= j, z + j <= c.E - 1
            pl.when(lower)(lambda: got(up[j], z - j, y))
            if j < c.E - 1:
                send_if(jnp.logical_and(lower, z < c.E - 1), up[j + 1], z - j, y, above)
            send_if(lower, y_up[j], z - j, y, y_dev)
            send_if(lower, core_up[0][j], z - j, y, core_dev)
            pl.when(upper)(lambda: got(down[j], z + j, y))
            if j < c.E - 1:
                send_if(jnp.logical_and(upper, z > 0), down[j + 1], z + j, y, below)
            send_if(upper, y_down[j], z + j, y, y_dev)
            send_if(upper, core_down[0][j], z + j, y, core_dev)
            if j == 1:
                pass_y(y_up[0], z, core_up[1][0], always)
            else:
                pass_y(y_up[j - 1], z - j + 1, core_up[1][j - 1], z >= j - 1)
                pass_y(y_down[j - 1], z + j - 1, core_down[1][j - 1], z + j - 1 <= c.E - 1)
        last = c.E - 1
        pass_y(y_up[last], z - last, core_up[1][last], z >= last)
        pass_y(y_down[last], z + last, core_down[1][last], z + last <= c.E - 1)

        def got_core(at, z_at, y_at):
            there = other_unit(z_at, y_at)
            links.make(at, there, there, core_dev).wait_recv()

        for side in range(2):
            y_at = y if side == 0 else 1 - y
            if side:
                got_core(core_up[side][0], z, y_at)
            for j in range(1, c.E):
                pl.when(z >= j)(lambda: got_core(core_up[side][j], z - j, y_at))
                pl.when(z + j <= c.E - 1)(lambda: got_core(core_down[side][j], z + j, y_at))

    normed = norm_ref[...]
    own_at = pl.ds(pl.multiple_of(x * c.B, 32), c.B)
    kv_ids = [[links.new() for _ in range(3)] for _ in range(c.N)]
    keys = mm(normed, w_ref[1]).astype(BF16)
    values = mm(normed, w_ref[2]).astype(BF16)
    for image in range(c.N):
        rows = slice(image * c.B, (image + 1) * c.B)
        kv_ref[image, own_at, 0 : c.D] = keys[rows]
        kv_ref[image, own_at, c.D : 2 * c.D] = values[rows]
        block = kv_ref.at[image, own_at, :]
        go(kv_ids[image][0], block, block, far_dev)
        go(kv_ids[image][1], block, block, core_dev)
    dy_ids = [links.new() for _ in experts]
    for k, (at, device) in enumerate(zip(dy_ids, experts), 1):
        go(at, dysend.at[:, z ^ k], dyarr_ref.at[z], device)
    q_ref[...] = mm(normed, w_ref[0]).astype(BF16)

    block_of = lambda image, who: kv_ref.at[image, pl.ds(pl.multiple_of(who * c.B, 32), c.B), :]

    for image in range(c.N):
        rows = pl.ds(image * c.B, c.B)
        far_block = block_of(image, x ^ 2)
        links.make(kv_ids[image][0], far_block, far_block, far_dev).wait_recv()
        go(kv_ids[image][2], far_block, far_block, core_dev)
        near_block = block_of(image, x ^ 1)
        links.make(kv_ids[image][1], near_block, near_block, core_dev).wait_recv()
        cross_block = block_of(image, x ^ 3)
        links.make(kv_ids[image][2], cross_block, cross_block, core_dev).wait_recv()
        bias = key_bias(c, len_ref, image)

        def pair_step(pair, carry):
            lanes = pl.ds(pl.multiple_of(pair * 128, 128), 128)
            value_lanes = pl.ds(pl.multiple_of(c.D + pair * 128, 128), 128)
            queries = two_heads(q_ref[rows, lanes]) * jnp.asarray(c.scale, BF16)
            scores = mm(kv_ref[image, :, lanes], queries, NT) + bias
            top = jnp.max(scores, axis=0, keepdims=True)
            exponent = jnp.exp(scores - top)
            total = jnp.sum(exponent, axis=0, keepdims=True)
            probs = (exponent * (1.0 / total)).astype(BF16)
            lse_ref[image, pair] = jnp.broadcast_to(top + jnp.log(total), (8, 2 * c.B))
            mixed_values = mm(kv_ref[image, :, value_lanes].T, probs)
            att_ref[rows, lanes] = one_pair(mixed_values.T).astype(BF16)
            return carry

        lax.fori_loop(0, c.D // 128, pair_step, 0)

    branch = mm(att_ref[...], w_ref[3])
    hidden = tok_ref[...].astype(F32) + branch
    hid_ref[...] = hidden
    unit_two, _ = normalize(hidden)
    mixed = (unit_two * vec[1:2] + vec[3:4]).astype(BF16)
    mix_ref[...] = mixed
    pad = jnp.zeros((128 - c.r8, c.D), BF16)
    logits = mm(mixed, jnp.concatenate([vec.astype(BF16), pad], axis=0), NT)
    lane = lane_of((c.N * c.B, 128))
    valid = jnp.logical_and(lane >= LOGIT_LANE, lane < LOGIT_LANE + c.E)
    logits = jnp.where(valid, logits, -1e30)
    weight = jnp.exp(logits - jnp.max(logits, axis=1, keepdims=True))
    router = weight / jnp.sum(weight, axis=1, keepdims=True)
    router_ref[...] = router
    gsend_ref[...] = jnp.zeros_like(gsend_ref)
    lane = lane_of((c.B, 128))
    for image in range(c.N):
        rows = slice(image * c.B, (image + 1) * c.B)
        first, second, kept, slot_first, slot_second, place = choices[image]
        here = router[rows]
        gate_first = kept[:, 0:1] * jnp.sum(
            jnp.where(lane == LOGIT_LANE + first, here, 0.0), axis=1, keepdims=True
        )
        gate_second = kept[:, 1:2] * jnp.sum(
            jnp.where(lane == LOGIT_LANE + second, here, 0.0), axis=1, keepdims=True
        )
        send_ref[image] = mm(place, mixed[rows], TN).astype(BF16).reshape(c.E, c.cap, c.D)
        at = lane_of((c.B, c.cap))
        for expert in range(c.E):
            gates = jnp.where(at == slot_first - expert * c.cap, gate_first, 0.0)
            gates = gates + jnp.where(at == slot_second - expert * c.cap, gate_second, 0.0)
            gsend_ref[expert, image : image + 1, :] = jnp.sum(gates, axis=0, keepdims=True)
        columns = (
            slot_first.astype(F32),
            slot_second.astype(F32),
            kept[:, 0:1],
            kept[:, 1:2],
            gate_first,
            gate_second,
            first.astype(F32),
            second.astype(F32),
        )
        meta = jnp.zeros((c.B, 128), F32)
        for index, column in enumerate(columns):
            meta = jnp.where(lane == index, column, meta)
        meta_ref[rows, :] = meta

    for k, (at, device) in enumerate(zip(dy_ids, experts), 1):
        links.make(at, dyarr_ref.at[z ^ k], dyarr_ref.at[z ^ k], device).wait_recv()
    for copy in ends:
        copy.wait_send()
    if c.gather:
        for condition, at, z_at, y_at, device in pending:
            pl.when(condition)(lambda: copy_of(at, z_at, y_at, device).wait_send())


def spec(space):
    return pl.BlockSpec(memory_space=space)


def run_front(c, lengths, tok, route, keep, cot, weights):
    shape = jax.ShapeDtypeStruct
    made = [shape((4, c.D, c.D), BF16), shape((c.r8, c.D), F32)] if c.gather else []
    made += [
        shape((c.T, c.D), BF16),
        shape((c.N, c.S, 2 * c.D), BF16),
        shape((c.N, c.D // 128, 8, 2 * c.B), F32),
        shape((c.T, c.D), BF16),
        shape((c.T, c.D), F32),
        shape((c.T, c.D), BF16),
        shape((c.T, 128), F32),
        shape((c.T, 128), F32),
        shape((c.N, c.E, c.cap, c.D), BF16),
        shape((c.E, 8, c.cap), F32),
        shape((c.E, c.N, c.cap, c.D), BF16),
    ]
    count = 96 if c.gather else 2 * c.E + 16
    out = pl.pallas_call(
        functools.partial(front_kernel, c),
        out_shape=made,
        in_specs=[spec(pltpu.SMEM)] + [spec(pltpu.VMEM)] * (4 + len(weights)),
        out_specs=[spec(pltpu.VMEM)] * len(made),
        scratch_shapes=[
            pltpu.VMEM((c.E * c.Y, c.r8, 128), F32),
            pltpu.VMEM((c.N, c.E, c.cap, c.D), BF16),
            pltpu.VMEM((c.T, c.D), BF16),
            pltpu.SemaphoreType.DMA((count,)),
            pltpu.SemaphoreType.DMA((count,)),
        ],
        compiler_params=pltpu.CompilerParams(
            collective_id=0, has_side_effects=True, vmem_limit_bytes=VMEM_LIMIT
        ),
        name="front",
    )(lengths, tok, route, keep, cot, *weights)
    return out if c.gather else list(weights) + list(out)


def gelu_both(pre):
    inner = 0.7978845608028654 * (pre + 0.044715 * pre * pre * pre)
    bend = jnp.tanh(inner)
    half = 0.5 * (1.0 + bend)
    slope = 0.7978845608028654 * (1.0 + 0.134145 * pre * pre)
    return pre * half, half + 0.5 * pre * (1.0 - bend * bend) * slope


def expert_kernel(
    c,
    send_ref,
    gsend_ref,
    dyarr_ref,
    win_hbm,
    wdown_hbm,
    xback_ref,
    gback_ref,
    yloc_ref,
    grad_ref,
    win,
    wdown,
    arr,
    garr,
    act_all,
    dpre_all,
    dout_all,
    dxs,
    dgs,
    turned,
    wsem,
    ssem,
    rsem,
):
    links = Links(ssem, rsem)
    z, x, y = lax.axis_index("expert"), lax.axis_index("context"), lax.axis_index("dp")
    experts = [(z ^ k, x, y) for k in range(1, c.E)]
    load_in = pltpu.make_async_copy(win_hbm, win, wsem.at[0])
    load_down = pltpu.make_async_copy(wdown_hbm, wdown, wsem.at[1])
    load_in.start()
    load_down.start()
    greet(experts)
    ids = [[links.new() for _ in range(4)] for _ in range(c.E)]
    ends = []

    def go(at, src, dst, device):
        copy = links.make(at, src, dst, device)
        copy.start()
        ends.append(copy)

    for k in range(1, c.E):
        go(ids[k][0], send_ref.at[:, z ^ k], arr.at[z], experts[k - 1])
        go(ids[k][1], gsend_ref.at[z ^ k], garr.at[z], experts[k - 1])
    for image in range(c.N):
        arr[z, image] = send_ref[image, z]
    garr[z] = gsend_ref[z]
    load_in.wait()
    load_down.wait()
    dgs[...] = jnp.zeros_like(dgs)
    group = c.E // c.chunks
    height = group * c.N * c.cap
    for g in range(c.chunks):
        slab = lax.div(z, group) ^ g
        for k in range(g * group, (g + 1) * group):
            if k:
                there = z ^ k
                links.make(ids[k][0], arr.at[there], arr.at[there], experts[k - 1]).wait_recv()
                links.make(ids[k][1], garr.at[there], garr.at[there], experts[k - 1]).wait_recv()
        start = pl.multiple_of(slab * height, 32)
        rows = pl.ds(start, height)
        for member in range(group):
            source = slab * group + member
            for image in range(c.N):
                gates = to_column(garr[source, image : image + 1, :])
                offset = (member * c.N + image) * c.cap
                part = pl.ds(pl.multiple_of(start + offset, 16), c.cap)
                dout_all[part, :] = (gates * dyarr_ref[source, image].astype(F32)).astype(BF16)
        inputs = arr[pl.ds(slab * group, group)].reshape(height, c.D)
        douts = dout_all[rows, :]

        def ff_step(step, carry):
            lanes = pl.ds(pl.multiple_of(step * c.FB, 128), c.FB)
            pre = mm(inputs, win[:, lanes])
            act, slope = gelu_both(pre)
            act_all[rows, lanes] = act.astype(BF16)
            dact = mm(douts, wdown[lanes, :], NT)
            dpre_all[rows, lanes] = (dact * slope).astype(BF16)
            return carry

        lax.fori_loop(0, c.FF // c.FB, ff_step, 0)
        dx = mm(dpre_all[rows, :], win[...], NT).astype(BF16)
        dxs[pl.ds(slab * group, group)] = dx.reshape(group, c.N, c.cap, c.D)
        made = mm(act_all[rows, :], wdown[...]).astype(BF16)
        yloc_ref[pl.ds(slab * group, group)] = made.reshape(group, c.N, c.cap, c.D)
        for member in range(group):
            source = slab * group + member
            for image in range(c.N):
                offset = (member * c.N + image) * c.cap
                dots = made[offset : offset + c.cap].astype(F32) * dyarr_ref[source, image].astype(
                    F32
                )
                dgs[source, image : image + 1, :] = to_row(jnp.sum(dots, axis=1, keepdims=True))
        for k in range(g * group, (g + 1) * group):
            if k:
                there = z ^ k
                go(ids[k][2], dxs.at[there], xback_ref.at[:, z], experts[k - 1])
                go(ids[k][3], dgs.at[there], gback_ref.at[z], experts[k - 1])
    for image in range(c.N):
        xback_ref[image, z] = dxs[z, image]
    gback_ref[z] = dgs[z]

    total = c.E * c.N * c.cap
    turned[0] = arr[...].reshape(total, c.D).T
    turned[1] = dout_all[...].T

    def grad_step(step, carry):
        lanes = pl.ds(pl.multiple_of(step * c.FB, 128), c.FB)
        grad_ref[0, :, lanes] = mm(turned[0], dpre_all[:, lanes]).astype(BF16)
        grad_ref[1, :, lanes] = mm(turned[1], act_all[:, lanes]).astype(BF16)
        return carry

    lax.fori_loop(0, c.FF // c.FB, grad_step, 0)
    for k in range(1, c.E):
        there = z ^ k
        links.make(ids[k][2], xback_ref.at[:, there], xback_ref.at[:, there], experts[k - 1]).wait_recv()
        links.make(ids[k][3], gback_ref.at[there], gback_ref.at[there], experts[k - 1]).wait_recv()
    for copy in ends:
        copy.wait_send()


def run_experts(c, send, gsend, dyarr, w_in, w_down):
    shape = jax.ShapeDtypeStruct
    total = c.E * c.N * c.cap
    count = 4 * c.E
    return pl.pallas_call(
        functools.partial(expert_kernel, c),
        out_shape=[
            shape((c.N, c.E, c.cap, c.D), BF16),
            shape((c.E, 8, c.cap), F32),
            shape((c.E, c.N, c.cap, c.D), BF16),
            shape((2, c.D, c.FF), BF16),
        ],
        in_specs=[spec(pltpu.VMEM)] * 3 + [spec(pl.ANY)] * 2,
        out_specs=[spec(pltpu.VMEM)] * 4,
        scratch_shapes=[
            pltpu.VMEM((c.D, c.FF), BF16),
            pltpu.VMEM((c.FF, c.D), BF16),
            pltpu.VMEM((c.E, c.N, c.cap, c.D), BF16),
            pltpu.VMEM((c.E, 8, c.cap), F32),
            pltpu.VMEM((total, c.FF), BF16),
            pltpu.VMEM((total, c.FF), BF16),
            pltpu.VMEM((total, c.D), BF16),
            pltpu.VMEM((c.E, c.N, c.cap, c.D), BF16),
            pltpu.VMEM((c.E, 8, c.cap), F32),
            pltpu.VMEM((2, c.D, total), BF16),
            pltpu.SemaphoreType.DMA((2,)),
            pltpu.SemaphoreType.DMA((count,)),
            pltpu.SemaphoreType.DMA((count,)),
        ],
        compiler_params=pltpu.CompilerParams(
            collective_id=1, has_side_effects=True, vmem_limit_bytes=VMEM_LIMIT
        ),
        name="experts",
    )(send, gsend, dyarr, w_in, w_down)


def in_parts(values, count):
    parts = []
    for _ in range(count):
        parts.append(values.astype(BF16))
        values = values - parts[-1].astype(F32)
    return parts


def back_kernel(c, *refs):
    refs = list(refs)
    take = lambda count: [refs.pop(0) for _ in range(count)]
    len_ref, tok_ref, cot_ref, vec_ref, q_ref, lse_ref, att_ref, hid_ref, mix_ref = take(9)
    meta_ref, router_ref, xback_ref, gback_ref = take(4)
    w_hbm, kv_hbm, yloc_hbm, grad_hbm = take(4)
    out_ref, gtok_ref, gin_ref, gdown_ref = take(4)
    if c.gather:
        gqkv_ref, gout_ref, gsmall_ref = take(3)
    else:
        dd, gsmall_ref = take(2)
    w_ref, kv_ref, made = take(3)
    gsum, gcore, gy, gx = take(4)
    dkv, kvcore, kvfar, dproj, datt, dhid, norm_t, router_sum = take(8)
    if c.gather:
        dd, dcore, done_x, done_y, done_z, whole, small, small_in = take(8)
    lsem, ssem, rsem = take(3)
    links = Links(ssem, rsem)
    z, x, y = lax.axis_index("expert"), lax.axis_index("context"), lax.axis_index("dp")
    core, side = lax.rem(x, 2), lax.div(x, 2)
    core_dev, far_dev, y_dev = (z, x ^ 1, y), (z, x ^ 2, y), (z, x, 1 - y)
    experts = [(z ^ k, x, y) for k in range(1, c.E)]
    ends = []

    def go(at, src, dst, device):
        copy = links.make(at, src, dst, device)
        copy.start()
        ends.append(copy)

    def got(at, dst, device):
        links.make(at, dst, dst, device).wait_recv()

    half = c.FF // 4
    piece = half // 2
    loads = [
        pltpu.make_async_copy(w_hbm, w_ref, lsem.at[0]),
        pltpu.make_async_copy(kv_hbm, kv_ref, lsem.at[1]),
    ]
    own_start = pl.multiple_of(core * half, 128)
    for part in range(2):
        columns = pl.ds(pl.multiple_of(part * 2 * half + own_start, 128), half)
        loads.append(
            pltpu.make_async_copy(grad_hbm.at[:, :, columns], gsum.at[part], lsem.at[2 + part])
        )
    loads.append(pltpu.make_async_copy(yloc_hbm.at[z], made.at[:, z], lsem.at[4]))
    for load in loads:
        load.start()
    greet([core_dev, far_dev, y_dev] + experts)

    made_ids = [links.new() for _ in experts]
    for k, (at, device) in enumerate(zip(made_ids, experts), 1):
        go(at, yloc_hbm.at[z ^ k], made.at[:, z], device)
    gcore_ids = [[links.new() for _ in range(2)] for _ in range(2)]
    other_start = (1 - core) * half
    for part in range(2):
        columns = pl.ds(pl.multiple_of(part * 2 * half + other_start, 128), half)
        for which in range(2):
            go(
                gcore_ids[part][which],
                grad_hbm.at[which, :, columns],
                gcore.at[part, which],
                core_dev,
            )
    gy_ids = [[links.new() for _ in range(2)] for _ in range(2)]
    gx_ids = [links.new() for _ in range(2)]
    own_piece = pl.ds(pl.multiple_of(y * piece, 128), piece)
    other_piece = pl.ds(pl.multiple_of((1 - y) * piece, 128), piece)

    def grads_after_core():
        loads[2].wait()
        loads[3].wait()
        for order in range(2):
            part = 1 - side if order == 0 else side
            for which in range(2):
                for p in range(2):
                    if order == 0:
                        got(gcore_ids[p][which], gcore.at[p, which], core_dev)
                gsum[part, which] = (
                    gsum[part, which].astype(F32) + gcore[part, which].astype(F32)
                ).astype(BF16)
                go(
                    gy_ids[order][which],
                    gsum.at[part, which, :, other_piece],
                    gy.at[order, which],
                    y_dev,
                )

    def grads_after_y_far():
        part = 1 - side
        for which in range(2):
            got(gy_ids[0][which], gy.at[0, which], y_dev)
            gsum[part, which, :, own_piece] = (
                gsum[part, which, :, own_piece].astype(F32) + gy[0, which].astype(F32)
            ).astype(BF16)
            go(gx_ids[which], gsum.at[part, which, :, own_piece], gx.at[which], far_dev)

    def grads_end():
        for which in range(2):
            got(gy_ids[1][which], gy.at[1, which], y_dev)
            got(gx_ids[which], gx.at[which], far_dev)
            total = gsum[side, which, :, own_piece].astype(F32) + gy[1, which].astype(F32)
            total = total + gx[which].astype(F32)
            if which == 0:
                gin_ref[...] = total
            else:
                gdown_ref[...] = total.T

    if c.gather:
        n_dense = 4
        core_cols = c.D // 2
        keep_cols = pl.ds(pl.multiple_of(core * core_cols, 128), core_cols)
        give_cols = pl.ds(pl.multiple_of((1 - core) * core_cols, 128), core_cols)
        rows_half = c.sh // 2
        keep_rows = pl.ds(pl.multiple_of(side * rows_half, 16), rows_half)
        give_rows = pl.ds(pl.multiple_of((1 - side) * rows_half, 16), rows_half)
        ids_core = [links.new() for _ in range(n_dense)]
        ids_x = [links.new() for _ in range(n_dense)]
        ids_y = [links.new() for _ in range(n_dense)]
        ids_z = [[links.new() for _ in experts] for _ in range(n_dense)]
        ids_far = [links.new() for _ in range(n_dense)]
        ids_own = [links.new() for _ in range(n_dense)]
        ids_cross = [links.new() for _ in range(n_dense)]

        def dense_start(m, value):
            dd[m] = value.astype(BF16).reshape(c.E, c.Y, c.sh, c.D)
            go(ids_core[m], dd.at[m, :, :, :, give_cols], dcore.at[m], core_dev)

        def dense_x(m):
            got(ids_core[m], dcore.at[m], core_dev)
            dd[m, :, :, :, keep_cols] = (
                dd[m, :, :, :, keep_cols].astype(F32) + dcore[m].astype(F32)
            ).astype(BF16)
            go(ids_x[m], dd.at[m, :, :, give_rows, keep_cols], done_x.at[m], far_dev)

        def dense_y(m):
            got(ids_x[m], done_x.at[m], far_dev)
            dd[m, :, :, keep_rows, keep_cols] = (
                dd[m, :, :, keep_rows, keep_cols].astype(F32) + done_x[m].astype(F32)
            ).astype(BF16)
            go(ids_y[m], dd.at[m, :, 1 - y, keep_rows, keep_cols], done_y.at[m], y_dev)

        def dense_z(m):
            got(ids_y[m], done_y.at[m], y_dev)
            dd[m, :, y, keep_rows, keep_cols] = (
                dd[m, :, y, keep_rows, keep_cols].astype(F32) + done_y[m].astype(F32)
            ).astype(BF16)
            for k, device in enumerate(experts, 1):
                go(
                    ids_z[m][k - 1],
                    dd.at[m, z ^ k, y, keep_rows, keep_cols],
                    done_z.at[m, z],
                    device,
                )

        def dense_share(m):
            total = dd[m, z, y, keep_rows, keep_cols].astype(F32)
            for k, device in enumerate(experts, 1):
                got(ids_z[m][k - 1], done_z.at[m, z ^ k], device)
                total = total + done_z[m, z ^ k].astype(F32)
            whole[m, side, core] = total
            own = whole.at[m, side, core]
            go(ids_far[m], own, own, far_dev)
            go(ids_own[m], own, own, core_dev)

        def dense_cross(m):
            there = whole.at[m, 1 - side, core]
            got(ids_far[m], there, far_dev)
            go(ids_cross[m], there, there, core_dev)

        def dense_end(m):
            there = whole.at[m, side, 1 - core]
            got(ids_own[m], there, core_dev)
            there = whole.at[m, 1 - side, 1 - core]
            got(ids_cross[m], there, core_dev)
            for s in range(2):
                for k in range(2):
                    rows = slice(s * rows_half, (s + 1) * rows_half)
                    if m == 3:
                        gout_ref[rows, k * core_cols : (k + 1) * core_cols] = whole[m, s, k]
                    else:
                        start = m * c.D + k * core_cols
                        gqkv_ref[rows, start : start + core_cols] = whole[m, s, k]

    else:

        def dense_start(m, value):
            dd[m] = value.astype(BF16)

    vec = vec_ref[...]
    lane = lane_of((c.B, 128))
    d_mixed, dy_rows, lives = [], [], []
    d_logits = []
    for image in range(c.N):
        rows = slice(image * c.B, (image + 1) * c.B)
        meta = meta_ref[rows, :]
        slots = [meta[:, j : j + 1].astype(jnp.int32) for j in range(2)]
        kept = [meta[:, 2 + j : 3 + j] for j in range(2)]
        names = [meta[:, 6 + j : 7 + j].astype(jnp.int32) for j in range(2)]
        at = lane_of((c.B, c.E * c.cap))
        place = jnp.where(at == slots[0], kept[0], 0.0) + jnp.where(at == slots[1], kept[1], 0.0)
        copies = xback_ref[image].reshape(c.E * c.cap, c.D)
        d_mixed.append(mm(place.astype(BF16), copies))
        d_router = jnp.zeros((c.B, 128), F32)
        at = lane_of((c.B, c.cap))
        for j in range(2):
            d_gate = jnp.zeros((c.B, c.cap), F32)
            for expert in range(c.E):
                row = gback_ref[expert, image : image + 1, :]
                d_gate = d_gate + jnp.where(at == slots[j] - expert * c.cap, row, 0.0)
            d_gate = jnp.sum(d_gate, axis=1, keepdims=True) * kept[j]
            d_router = d_router + jnp.where(lane == LOGIT_LANE + names[j], d_gate, 0.0)
        router = router_ref[rows, :]
        dot = jnp.sum(router * d_router, axis=1, keepdims=True)
        d_logits.append(router * (d_router - dot))
        live = jnp.where(row_of((c.B, 1)) < len_ref[image, x], 1.0, 0.0)
        lives.append(live)
        dy_rows.append(cot_ref[rows, :].astype(F32) * live)
    d_mixed = jnp.concatenate(d_mixed, axis=0)
    d_logits = jnp.concatenate(d_logits, axis=0)
    dy_rows = jnp.concatenate(dy_rows, axis=0)
    logit_rows = jnp.concatenate([vec, jnp.zeros((128 - c.r8, c.D), F32)], axis=0)
    lane_here = row_of((128, c.D))
    is_router = jnp.logical_and(lane_here >= LOGIT_LANE, lane_here < LOGIT_LANE + c.E)
    w_router = jnp.where(is_router, logit_rows, 0.0)
    high, low = in_parts(d_logits, 2)
    w_router = w_router.astype(BF16)
    d_mixed = d_mixed + mm(high, w_router) + mm(low, w_router)
    router_sum[...] = mm(high, mix_ref[...], TN) + mm(low, mix_ref[...], TN)
    unit_two, inverse_two = normalize(hid_ref[...])
    gains_two = jnp.sum(d_mixed * unit_two, axis=0, keepdims=True)
    biases_two = jnp.sum(d_mixed, axis=0, keepdims=True)
    d_hidden = dy_rows + normalize_back(d_mixed, unit_two, inverse_two, vec[1:2])
    dhid[...] = d_hidden
    d_branch = d_hidden.astype(BF16)
    dense_start(3, mm(att_ref[...], d_branch, TN))
    loads[0].wait()
    datt[...] = mm(d_branch, w_ref[3], NT).astype(BF16)
    unit_one, inverse_one = normalize(tok_ref[...].astype(F32))
    norm_t[...] = (unit_one * vec[0:1] + vec[2:3]).astype(BF16).T
    grads_after_core()
    loads[1].wait()

    kvcore_ids = [[links.new() for _ in range(2)] for _ in range(c.N)]
    kvfar_ids = [links.new() for _ in range(c.N)]

    def block_rows(who):
        return pl.ds(pl.multiple_of(who * c.B, 32), c.B)

    def attend_back(image, first_pair, last_pair):
        rows = pl.ds(image * c.B, c.B)
        bias = key_bias(c, len_ref, image)

        def pair_step(pair, carry):
            lanes = pl.ds(pl.multiple_of(pair * 128, 128), 128)
            value_lanes = pl.ds(pl.multiple_of(c.D + pair * 128, 128), 128)
            scale = jnp.asarray(c.scale, BF16)
            queries = two_heads(q_ref[rows, lanes]) * scale
            grads = two_heads(datt[rows, lanes])
            keys = kv_ref[image, :, lanes]
            probs = jnp.exp(mm(keys, queries, NT) + bias - lse_ref[image, pair][0:1])
            d_probs = mm(kv_ref[image, :, value_lanes], grads, NT)
            dot = jnp.sum(probs * d_probs, axis=0, keepdims=True)
            d_scores = (probs * (d_probs - dot)).astype(BF16)
            dkv[image, :, value_lanes] = mm(probs.astype(BF16), grads).astype(BF16)
            dkv[image, :, lanes] = mm(d_scores, queries).astype(BF16)
            d_queries = mm(keys.T, d_scores).T
            dproj[rows, lanes] = (one_pair(d_queries) * c.scale).astype(BF16)
            return carry

        lax.fori_loop(first_pair, last_pair, pair_step, 0)

    def kv_to_core(image):
        for s in range(2):
            block = dkv.at[image, block_rows(2 * s + 1 - core), :]
            go(kvcore_ids[image][s], block, kvcore.at[image, s], core_dev)

    def kv_to_far(image):
        for s in range(2):
            got(kvcore_ids[image][s], kvcore.at[image, s], core_dev)
        rows = block_rows(2 * (1 - side) + core)
        dkv[image, rows, :] = (
            dkv[image, rows, :].astype(F32) + kvcore[image, 1 - side].astype(F32)
        ).astype(BF16)
        go(kvfar_ids[image], dkv.at[image, rows, :], kvfar.at[image], far_dev)

    def kv_end(image):
        got(kvfar_ids[image], kvfar.at[image], far_dev)
        total = dkv[image, block_rows(2 * side + core), :].astype(F32)
        total = total + kvcore[image, side].astype(F32) + kvfar[image].astype(F32)
        rows = pl.ds(image * c.B, c.B)
        dproj[rows, c.D : 3 * c.D] = total.astype(BF16)

    pairs = c.D // 128
    attend_back(0, 0, pairs)
    kv_to_core(0)
    if c.gather:
        dense_x(3)
    attend_back(1, 0, pairs // 2)
    kv_to_far(0)
    if c.gather:
        dense_y(3)
    attend_back(1, pairs // 2, pairs)
    kv_to_core(1)
    dense_start(0, mm(norm_t[...], dproj[:, 0 : c.D]))
    grads_after_y_far()
    kv_to_far(1)
    kv_end(0)
    if c.gather:
        dense_x(0)
        dense_z(3)
    kv_end(1)
    dense_start(1, mm(norm_t[...], dproj[:, c.D : 2 * c.D]))
    dense_start(2, mm(norm_t[...], dproj[:, 2 * c.D : 3 * c.D]))
    if c.gather:
        dense_y(0)
        dense_x(1)
        dense_x(2)
    d_normed = mm(dproj[:, 0 : c.D], w_ref[0], NT)
    d_normed = d_normed + mm(dproj[:, c.D : 2 * c.D], w_ref[1], NT)
    d_normed = d_normed + mm(dproj[:, 2 * c.D : 3 * c.D], w_ref[2], NT)
    unit_one, inverse_one = normalize(tok_ref[...].astype(F32))
    gains_one = jnp.sum(d_normed * unit_one, axis=0, keepdims=True)
    biases_one = jnp.sum(d_normed, axis=0, keepdims=True)
    small_here = jnp.concatenate([gains_one, gains_two, biases_one, biases_two], axis=0)
    small_here = jnp.concatenate(
        [small_here, router_sum[LOGIT_LANE : LOGIT_LANE + c.r8 - 4]], axis=0
    )
    if c.gather:
        small[0] = small_here
        small_ids = [links.new() for _ in range(3)]
        small_z = [links.new() for _ in experts]
        go(small_ids[0], small.at[0], small_in.at[0], core_dev)
    gtok_ref[...] = dhid[...] + normalize_back(d_normed, unit_one, inverse_one, vec[0:1])

    def block_output():
        loads[4].wait()
        for k, (at, device) in enumerate(zip(made_ids, experts), 1):
            got(at, made.at[:, z ^ k], device)
        for image in range(c.N):
            rows = slice(image * c.B, (image + 1) * c.B)
            meta = meta_ref[rows, :]
            slots = [meta[:, j : j + 1].astype(jnp.int32) for j in range(2)]
            at = lane_of((c.B, c.E * c.cap))
            gates = jnp.where(at == slots[0], meta[:, 4:5], 0.0)
            gates = gates + jnp.where(at == slots[1], meta[:, 5:6], 0.0)
            high, low = in_parts(gates, 2)
            rows_made = made[image].reshape(c.E * c.cap, c.D)
            mixture = mm(high, rows_made) + mm(low, rows_made)
            out_ref[rows, :] = (lives[image] * (hid_ref[rows, :] + mixture)).astype(BF16)

    if c.gather:

        def small_step(step, device):
            source = core_dev if step == 0 else far_dev if step == 1 else y_dev
            got(small_ids[step], small_in.at[step], source)
            small[step + 1] = small[step] + small_in[step]
            if step < 2:
                go(small_ids[step + 1], small.at[step + 1], small_in.at[step + 1], device)

        small_step(0, far_dev)
        dense_z(0)
        dense_share(3)
        dense_y(1)
        dense_y(2)
        small_step(1, y_dev)
        block_output()
        small_step(2, None)
        for k, (at, device) in enumerate(zip(small_z, experts), 1):
            go(at, small.at[3], small_in.at[3 + z], device)
        dense_z(1)
        dense_z(2)
        dense_cross(3)
        dense_share(0)
        dense_end(3)
        total = small[3]
        for k, (at, device) in enumerate(zip(small_z, experts), 1):
            got(at, small_in.at[3 + (z ^ k)], device)
            total = total + small_in[3 + (z ^ k)]
        src, dst = row_of((c.D, 128)), lane_of((c.D, 128))
        pick = jnp.logical_and(dst < c.sh, src == dst + (z * c.Y + y) * c.sh)
        pick = jnp.where(pick, 1.0, 0.0).astype(BF16)
        gsmall_ref[...] = sum(mm(part, pick) for part in in_parts(total, 3))
        dense_cross(0)
        dense_share(1)
        dense_share(2)
        dense_end(0)
        dense_cross(1)
        dense_cross(2)
        grads_end()
        dense_end(1)
        dense_end(2)
    else:
        gsmall_ref[...] = small_here
        block_output()
        grads_end()
    for copy in ends:
        copy.wait_send()


def run_back(c, tok, cot, lengths, weights, vec, q, kv, lse, att, hid, mix, meta, router, xback, gback, yloc, grads):
    shape = jax.ShapeDtypeStruct
    piece = c.FF // 8
    made = [
        shape((c.T, c.D), BF16),
        shape((c.T, c.D), F32),
        shape((c.D, piece), F32),
        shape((piece, c.D), F32),
    ]
    dense_scratch = []
    if c.gather:
        made += [
            shape((c.sh, 3 * c.D), F32),
            shape((c.sh, c.D), F32),
            shape((c.r8, 128), F32),
        ]
        half_rows, half_cols = c.sh // 2, c.D // 2
        dense_scratch = [
            pltpu.VMEM((4, c.E, c.Y, c.sh, c.D), BF16),
            pltpu.VMEM((4, c.E, c.Y, c.sh, half_cols), BF16),
            pltpu.VMEM((4, c.E, c.Y, half_rows, half_cols), BF16),
            pltpu.VMEM((4, c.E, half_rows, half_cols), BF16),
            pltpu.VMEM((4, c.E, half_rows, half_cols), BF16),
            pltpu.VMEM((4, 2, 2, half_rows, half_cols), F32),
            pltpu.VMEM((4, c.r8, c.D), F32),
            pltpu.VMEM((3 + c.E, c.r8, c.D), F32),
        ]
    else:
        made += [shape((4, c.D, c.D), BF16), shape((c.r8, c.D), F32)]
    count = 5 * c.E + 64
    results = pl.pallas_call(
        functools.partial(back_kernel, c),
        out_shape=made,
        in_specs=[spec(pltpu.SMEM)] + [spec(pltpu.VMEM)] * 12 + [spec(pl.ANY)] * 4,
        out_specs=[spec(pltpu.VMEM)] * len(made),
        scratch_shapes=[
            pltpu.VMEM((4, c.D, c.D), BF16),
            pltpu.VMEM((c.N, c.S, 2 * c.D), BF16),
            pltpu.VMEM((c.N, c.E, c.cap, c.D), BF16),
            pltpu.VMEM((2, 2, c.D, 2 * piece), BF16),
            pltpu.VMEM((2, 2, c.D, 2 * piece), BF16),
            pltpu.VMEM((2, 2, c.D, piece), BF16),
            pltpu.VMEM((2, c.D, piece), BF16),
            pltpu.VMEM((c.N, c.S, 2 * c.D), BF16),
            pltpu.VMEM((c.N, 2, c.B, 2 * c.D), BF16),
            pltpu.VMEM((c.N, c.B, 2 * c.D), BF16),
            pltpu.VMEM((c.T, 3 * c.D), BF16),
            pltpu.VMEM((c.T, c.D), BF16),
            pltpu.VMEM((c.T, c.D), F32),
            pltpu.VMEM((c.D, c.T), BF16),
            pltpu.VMEM((128, c.D), F32),
            *dense_scratch,
            pltpu.SemaphoreType.DMA((5,)),
            pltpu.SemaphoreType.DMA((count,)),
            pltpu.SemaphoreType.DMA((count,)),
        ],
        compiler_params=pltpu.CompilerParams(
            collective_id=2, has_side_effects=True, vmem_limit_bytes=VMEM_LIMIT
        ),
        name="back",
    )(lengths, tok, cot, vec, q, lse, att, hid, mix, meta, router, xback, gback, weights, kv, yloc, grads)
    out, g_tok, g_in, g_down = results[:4]
    if c.gather:
        g_qkv, g_out, small = results[4:]
        small = small[:, : c.sh]
    else:
        dense, small = results[4:]
        both = ("expert", "dp")
        flat = dense.astype(F32).transpose(1, 0, 2).reshape(c.D, 4 * c.D)
        flat = lax.psum_scatter(flat, both, scatter_dimension=0, tiled=True)
        small = lax.psum_scatter(small, both, scatter_dimension=1, tiled=True)
        flat, small = lax.psum((flat, small), "context")
        g_qkv, g_out = flat[:, : 3 * c.D], flat[:, 3 * c.D :]
    rows = (c.N, c.B, c.D)
    return (
        out.reshape(rows),
        g_tok.reshape(rows),
        g_qkv,
        g_out,
        small[LOGIT_LANE : LOGIT_LANE + c.E].T,
        small[0:2],
        small[2:4],
        g_in[None],
        g_down[None],
    )


def pack_small(c, w_router, norm_gains, norm_biases):
    rows = jnp.concatenate([norm_gains, norm_biases, w_router.T], axis=0).astype(F32)
    return jnp.pad(rows, ((0, c.r8 - rows.shape[0]), (0, 128 - rows.shape[1])))


def per_device(
    mesh_shape,
    tokens,
    lengths,
    route_ids,
    keep_mask,
    w_qkv,
    w_attn_out,
    w_router,
    norm_gains,
    norm_biases,
    w_expert_in,
    w_expert_down,
    cotangent,
):
    images, block, width = tokens.shape
    experts = mesh_shape["expert"] * w_expert_in.shape[0]
    c = types.SimpleNamespace(
        E=experts,
        Y=mesh_shape["dp"],
        C=mesh_shape["context"],
        N=images,
        B=block,
        D=width,
        T=images * block,
        S=mesh_shape["context"] * block,
        FF=w_expert_in.shape[2],
        FB=512,
        cap=max(2, 16 * block // (5 * experts)),
        sh=w_qkv.shape[0],
        r8=-(-(LOGIT_LANE + experts) // 8) * 8,
        scale=(width // HEADS) ** -0.5,
        chunks=4,
    )
    c.gather = c.sh % 32 == 0
    tok = tokens.reshape(c.T, width)
    cot = cotangent.reshape(c.T, width)
    route = route_ids.reshape(c.T, 2)
    keep = keep_mask.reshape(c.T, 2)
    both = ("expert", "dp")
    if c.gather:
        given = (w_qkv, w_attn_out, pack_small(c, w_router, norm_gains, norm_biases))
    else:
        qkv = lax.all_gather(w_qkv, both, axis=0, tiled=True)
        out = lax.all_gather(w_attn_out, both, axis=0, tiled=True)
        small = pack_small(c, w_router, norm_gains, norm_biases)[:, : c.sh]
        vec = lax.all_gather(small, both, axis=1, tiled=True)
        stacked = jnp.concatenate([qkv, out], axis=1).reshape(width, 4, width).transpose(1, 0, 2)
        given = (stacked, vec)
    front = run_front(c, lengths, tok, route, keep, cot, given)
    weights, vec, q, kv, lse, att, hid, mix, meta, router, send, gsend, dyarr = front
    back = run_experts(c, send, gsend, dyarr, w_expert_in[0], w_expert_down[0])
    return run_back(
        c, tok, cot, lengths, weights, vec, q, kv, lse, att, hid, mix, meta, router, *back
    )


def solution(mesh):
    rows = P(("expert", "dp"), "context", None)
    shard = P(("expert", "dp"), None)
    column = P(None, ("expert", "dp"))
    expert = P("expert", None, None)
    return jax.shard_map(
        functools.partial(per_device, dict(mesh.shape)),
        mesh=mesh,
        in_specs=(rows, shard, rows, rows, shard, shard, shard, column, column, expert, expert, rows),
        out_specs=(
            rows,
            rows,
            shard,
            shard,
            shard,
            column,
            column,
            P("expert", None, ("context", "dp")),
            P("expert", ("context", "dp"), None),
        ),
        check_vma=False,
    )
```

```python
import functools
import itertools
import types

import jax
import jax.numpy as jnp
from jax import lax
from jax.experimental import pallas as pl
from jax.experimental.pallas import tpu as pltpu
from jax.sharding import PartitionSpec as P

HEADS = 12
EPS = 1e-06
F32 = jnp.float32
BF16 = jnp.bfloat16
MESH = pl.DeviceIdType.MESH
NN = (((1,), (0,)), ((), ()))
NT = (((1,), (1,)), ((), ()))
TN = (((0,), (0,)), ((), ()))
VMEM_LIMIT = 60 * 2**20
LOGIT_LANE = 4


def mm(left, right, dims=NN):
    return lax.dot_general(left, right, dims, preferred_element_type=F32)


def lane_of(shape):
    return lax.broadcasted_iota(jnp.int32, shape, 1)


def row_of(shape):
    return lax.broadcasted_iota(jnp.int32, shape, 0)


class Links:
    def __init__(self, send, recv):
        self.send, self.recv, self.ids = send, recv, itertools.count()

    def new(self):
        return next(self.ids)

    def make(self, at, src, dst, device):
        return pltpu.make_async_remote_copy(
            src_ref=src,
            dst_ref=dst,
            send_sem=self.send.at[at],
            recv_sem=self.recv.at[at],
            device_id=device,
            device_id_type=MESH,
        )


def greet(devices):
    barrier = pltpu.get_barrier_semaphore()
    for device in devices:
        pl.semaphore_signal(barrier, inc=1, device_id=device, device_id_type=MESH)
    pl.semaphore_wait(barrier, len(devices))


def normalize(values):
    centred = values - jnp.mean(values, axis=-1, keepdims=True)
    inverse = lax.rsqrt(jnp.mean(centred * centred, axis=-1, keepdims=True) + EPS)
    return centred * inverse, inverse


def normalize_back(grad_out, unit_rows, inverse, gain):
    scaled = grad_out * gain
    centre_term = jnp.mean(scaled, axis=-1, keepdims=True)
    slope_term = jnp.mean(scaled * unit_rows, axis=-1, keepdims=True)
    return inverse * (scaled - centre_term - unit_rows * slope_term)


def to_column(row):
    size = row.shape[1]
    eye = row_of((size, size)) == lane_of((size, size))
    return jnp.sum(jnp.where(eye, row, 0.0), axis=1, keepdims=True)


def to_row(column):
    size = column.shape[0]
    eye = row_of((size, size)) == lane_of((size, size))
    return jnp.sum(jnp.where(eye, column, 0.0), axis=0, keepdims=True)


def key_bias(c, len_ref, image):
    at = row_of((c.S, 1))
    bias = jnp.full((c.S, 1), -1e30, F32)
    for block in range(c.C):
        start = block * c.B
        inside = jnp.logical_and(at >= start, at < start + len_ref[image, block])
        bias = jnp.where(inside, 0.0, bias)
    return bias


def two_heads(pair):
    first = lane_of(pair.shape) < pair.shape[1] // 2
    zero = jnp.zeros_like(pair)
    return jnp.concatenate([jnp.where(first, pair, zero), jnp.where(first, zero, pair)], axis=0)


def one_pair(stacked):
    half = stacked.shape[0] // 2
    first = lane_of((half, stacked.shape[1])) < stacked.shape[1] // 2
    return jnp.where(first, stacked[:half], stacked[half:])


class Gather:
    def __init__(self, c, links, w_ref, rows_of, z, y, own_part, other_part):
        self.c, self.links, self.w_ref, self.rows_of = c, links, w_ref, rows_of
        self.z, self.y, self.own_part, self.other_part = z, y, own_part, other_part
        span = range(c.E)
        self.up = [links.new() for _ in span]
        self.down = [links.new() for _ in span]
        self.y_up = [links.new() for _ in span]
        self.y_down = [links.new() for _ in span]
        self.core_up = [[links.new() for _ in span] for _ in range(2)]
        self.core_down = [[links.new() for _ in span] for _ in range(2)]
        self.sent = []

    def route(self, above, below, y_dev, core_dev):
        self.above, self.below, self.y_dev, self.core_dev = above, below, y_dev, core_dev

    def unit(self, at, z_at, y_at, device, part=None):
        ref = self.w_ref.at[self.own_part if part is None else part, self.rows_of(z_at, y_at), :]
        return self.links.make(at, ref, ref, device)

    def send(self, condition, *where):
        pl.when(condition)(lambda: self.unit(*where).start())
        self.sent.append((condition, where))

    def got(self, condition, at, z_at, y_at, part=None):
        pl.when(condition)(lambda: self.unit(at, z_at, y_at, self.core_dev, part).wait_recv())

    def open(self):
        z, y = self.z, self.y
        self.send(z < self.c.E - 1, self.up[1], z, y, self.above)
        self.send(z > 0, self.down[1], z, y, self.below)
        self.send(z >= 0, self.y_up[0], z, y, self.y_dev)

    def pass_y(self, j):
        z, y = self.z, 1 - self.y
        lower, upper = z >= j, z + j <= self.c.E - 1
        self.got(lower, self.y_up[j], z - j, y)
        self.send(lower, self.core_up[1][j], z - j, y, self.core_dev)
        if j:
            self.got(upper, self.y_down[j], z + j, y)
            self.send(upper, self.core_down[1][j], z + j, y, self.core_dev)

    def step(self, j):
        z, y, last = self.z, self.y, self.c.E - 1
        if j <= last:
            lower, upper = z >= j, z + j <= last
            self.got(lower, self.up[j], z - j, y)
            if j < last:
                self.send(jnp.logical_and(lower, z < last), self.up[j + 1], z - j, y, self.above)
            self.send(lower, self.y_up[j], z - j, y, self.y_dev)
            self.send(lower, self.core_up[0][j], z - j, y, self.core_dev)
            self.got(upper, self.down[j], z + j, y)
            if j < last:
                self.send(jnp.logical_and(upper, z > 0), self.down[j + 1], z + j, y, self.below)
            self.send(upper, self.y_down[j], z + j, y, self.y_dev)
            self.send(upper, self.core_down[0][j], z + j, y, self.core_dev)
        self.pass_y(j - 1)

    def finish(self):
        z, last = self.z, self.c.E - 1
        for side in range(2):
            y = self.y if side == 0 else 1 - self.y
            if side:
                self.got(z >= 0, self.core_up[1][0], z, y, self.other_part)
            for j in range(1, self.c.E):
                self.got(z >= j, self.core_up[side][j], z - j, y, self.other_part)
                self.got(z + j <= last, self.core_down[side][j], z + j, y, self.other_part)

    def close(self):
        for condition, where in self.sent:
            pl.when(condition)(lambda: self.unit(*where).wait_send())


def front_kernel(c, *refs):
    refs = list(refs)
    take = lambda count: [refs.pop(0) for _ in range(count)]
    len_ref, tok_ref, route_ref, keep_ref, cot_ref = take(5)
    if c.gather:
        wqkv_ref, wout_ref, small_ref = take(3)
        w_hbm, vec_ref = take(2)
    else:
        w_ref, vec_ref = take(2)
    q_ref, kv_hbm, lse_ref, att_ref, hid_ref, mix_ref, meta_ref, router_ref = take(8)
    send_ref, gsend_ref, dyarr_ref = take(3)
    if c.gather:
        smalls, w_ref = take(2)
    kv_ref, dysend, norm_ref, lsem, ssem, rsem = take(6)
    links = Links(ssem, rsem)
    z, x, y = lax.axis_index("expert"), lax.axis_index("context"), lax.axis_index("dp")
    core = lax.rem(x, 2)
    shard = z * c.Y + y
    core_dev, far_dev, y_dev = (z, x ^ 1, y), (z, x ^ 2, y), (z, x, 1 - y)
    plane = [(lax.div(shard ^ k, c.Y), x, lax.rem(shard ^ k, c.Y)) for k in range(1, c.E * c.Y)]
    experts = [(z ^ k, x, y) for k in range(1, c.E)]
    greet([core_dev, far_dev] + (plane if c.gather else experts))
    ends = []

    def go(at, src, dst, device):
        copy = links.make(at, src, dst, device)
        copy.start()
        ends.append(copy)

    if c.gather:
        small_ids = [links.new() for _ in plane]
        smalls[shard] = small_ref[...]
        for at, device in zip(small_ids, plane):
            go(at, smalls.at[shard], smalls.at[shard], device)

        def rows_of(z_at, y_at):
            return pl.ds(pl.multiple_of((z_at * c.Y + y_at) * c.sh, 32), c.sh)

        own_rows = rows_of(z, y)
        for part in range(3):
            w_ref[part, own_rows, :] = wqkv_ref[:, part * c.D : (part + 1) * c.D]
        w_ref[3, own_rows, :] = wout_ref[...]

        above, below = (lax.rem(z + 1, c.E), x, y), (lax.rem(z + c.E - 1, c.E), x, y)
        stages = [Gather(c, links, w_ref, rows_of, z, y, *parts) for parts in (
            (1 + core, 2 - core), (3 * core, 3 - 3 * core))]
        for stage in stages:
            stage.route(above, below, y_dev, core_dev)
        stages[0].open()

    unit_rows = [None] * c.N
    choices = []
    for image in range(c.N):
        rows = slice(image * c.B, (image + 1) * c.B)
        live = jnp.where(row_of((c.B, 1)) < len_ref[image, x], 1.0, 0.0)
        kept = [to_column(keep_ref[image, j : j + 1, :].astype(F32)) * live for j in range(2)]
        first, second = [
            to_column(route_ref[image, j : j + 1, :].astype(F32)).astype(jnp.int32) for j in range(2)
        ]
        lane = lane_of((c.B, 128))
        named = jnp.where(lane == first, kept[0], 0.0) + jnp.where(
            lane == second, kept[1], 0.0
        )
        earlier = jnp.where(lane_of((c.B, c.B)) < row_of((c.B, c.B)), 1.0, 0.0).astype(BF16)
        rank = mm(earlier, named.astype(BF16))
        rank_first = jnp.sum(jnp.where(lane == first, rank, 0.0), axis=1, keepdims=True)
        rank_second = jnp.sum(jnp.where(lane == second, rank, 0.0), axis=1, keepdims=True)
        slot_first = first * c.cap + rank_first.astype(jnp.int32)
        slot_second = second * c.cap + rank_second.astype(jnp.int32)
        at = lane_of((c.B, c.E * c.cap))
        place = jnp.where(at == slot_first, kept[0], 0.0) + jnp.where(
            at == slot_second, kept[1], 0.0
        )
        place = place.astype(BF16)
        choices.append((first, second, kept, slot_first, slot_second, place))
        dysend[image] = mm(place, cot_ref[rows, :], TN).astype(BF16).reshape(c.E, c.cap, c.D)

    if c.gather:
        for at, device in zip(small_ids, plane):
            other = lax.div(shard, 1)
            links.make(at, smalls.at[other], smalls.at[other], device).wait_recv()
        wide = jnp.concatenate([smalls[k] for k in range(c.E * c.Y)], axis=1).astype(BF16)
        span = c.E * c.Y * 128
        src, dst = row_of((span, c.D)), lane_of((span, c.D))
        inside = lax.rem(src, 128)
        pick = jnp.logical_and(inside < c.sh, lax.div(src, 128) * c.sh + inside == dst)
        vec_ref[...] = mm(wide, jnp.where(pick, 1.0, 0.0).astype(BF16))
    vec = vec_ref[...]
    for image in range(c.N):
        rows = slice(image * c.B, (image + 1) * c.B)
        unit_one, _ = normalize(tok_ref[rows, :].astype(F32))
        norm_ref[rows, :] = (unit_one * vec[0:1] + vec[2:3]).astype(BF16)

    if c.gather:
        stages[0].step(1)
        stages[1].open()
        for j in range(2, c.E + 1):
            stages[0].step(j)
        stages[0].finish()

    normed = norm_ref[...]
    own_at = pl.ds(pl.multiple_of(x * c.B, 32), c.B)
    kv_ids = [[links.new() for _ in range(3)] for _ in range(c.N)]
    keys = mm(normed, w_ref[1]).astype(BF16)
    values = mm(normed, w_ref[2]).astype(BF16)
    for image in range(c.N):
        rows = slice(image * c.B, (image + 1) * c.B)
        kv_ref[image, own_at, 0 : c.D] = keys[rows]
        kv_ref[image, own_at, c.D : 2 * c.D] = values[rows]
        block = kv_ref.at[image, own_at, :]
        go(kv_ids[image][0], block, block, far_dev)
        go(kv_ids[image][1], block, block, core_dev)
    if c.gather:
        for j in range(1, c.E + 1):
            stages[1].step(j)
    dy_ids = [links.new() for _ in experts]
    for k, (at, device) in enumerate(zip(dy_ids, experts), 1):
        go(at, dysend.at[:, z ^ k], dyarr_ref.at[z], device)
    own_dy = pltpu.make_async_copy(dysend.at[:, z], dyarr_ref.at[z], lsem.at[0])
    own_dy.start()
    leaving = [own_dy]
    if c.gather:
        stages[1].finish()
        leaving.append(pltpu.make_async_copy(w_ref, w_hbm, lsem.at[1]))
        leaving[-1].start()
    q_ref[...] = mm(normed, w_ref[0]).astype(BF16)

    block_of = lambda image, who: kv_ref.at[image, pl.ds(pl.multiple_of(who * c.B, 32), c.B), :]

    for image in range(c.N):
        rows = pl.ds(image * c.B, c.B)
        far_block = block_of(image, x ^ 2)
        links.make(kv_ids[image][0], far_block, far_block, far_dev).wait_recv()
        go(kv_ids[image][2], far_block, far_block, core_dev)
        near_block = block_of(image, x ^ 1)
        links.make(kv_ids[image][1], near_block, near_block, core_dev).wait_recv()
        cross_block = block_of(image, x ^ 3)
        links.make(kv_ids[image][2], cross_block, cross_block, core_dev).wait_recv()
        leaving.append(pltpu.make_async_copy(kv_ref.at[image], kv_hbm.at[image], lsem.at[2 + image]))
        leaving[-1].start()
        bias = key_bias(c, len_ref, image)

        def pair_step(pair, carry):
            lanes = pl.ds(pl.multiple_of(pair * 128, 128), 128)
            value_lanes = pl.ds(pl.multiple_of(c.D + pair * 128, 128), 128)
            queries = two_heads(q_ref[rows, lanes]) * jnp.asarray(c.scale, BF16)
            scores = mm(kv_ref[image, :, lanes], queries, NT) + bias
            top = jnp.max(scores, axis=0, keepdims=True)
            exponent = jnp.exp(scores - top)
            total = jnp.sum(exponent, axis=0, keepdims=True)
            probs = (exponent * (1.0 / total)).astype(BF16)
            lse_ref[image, pair] = jnp.broadcast_to(top + jnp.log(total), (8, 2 * c.B))
            mixed_values = mm(kv_ref[image, :, value_lanes].T, probs)
            att_ref[rows, lanes] = one_pair(mixed_values.T).astype(BF16)
            return carry

        lax.fori_loop(0, c.D // 128, pair_step, 0)

    branch = mm(att_ref[...], w_ref[3])
    hidden = tok_ref[...].astype(F32) + branch
    hid_ref[...] = hidden
    unit_two, _ = normalize(hidden)
    mixed = (unit_two * vec[1:2] + vec[3:4]).astype(BF16)
    mix_ref[...] = mixed
    pad = jnp.zeros((128 - c.r8, c.D), BF16)
    logits = mm(mixed, jnp.concatenate([vec.astype(BF16), pad], axis=0), NT)
    lane = lane_of((c.N * c.B, 128))
    valid = jnp.logical_and(lane >= LOGIT_LANE, lane < LOGIT_LANE + c.E)
    logits = jnp.where(valid, logits, -1e30)
    weight = jnp.exp(logits - jnp.max(logits, axis=1, keepdims=True))
    router = weight / jnp.sum(weight, axis=1, keepdims=True)
    router_ref[...] = router
    gsend_ref[...] = jnp.zeros_like(gsend_ref)
    lane = lane_of((c.B, 128))
    for image in range(c.N):
        rows = slice(image * c.B, (image + 1) * c.B)
        first, second, kept, slot_first, slot_second, place = choices[image]
        here = router[rows]
        gate_first = kept[0] * jnp.sum(
            jnp.where(lane == LOGIT_LANE + first, here, 0.0), axis=1, keepdims=True
        )
        gate_second = kept[1] * jnp.sum(
            jnp.where(lane == LOGIT_LANE + second, here, 0.0), axis=1, keepdims=True
        )
        send_ref[image] = mm(place, mixed[rows], TN).astype(BF16).reshape(c.E, c.cap, c.D)
        at = lane_of((c.B, c.cap))
        for expert in range(c.E):
            gates = jnp.where(at == slot_first - expert * c.cap, gate_first, 0.0)
            gates = gates + jnp.where(at == slot_second - expert * c.cap, gate_second, 0.0)
            gsend_ref[expert, image : image + 1, :] = jnp.sum(gates, axis=0, keepdims=True)
        columns = (
            slot_first.astype(F32),
            slot_second.astype(F32),
            kept[0],
            kept[1],
            gate_first,
            gate_second,
            first.astype(F32),
            second.astype(F32),
        )
        meta = jnp.zeros((c.B, 128), F32)
        for index, column in enumerate(columns):
            meta = jnp.where(lane == index, column, meta)
        meta_ref[rows, :] = meta

    for k, (at, device) in enumerate(zip(dy_ids, experts), 1):
        links.make(at, dyarr_ref.at[z ^ k], dyarr_ref.at[z ^ k], device).wait_recv()
    for copy in leaving:
        copy.wait()
    for copy in ends:
        copy.wait_send()
    if c.gather:
        for stage in stages:
            stage.close()


def spec(space):
    return pl.BlockSpec(memory_space=space)


def run_front(c, lengths, tok, route, keep, cot, weights):
    shape = jax.ShapeDtypeStruct
    made = [shape((4, c.D, c.D), BF16), shape((c.r8, c.D), F32)] if c.gather else []
    made += [
        shape((c.T, c.D), BF16),
        shape((c.N, c.S, 2 * c.D), BF16),
        shape((c.N, c.D // 128, 8, 2 * c.B), F32),
        shape((c.T, c.D), BF16),
        shape((c.T, c.D), F32),
        shape((c.T, c.D), BF16),
        shape((c.T, 128), F32),
        shape((c.T, 128), F32),
        shape((c.N, c.E, c.cap, c.D), BF16),
        shape((c.E, 8, c.cap), F32),
        shape((c.E, c.N, c.cap, c.D), BF16),
    ]
    count = 112 if c.gather else 2 * c.E + 16
    places = [spec(pltpu.VMEM)] * len(made)
    places[-1] = places[-10] = spec(pl.ANY)
    gather_scratch = []
    if c.gather:
        places[0] = spec(pl.ANY)
        gather_scratch = [
            pltpu.VMEM((c.E * c.Y, c.r8, 128), F32),
            pltpu.VMEM((4, c.D, c.D), BF16),
        ]
    out = pl.pallas_call(
        functools.partial(front_kernel, c),
        out_shape=made,
        in_specs=[spec(pltpu.SMEM)] + [spec(pltpu.VMEM)] * (4 + len(weights)),
        out_specs=places,
        scratch_shapes=gather_scratch
        + [
            pltpu.VMEM((c.N, c.S, 2 * c.D), BF16),
            pltpu.VMEM((c.N, c.E, c.cap, c.D), BF16),
            pltpu.VMEM((c.T, c.D), BF16),
            pltpu.SemaphoreType.DMA((2 + c.N,)),
            pltpu.SemaphoreType.DMA((count,)),
            pltpu.SemaphoreType.DMA((count,)),
        ],
        compiler_params=pltpu.CompilerParams(
            collective_id=0, has_side_effects=True, vmem_limit_bytes=VMEM_LIMIT
        ),
        name="front",
    )(lengths, tok, route, keep, cot, *weights)
    return out if c.gather else list(weights) + list(out)


def gelu_both(pre):
    inner = 0.7978845608028654 * (pre + 0.044715 * pre * pre * pre)
    bend = jnp.tanh(inner)
    half = 0.5 * (1.0 + bend)
    slope = 0.7978845608028654 * (1.0 + 0.134145 * pre * pre)
    return pre * half, half + 0.5 * pre * (1.0 - bend * bend) * slope


def expert_kernel(
    c,
    send_ref,
    gsend_ref,
    dyarr_ref,
    win_hbm,
    wdown_hbm,
    xback_ref,
    gback_ref,
    yloc_ref,
    grad_hbm,
    gnext_hbm,
    win,
    wdown,
    arr,
    garr,
    act_all,
    dpre_all,
    dout_all,
    dxs,
    dgs,
    turned,
    gsend,
    grecv,
    gown,
    wsem,
    ssem,
    rsem,
):
    links = Links(ssem, rsem)
    z, x, y = lax.axis_index("expert"), lax.axis_index("context"), lax.axis_index("dp")
    experts = [(z ^ k, x, y) for k in range(1, c.E)]
    load_in = pltpu.make_async_copy(win_hbm, win, wsem.at[0])
    load_down = pltpu.make_async_copy(wdown_hbm, wdown, wsem.at[1])
    load_in.start()
    load_down.start()
    greet(experts + [(z, x ^ 1, y), (z, x ^ 2, y), (z, x, 1 - y)])
    ids = [[links.new() for _ in range(4)] for _ in range(c.E)]
    ends = []

    def go(at, src, dst, device):
        copy = links.make(at, src, dst, device)
        copy.start()
        ends.append(copy)

    group = c.E // c.chunks
    height = group * c.N * c.cap

    def dispatch(g):
        started = len(ends)
        for k in range(max(1, g * group), (g + 1) * group):
            go(ids[k][1], gsend_ref.at[z ^ k], garr.at[z], experts[k - 1])
            go(ids[k][0], send_ref.at[:, z ^ k], arr.at[z], experts[k - 1])
        return ends[started:]

    dispatch(0)
    early = dispatch(c.chunks - 2)
    for g in range(1, c.chunks - 2):
        dispatch(g)
    for image in range(c.N):
        arr[z, image] = send_ref[image, z]
    garr[z] = gsend_ref[z]
    load_in.wait()
    load_down.wait()
    dgs[...] = jnp.zeros_like(dgs)
    for g in range(c.chunks):
        if g == 1:
            for copy in early:
                copy.wait_send()
            ends[:] = [copy for copy in ends if all(copy is not other for other in early)]
            dispatch(c.chunks - 1)
        slab = lax.div(z, group) ^ g
        for k in range(g * group, (g + 1) * group):
            if k:
                there = z ^ k
                links.make(ids[k][0], arr.at[there], arr.at[there], experts[k - 1]).wait_recv()
                links.make(ids[k][1], garr.at[there], garr.at[there], experts[k - 1]).wait_recv()
        start = pl.multiple_of(slab * height, 32)
        rows = pl.ds(start, height)
        for member in range(group):
            source = slab * group + member
            for image in range(c.N):
                gates = to_column(garr[source, image : image + 1, :])
                offset = (member * c.N + image) * c.cap
                part = pl.ds(pl.multiple_of(start + offset, 16), c.cap)
                dout_all[part, :] = (gates * dyarr_ref[source, image].astype(F32)).astype(BF16)
        inputs = arr[pl.ds(slab * group, group)].reshape(height, c.D)
        douts = dout_all[rows, :]

        def ff_step(step, carry):
            lanes = pl.ds(pl.multiple_of(step * c.FB, 128), c.FB)
            pre = mm(inputs, win[:, lanes])
            act, slope = gelu_both(pre)
            act_all[rows, lanes] = act.astype(BF16)
            dact = mm(douts, wdown[lanes, :], NT)
            dpre_all[rows, lanes] = (dact * slope).astype(BF16)
            return carry

        lax.fori_loop(0, c.FF // c.FB, ff_step, 0)
        dx = mm(dpre_all[rows, :], win[...], NT).astype(BF16)
        dxs[pl.ds(slab * group, group)] = dx.reshape(group, c.N, c.cap, c.D)
        made = mm(act_all[rows, :], wdown[...]).astype(BF16)
        yloc_ref[pl.ds(slab * group, group)] = made.reshape(group, c.N, c.cap, c.D)
        for member in range(group):
            source = slab * group + member
            for image in range(c.N):
                offset = (member * c.N + image) * c.cap
                dots = made[offset : offset + c.cap].astype(F32) * dyarr_ref[source, image].astype(
                    F32
                )
                dgs[source, image : image + 1, :] = to_row(jnp.sum(dots, axis=1, keepdims=True))
        for k in range(g * group, (g + 1) * group):
            if k:
                there = z ^ k
                go(ids[k][2], dxs.at[there], xback_ref.at[:, z], experts[k - 1])
                go(ids[k][3], dgs.at[there], gback_ref.at[z], experts[k - 1])
    for image in range(c.N):
        xback_ref[image, z] = dxs[z, image]
    gback_ref[z] = dgs[z]

    total = c.E * c.N * c.cap
    turned[0] = arr[...].reshape(total, c.D).T
    turned[1] = dout_all[...].T

    core = lax.rem(x, 2)
    core_dev, far_dev, y_dev = (z, x ^ 1, y), (z, x ^ 2, y), (z, x, 1 - y)
    half = c.FF // 4
    grad_ids = [[links.new() for _ in range(2)] for _ in range(2)]
    sources = (dpre_all, act_all)

    def blocks(which, owner, into):
        def block_step(part, carry):
            lanes = pl.ds(pl.multiple_of((2 * part + owner) * half, 128), half)
            into[part, which] = mm(turned[which], sources[which][:, lanes]).astype(BF16)
            return carry

        lax.fori_loop(0, 2, block_step, 0)

    piece = half // 2
    side = lax.div(x, 2)
    other_piece = pl.ds(pl.multiple_of((1 - y) * piece, 128), piece)
    next_ids = [links.new() for _ in range(2)]
    leaving = []
    for which in range(2):
        blocks(which, 1 - core, gsend)
        for part in range(2):
            go(grad_ids[which][part], gsend.at[part, which], grecv.at[part, which], core_dev)
        blocks(which, core, gown)
        for part in range(2):
            there = grecv.at[part, which]
            links.make(grad_ids[which][part], there, there, core_dev).wait_recv()
            gown[part, which] = (
                gown[part, which].astype(F32) + grecv[part, which].astype(F32)
            ).astype(BF16)
        first = gown.at[1 - side, which, :, other_piece]
        go(next_ids[which], first, gnext_hbm.at[which], y_dev if which == 0 else far_dev)
        for part in range(2):
            leaving.append(
                pltpu.make_async_copy(
                    gown.at[part, which], grad_hbm.at[part, which], wsem.at[2 + 2 * which + part]
                )
            )
            leaving[-1].start()
    for which in range(2):
        there = gnext_hbm.at[which]
        links.make(next_ids[which], there, there, core_dev).wait_recv()
    for copy in leaving:
        copy.wait()
    for k in range(1, c.E):
        there = z ^ k
        links.make(ids[k][2], xback_ref.at[:, there], xback_ref.at[:, there], experts[k - 1]).wait_recv()
        links.make(ids[k][3], gback_ref.at[there], gback_ref.at[there], experts[k - 1]).wait_recv()
    for copy in ends:
        copy.wait_send()


def run_experts(c, send, gsend, dyarr, w_in, w_down):
    shape = jax.ShapeDtypeStruct
    total = c.E * c.N * c.cap
    count = 4 * c.E + 6
    return pl.pallas_call(
        functools.partial(expert_kernel, c),
        out_shape=[
            shape((c.N, c.E, c.cap, c.D), BF16),
            shape((c.E, 8, c.cap), F32),
            shape((c.E, c.N, c.cap, c.D), BF16),
            shape((2, 2, c.D, c.FF // 4), BF16),
            shape((2, c.D, c.FF // 8), BF16),
        ],
        in_specs=[spec(pltpu.VMEM)] * 3 + [spec(pl.ANY)] * 2,
        out_specs=[spec(pltpu.VMEM)] * 3 + [spec(pl.ANY)] * 2,
        scratch_shapes=[
            pltpu.VMEM((c.D, c.FF), BF16),
            pltpu.VMEM((c.FF, c.D), BF16),
            pltpu.VMEM((c.E, c.N, c.cap, c.D), BF16),
            pltpu.VMEM((c.E, 8, c.cap), F32),
            pltpu.VMEM((total, c.FF), BF16),
            pltpu.VMEM((total, c.FF), BF16),
            pltpu.VMEM((total, c.D), BF16),
            pltpu.VMEM((c.E, c.N, c.cap, c.D), BF16),
            pltpu.VMEM((c.E, 8, c.cap), F32),
            pltpu.VMEM((2, c.D, total), BF16),
            pltpu.VMEM((2, 2, c.D, c.FF // 4), BF16),
            pltpu.VMEM((2, 2, c.D, c.FF // 4), BF16),
            pltpu.VMEM((2, 2, c.D, c.FF // 4), BF16),
            pltpu.SemaphoreType.DMA((6,)),
            pltpu.SemaphoreType.DMA((count,)),
            pltpu.SemaphoreType.DMA((count,)),
        ],
        compiler_params=pltpu.CompilerParams(
            collective_id=1, has_side_effects=True, vmem_limit_bytes=VMEM_LIMIT
        ),
        name="experts",
    )(send, gsend, dyarr, w_in, w_down)


def in_parts(values, count):
    parts = []
    for _ in range(count):
        parts.append(values.astype(BF16))
        values = values - parts[-1].astype(F32)
    return parts


def back_kernel(c, *refs):
    refs = list(refs)
    take = lambda count: [refs.pop(0) for _ in range(count)]
    len_ref, tok_ref, cot_ref, vec_ref, q_ref, lse_ref, att_ref, hid_ref, mix_ref = take(9)
    meta_ref, router_ref, xback_ref, gback_ref = take(4)
    w_hbm, kv_hbm, yloc_hbm, grad_hbm, gnext_hbm = take(5)
    gtok_hbm, made, gy, gx = take(4)
    if c.gather:
        whole, gsmall_ref = take(2)
    else:
        dd, gsmall_ref = take(2)
    w_ref, kv_ref, gtok_ref, gpart, gnext = take(5)
    dkv, kvcore, kvfar, dproj, datt, dhid, norm_t, router_sum = take(8)
    if c.gather:
        dd, dcore, done_x, done_y, done_z, small, small_in = take(7)
    lsem, ssem, rsem = take(3)
    links = Links(ssem, rsem)
    z, x, y = lax.axis_index("expert"), lax.axis_index("context"), lax.axis_index("dp")
    core, side = lax.rem(x, 2), lax.div(x, 2)
    core_dev, far_dev, y_dev = (z, x ^ 1, y), (z, x ^ 2, y), (z, x, 1 - y)
    experts = [(z ^ k, x, y) for k in range(1, c.E)]
    ends = []

    def go(at, src, dst, device):
        copy = links.make(at, src, dst, device)
        copy.start()
        ends.append(copy)

    def got(at, dst, device):
        links.make(at, dst, dst, device).wait_recv()

    half = c.FF // 4
    piece = half // 2
    loads = [
        pltpu.make_async_copy(w_hbm, w_ref, lsem.at[0]),
        pltpu.make_async_copy(kv_hbm, kv_ref, lsem.at[1]),
    ]
    own_piece = pl.ds(pl.multiple_of(y * piece, 128), piece)
    other_piece = pl.ds(pl.multiple_of((1 - y) * piece, 128), piece)
    parts = (grad_hbm.at[1 - side, 0, :, own_piece], grad_hbm.at[side, 1, :, other_piece])
    for which in range(2):
        loads.append(pltpu.make_async_copy(parts[which], gpart.at[which], lsem.at[2 + which]))
        loads.append(
            pltpu.make_async_copy(gnext_hbm.at[which], gnext.at[which], lsem.at[6 + which])
        )
    own_made = pltpu.make_async_copy(yloc_hbm.at[z], made.at[:, z], lsem.at[4])
    loads.append(own_made)
    for load in loads:
        load.start()
    greet([core_dev, far_dev, y_dev] + experts)

    made_ids = [links.new() for _ in experts]
    for k, (at, device) in enumerate(zip(made_ids, experts), 1):
        go(at, yloc_hbm.at[z ^ k], made.at[:, z], device)
    gy_ids = [links.new() for _ in range(2)]
    gx_ids = [links.new() for _ in range(2)]
    go(gy_ids[0], grad_hbm.at[side, 0, :, other_piece], gy.at[0], y_dev)
    go(gx_ids[1], grad_hbm.at[1 - side, 1, :, own_piece], gx.at[1], far_dev)
    for which in range(2):
        loads[2 + 2 * which].wait()
        loads[3 + 2 * which].wait()
        gpart[which] = (gpart[which].astype(F32) + gnext[which].astype(F32)).astype(BF16)
        if which == 0:
            go(gx_ids[0], gpart.at[0], gx.at[0], far_dev)
        else:
            go(gy_ids[1], gpart.at[1], gy.at[1], y_dev)

    def grads_end():
        for which in range(2):
            got(gy_ids[which], gy.at[which], y_dev)
            got(gx_ids[which], gx.at[which], far_dev)

    if c.gather:
        n_dense = 4
        core_cols = c.D // 2
        keep_cols = pl.ds(pl.multiple_of(core * core_cols, 128), core_cols)
        give_cols = pl.ds(pl.multiple_of((1 - core) * core_cols, 128), core_cols)
        ids_core = [links.new() for _ in range(n_dense)]
        ids_x = [links.new() for _ in range(n_dense)]
        ids_y = [links.new() for _ in range(n_dense)]
        ids_z = [[links.new() for _ in experts] for _ in range(n_dense)]
        ids_own = [links.new() for _ in range(n_dense)]

        def dense_start(m, value):
            dd[m] = value.astype(BF16).reshape(c.E, c.Y, c.sh, c.D)
            go(ids_core[m], dd.at[m, :, :, :, give_cols], dcore.at[m], core_dev)

        def dense_y(m):
            got(ids_core[m], dcore.at[m], core_dev)
            dd[m, :, :, :, keep_cols] = (
                dd[m, :, :, :, keep_cols].astype(F32) + dcore[m].astype(F32)
            ).astype(BF16)
            go(ids_y[m], dd.at[m, :, 1 - y, :, keep_cols], done_y.at[m], y_dev)

        def dense_z(m):
            got(ids_y[m], done_y.at[m], y_dev)
            dd[m, :, y, :, keep_cols] = (
                dd[m, :, y, :, keep_cols].astype(F32) + done_y[m].astype(F32)
            ).astype(BF16)
            for k, device in enumerate(experts, 1):
                go(
                    ids_z[m][k - 1],
                    dd.at[m, z ^ k, y, :, keep_cols],
                    done_z.at[m, z],
                    device,
                )

        def dense_x(m):
            total = dd[m, z, y, :, keep_cols].astype(F32)
            for k, device in enumerate(experts, 1):
                got(ids_z[m][k - 1], done_z.at[m, z ^ k], device)
                total = total + done_z[m, z ^ k].astype(F32)
            done_x[m, 0] = total.astype(BF16)
            go(ids_x[m], done_x.at[m, 0], done_x.at[m, 1], far_dev)

        def dense_share(m):
            got(ids_x[m], done_x.at[m, 1], far_dev)
            whole[m, core] = done_x[m, 0].astype(F32) + done_x[m, 1].astype(F32)
            go(ids_own[m], whole.at[m, core], whole.at[m, core], core_dev)

        def dense_end(m):
            there = whole.at[m, 1 - core]
            got(ids_own[m], there, core_dev)

    else:

        def dense_start(m, value):
            dd[m] = value.astype(BF16)

    vec = vec_ref[...]
    lane = lane_of((c.B, 128))
    d_mixed, dy_rows = [], []
    d_logits = []
    for image in range(c.N):
        rows = slice(image * c.B, (image + 1) * c.B)
        meta = meta_ref[rows, :]
        slots = [meta[:, j : j + 1].astype(jnp.int32) for j in range(2)]
        kept = [meta[:, 2 + j : 3 + j] for j in range(2)]
        names = [meta[:, 6 + j : 7 + j].astype(jnp.int32) for j in range(2)]
        at = lane_of((c.B, c.E * c.cap))
        place = jnp.where(at == slots[0], kept[0], 0.0) + jnp.where(at == slots[1], kept[1], 0.0)
        copies = xback_ref[image].reshape(c.E * c.cap, c.D)
        d_mixed.append(mm(place.astype(BF16), copies))
        d_router = jnp.zeros((c.B, 128), F32)
        at = lane_of((c.B, c.cap))
        for j in range(2):
            d_gate = jnp.zeros((c.B, c.cap), F32)
            for expert in range(c.E):
                row = gback_ref[expert, image : image + 1, :]
                d_gate = d_gate + jnp.where(at == slots[j] - expert * c.cap, row, 0.0)
            d_gate = jnp.sum(d_gate, axis=1, keepdims=True) * kept[j]
            d_router = d_router + jnp.where(lane == LOGIT_LANE + names[j], d_gate, 0.0)
        router = router_ref[rows, :]
        dot = jnp.sum(router * d_router, axis=1, keepdims=True)
        d_logits.append(router * (d_router - dot))
        live = jnp.where(row_of((c.B, 1)) < len_ref[image, x], 1.0, 0.0)
        dy_rows.append(cot_ref[rows, :].astype(F32) * live)
    d_mixed = jnp.concatenate(d_mixed, axis=0)
    d_logits = jnp.concatenate(d_logits, axis=0)
    dy_rows = jnp.concatenate(dy_rows, axis=0)
    logit_rows = jnp.concatenate([vec, jnp.zeros((128 - c.r8, c.D), F32)], axis=0)
    lane_here = row_of((128, c.D))
    is_router = jnp.logical_and(lane_here >= LOGIT_LANE, lane_here < LOGIT_LANE + c.E)
    w_router = jnp.where(is_router, logit_rows, 0.0)
    high, low = in_parts(d_logits, 2)
    w_router = w_router.astype(BF16)
    d_mixed = d_mixed + mm(high, w_router) + mm(low, w_router)
    router_sum[...] = mm(high, mix_ref[...], TN) + mm(low, mix_ref[...], TN)
    unit_two, inverse_two = normalize(hid_ref[...])
    gains_two = jnp.sum(d_mixed * unit_two, axis=0, keepdims=True)
    biases_two = jnp.sum(d_mixed, axis=0, keepdims=True)
    d_hidden = dy_rows + normalize_back(d_mixed, unit_two, inverse_two, vec[1:2])
    dhid[...] = d_hidden
    d_branch = d_hidden.astype(BF16)
    dense_start(3, mm(att_ref[...], d_branch, TN))
    loads[0].wait()
    datt[...] = mm(d_branch, w_ref[3], NT).astype(BF16)
    unit_one, inverse_one = normalize(tok_ref[...].astype(F32))
    norm_t[...] = (unit_one * vec[0:1] + vec[2:3]).astype(BF16).T
    loads[1].wait()

    kvcore_ids = [[links.new() for _ in range(2)] for _ in range(c.N)]
    kvfar_ids = [links.new() for _ in range(c.N)]

    def block_rows(who):
        return pl.ds(pl.multiple_of(who * c.B, 32), c.B)

    def attend_back(image, first_pair, last_pair):
        rows = pl.ds(image * c.B, c.B)
        bias = key_bias(c, len_ref, image)

        def pair_step(pair, carry):
            lanes = pl.ds(pl.multiple_of(pair * 128, 128), 128)
            value_lanes = pl.ds(pl.multiple_of(c.D + pair * 128, 128), 128)
            scale = jnp.asarray(c.scale, BF16)
            queries = two_heads(q_ref[rows, lanes]) * scale
            grads = two_heads(datt[rows, lanes])
            keys = kv_ref[image, :, lanes]
            probs = jnp.exp(mm(keys, queries, NT) + bias - lse_ref[image, pair][0:1])
            d_probs = mm(kv_ref[image, :, value_lanes], grads, NT)
            dot = jnp.sum(probs * d_probs, axis=0, keepdims=True)
            d_scores = (probs * (d_probs - dot)).astype(BF16)
            dkv[image, :, value_lanes] = mm(probs.astype(BF16), grads).astype(BF16)
            dkv[image, :, lanes] = mm(d_scores, queries).astype(BF16)
            d_queries = mm(keys.T, d_scores).T
            dproj[rows, lanes] = (one_pair(d_queries) * c.scale).astype(BF16)
            return carry

        lax.fori_loop(first_pair, last_pair, pair_step, 0)

    def kv_to_core(image):
        for s in range(2):
            block = dkv.at[image, block_rows(2 * s + 1 - core), :]
            go(kvcore_ids[image][s], block, kvcore.at[image, s], core_dev)

    def kv_to_far(image):
        for s in range(2):
            got(kvcore_ids[image][s], kvcore.at[image, s], core_dev)
        rows = block_rows(2 * (1 - side) + core)
        dkv[image, rows, :] = (
            dkv[image, rows, :].astype(F32) + kvcore[image, 1 - side].astype(F32)
        ).astype(BF16)
        go(kvfar_ids[image], dkv.at[image, rows, :], kvfar.at[image], far_dev)

    def kv_end(image):
        got(kvfar_ids[image], kvfar.at[image], far_dev)
        total = dkv[image, block_rows(2 * side + core), :].astype(F32)
        total = total + kvcore[image, side].astype(F32) + kvfar[image].astype(F32)
        rows = pl.ds(image * c.B, c.B)
        dproj[rows, c.D : 3 * c.D] = total.astype(BF16)

    pairs = c.D // 128
    attend_back(0, 0, pairs)
    kv_to_core(0)
    if c.gather:
        dense_y(3)
    attend_back(1, 0, pairs // 2)
    kv_to_far(0)
    attend_back(1, pairs // 2, pairs)
    kv_to_core(1)
    dense_start(0, mm(norm_t[...], dproj[:, 0 : c.D]))
    kv_to_far(1)
    if c.gather:
        dense_z(3)
    kv_end(0)
    if c.gather:
        dense_y(0)
        dense_x(3)
    kv_end(1)
    dense_start(1, mm(norm_t[...], dproj[:, c.D : 2 * c.D]))
    dense_start(2, mm(norm_t[...], dproj[:, 2 * c.D : 3 * c.D]))
    if c.gather:
        dense_y(1)
        dense_y(2)
        dense_z(0)
        dense_share(3)
    d_normed = mm(dproj[:, 0 : c.D], w_ref[0], NT)
    d_normed = d_normed + mm(dproj[:, c.D : 2 * c.D], w_ref[1], NT)
    d_normed = d_normed + mm(dproj[:, 2 * c.D : 3 * c.D], w_ref[2], NT)
    unit_one, inverse_one = normalize(tok_ref[...].astype(F32))
    gains_one = jnp.sum(d_normed * unit_one, axis=0, keepdims=True)
    biases_one = jnp.sum(d_normed, axis=0, keepdims=True)
    small_here = jnp.concatenate([gains_one, gains_two, biases_one, biases_two], axis=0)
    small_here = jnp.concatenate(
        [small_here, router_sum[LOGIT_LANE : LOGIT_LANE + c.r8 - 4]], axis=0
    )
    if c.gather:
        small[0] = small_here
        small_ids = [links.new() for _ in range(3)]
        small_z = [links.new() for _ in experts]
        go(small_ids[0], small.at[0], small_in.at[0], core_dev)
    gtok_ref[...] = dhid[...] + normalize_back(d_normed, unit_one, inverse_one, vec[0:1])
    leave = pltpu.make_async_copy(gtok_ref, gtok_hbm, lsem.at[5])
    leave.start()
    if c.gather:

        def small_step(step, device):
            source = core_dev if step == 0 else far_dev if step == 1 else y_dev
            got(small_ids[step], small_in.at[step], source)
            small[step + 1] = small[step] + small_in[step]
            if step < 2:
                go(small_ids[step + 1], small.at[step + 1], small_in.at[step + 1], device)

        small_step(0, far_dev)
        dense_end(3)
        dense_x(0)
        small_step(1, y_dev)
        dense_z(1)
        dense_z(2)
        small_step(2, None)
        for k, (at, device) in enumerate(zip(small_z, experts), 1):
            go(at, small.at[3], small_in.at[3 + z], device)
        dense_share(0)
        dense_x(1)
        dense_x(2)
        total = small[3]
        for k, (at, device) in enumerate(zip(small_z, experts), 1):
            got(at, small_in.at[3 + (z ^ k)], device)
            total = total + small_in[3 + (z ^ k)]
        gsmall_ref[...] = total
        dense_end(0)
        dense_share(1)
        dense_share(2)
        dense_end(1)
        dense_end(2)
    else:
        gsmall_ref[...] = small_here
    for k, (at, device) in enumerate(zip(made_ids, experts), 1):
        got(at, made.at[:, z ^ k], device)
    grads_end()
    leave.wait()
    own_made.wait()
    for copy in ends:
        copy.wait_send()


def last_kernel(c, *refs):
    refs = list(refs)
    take = lambda count: [refs.pop(0) for _ in range(count)]
    len_ref, hid_ref, meta_ref, gtok_in, made_in, grad_in, gy_in, gx_in = take(8)
    if c.gather:
        whole_ref, small_ref = take(2)
    out_ref, gtok_out, gin_ref, gdown_ref = take(4)
    if c.gather:
        gqkv_ref, gout_ref, gains_ref, biases_ref, grouter_ref = take(5)
    made, gown, gy, gx, sem = take(5)
    z, x, y = lax.axis_index("expert"), lax.axis_index("context"), lax.axis_index("dp")
    side = lax.div(x, 2)
    piece = c.FF // 8
    own_piece = pl.ds(pl.multiple_of(y * piece, 128), piece)
    loads = []
    for which in range(2):
        for index, (src, dst) in enumerate((
            (grad_in.at[side, which, :, own_piece], gown.at[which]),
            (gy_in.at[which], gy.at[which]),
            (gx_in.at[which], gx.at[which]),
        )):
            loads.append(pltpu.make_async_copy(src, dst, sem.at[3 * which + index]))
    loads.append(pltpu.make_async_copy(made_in, made, sem.at[6]))
    for load in loads:
        load.start()
    gtok_out[...] = gtok_in[...]
    if c.gather:
        core_cols = c.D // 2
        for m in range(4):
            for k in range(2):
                if m == 3:
                    gout_ref[:, k * core_cols : (k + 1) * core_cols] = whole_ref[m, k]
                else:
                    start = m * c.D + k * core_cols
                    gqkv_ref[:, start : start + core_cols] = whole_ref[m, k]
        src, dst = row_of((c.D, 128)), lane_of((c.D, 128))
        pick = jnp.logical_and(dst < c.sh, src == dst + (z * c.Y + y) * c.sh)
        pick = jnp.where(pick, 1.0, 0.0).astype(BF16)
        small = sum(mm(part, pick) for part in in_parts(small_ref[...], 3))
        gains_ref[...] = small[0:2, 0 : c.sh]
        biases_ref[...] = small[2:4, 0 : c.sh]
        grouter_ref[...] = small[LOGIT_LANE : LOGIT_LANE + c.E, 0 : c.sh]
    for which in range(2):
        for load in loads[3 * which : 3 * which + 3]:
            load.wait()
        total = gown[which].astype(F32) + gy[which].astype(F32) + gx[which].astype(F32)
        if which == 0:
            gin_ref[...] = total
        else:
            gdown_ref[...] = total.T
    loads[6].wait()
    for image in range(c.N):
        rows = slice(image * c.B, (image + 1) * c.B)
        meta = meta_ref[rows, :]
        slots = [meta[:, j : j + 1].astype(jnp.int32) for j in range(2)]
        at = lane_of((c.B, c.E * c.cap))
        gates = jnp.where(at == slots[0], meta[:, 4:5], 0.0)
        gates = gates + jnp.where(at == slots[1], meta[:, 5:6], 0.0)
        high, low = in_parts(gates, 2)
        rows_made = made[image].reshape(c.E * c.cap, c.D)
        mixture = mm(high, rows_made) + mm(low, rows_made)
        live = jnp.where(row_of((c.B, 1)) < len_ref[image, x], 1.0, 0.0)
        out_ref[rows, :] = (live * (hid_ref[rows, :] + mixture)).astype(BF16)


def run_back(c, tok, cot, lengths, weights, vec, q, kv, lse, att, hid, mix, meta, router, xback, gback, yloc, grads, gnext):
    shape = jax.ShapeDtypeStruct
    piece = c.FF // 8
    made = [
        shape((c.T, c.D), F32),
        shape((c.N, c.E, c.cap, c.D), BF16),
        shape((2, c.D, piece), BF16),
        shape((2, c.D, piece), BF16),
    ]
    dense_scratch = []
    if c.gather:
        half_cols = c.D // 2
        made += [shape((4, 2, c.sh, half_cols), F32), shape((c.r8, c.D), F32)]
        dense_scratch = [
            pltpu.VMEM((4, c.E, c.Y, c.sh, c.D), BF16),
            pltpu.VMEM((4, c.E, c.Y, c.sh, half_cols), BF16),
            pltpu.VMEM((4, 2, c.sh, half_cols), BF16),
            pltpu.VMEM((4, c.E, c.sh, half_cols), BF16),
            pltpu.VMEM((4, c.E, c.sh, half_cols), BF16),
            pltpu.VMEM((4, c.r8, c.D), F32),
            pltpu.VMEM((3 + c.E, c.r8, c.D), F32),
        ]
    else:
        made += [shape((4, c.D, c.D), BF16), shape((c.r8, c.D), F32)]
    count = 5 * c.E + 64
    results = pl.pallas_call(
        functools.partial(back_kernel, c),
        out_shape=made,
        in_specs=[spec(pltpu.SMEM)] + [spec(pltpu.VMEM)] * 12 + [spec(pl.ANY)] * 5,
        out_specs=[spec(pl.ANY)] * 4 + [spec(pltpu.VMEM)] * 2,
        scratch_shapes=[
            pltpu.VMEM((4, c.D, c.D), BF16),
            pltpu.VMEM((c.N, c.S, 2 * c.D), BF16),
            pltpu.VMEM((c.T, c.D), F32),
            pltpu.VMEM((2, c.D, piece), BF16),
            pltpu.VMEM((2, c.D, piece), BF16),
            pltpu.VMEM((c.N, c.S, 2 * c.D), BF16),
            pltpu.VMEM((c.N, 2, c.B, 2 * c.D), BF16),
            pltpu.VMEM((c.N, c.B, 2 * c.D), BF16),
            pltpu.VMEM((c.T, 3 * c.D), BF16),
            pltpu.VMEM((c.T, c.D), BF16),
            pltpu.VMEM((c.T, c.D), F32),
            pltpu.VMEM((c.D, c.T), BF16),
            pltpu.VMEM((128, c.D), F32),
            *dense_scratch,
            pltpu.SemaphoreType.DMA((8,)),
            pltpu.SemaphoreType.DMA((count,)),
            pltpu.SemaphoreType.DMA((count,)),
        ],
        compiler_params=pltpu.CompilerParams(
            collective_id=2, has_side_effects=True, vmem_limit_bytes=VMEM_LIMIT
        ),
        name="back",
    )(lengths, tok, cot, vec, q, lse, att, hid, mix, meta, router, xback, gback, weights, kv, yloc, grads, gnext)
    g_tok, made_home, gy, gx, dense, small = results
    last = [shape((c.T, c.D), BF16), shape((c.T, c.D), F32)]
    last += [shape((c.D, piece), F32), shape((piece, c.D), F32)]
    if c.gather:
        last += [shape((c.sh, 3 * c.D), F32), shape((c.sh, c.D), F32)]
        last += [shape((2, c.sh), F32), shape((2, c.sh), F32), shape((c.E, c.sh), F32)]
    more = (dense, small) if c.gather else ()
    results = pl.pallas_call(
        functools.partial(last_kernel, c),
        out_shape=last,
        in_specs=[spec(pltpu.SMEM)]
        + [spec(pltpu.VMEM)] * 3
        + [spec(pl.ANY)] * 4
        + [spec(pltpu.VMEM)] * len(more),
        out_specs=[spec(pltpu.VMEM)] * len(last),
        scratch_shapes=[
            pltpu.VMEM((c.N, c.E, c.cap, c.D), BF16),
            pltpu.VMEM((2, c.D, piece), BF16),
            pltpu.VMEM((2, c.D, piece), BF16),
            pltpu.VMEM((2, c.D, piece), BF16),
            pltpu.SemaphoreType.DMA((7,)),
        ],
        compiler_params=pltpu.CompilerParams(vmem_limit_bytes=VMEM_LIMIT),
        name="last",
    )(lengths, hid, meta, g_tok, made_home, grads, gy, gx, *more)
    out, g_tok, g_in, g_down = results[:4]
    if c.gather:
        g_qkv, g_out, g_gains, g_biases, g_router = results[4:]
    else:
        both = ("expert", "dp")
        flat = dense.astype(F32).transpose(1, 0, 2).reshape(c.D, 4 * c.D)
        flat = lax.psum_scatter(flat, both, scatter_dimension=0, tiled=True)
        small = lax.psum_scatter(small, both, scatter_dimension=1, tiled=True)
        flat, small = lax.psum((flat, small), "context")
        g_qkv, g_out = flat[:, : 3 * c.D], flat[:, 3 * c.D :]
        g_gains, g_biases = small[0:2], small[2:4]
        g_router = small[LOGIT_LANE : LOGIT_LANE + c.E]
    rows = (c.N, c.B, c.D)
    return (
        out.reshape(rows),
        g_tok.reshape(rows),
        g_qkv,
        g_out,
        g_router.T,
        g_gains,
        g_biases,
        g_in[None],
        g_down[None],
    )


def pack_small(c, w_router, norm_gains, norm_biases):
    rows = jnp.concatenate([norm_gains, norm_biases, w_router.T], axis=0).astype(F32)
    return jnp.pad(rows, ((0, c.r8 - rows.shape[0]), (0, 128 - rows.shape[1])))


def per_device(
    mesh_shape,
    tokens,
    lengths,
    route_ids,
    keep_mask,
    w_qkv,
    w_attn_out,
    w_router,
    norm_gains,
    norm_biases,
    w_expert_in,
    w_expert_down,
    cotangent,
):
    images, block, width = tokens.shape
    experts = mesh_shape["expert"] * w_expert_in.shape[0]
    c = types.SimpleNamespace(
        E=experts,
        Y=mesh_shape["dp"],
        C=mesh_shape["context"],
        N=images,
        B=block,
        D=width,
        T=images * block,
        S=mesh_shape["context"] * block,
        FF=w_expert_in.shape[2],
        FB=512,
        cap=max(2, 16 * block // (5 * experts)),
        sh=w_qkv.shape[0],
        r8=-(-(LOGIT_LANE + experts) // 8) * 8,
        scale=(width // HEADS) ** -0.5,
        chunks=4,
    )
    c.gather = c.sh % 32 == 0
    tok = tokens.reshape(c.T, width)
    cot = cotangent.reshape(c.T, width)
    route = route_ids.transpose(0, 2, 1)
    keep = keep_mask.transpose(0, 2, 1)
    both = ("expert", "dp")
    if c.gather:
        given = (w_qkv, w_attn_out, pack_small(c, w_router, norm_gains, norm_biases))
    else:
        qkv = lax.all_gather(w_qkv, both, axis=0, tiled=True)
        out = lax.all_gather(w_attn_out, both, axis=0, tiled=True)
        small = pack_small(c, w_router, norm_gains, norm_biases)[:, : c.sh]
        vec = lax.all_gather(small, both, axis=1, tiled=True)
        stacked = jnp.concatenate([qkv, out], axis=1).reshape(width, 4, width).transpose(1, 0, 2)
        given = (stacked, vec)
    front = run_front(c, lengths, tok, route, keep, cot, given)
    weights, vec, q, kv, lse, att, hid, mix, meta, router, send, gsend, dyarr = front
    back = run_experts(c, send, gsend, dyarr, w_expert_in[0], w_expert_down[0])
    return run_back(
        c, tok, cot, lengths, weights, vec, q, kv, lse, att, hid, mix, meta, router, *back
    )


def solution(mesh):
    rows = P(("expert", "dp"), "context", None)
    shard = P(("expert", "dp"), None)
    column = P(None, ("expert", "dp"))
    expert = P("expert", None, None)
    return jax.shard_map(
        functools.partial(per_device, dict(mesh.shape)),
        mesh=mesh,
        in_specs=(rows, shard, rows, rows, shard, shard, shard, column, column, expert, expert, rows),
        out_specs=(
            rows,
            rows,
            shard,
            shard,
            shard,
            column,
            column,
            P("expert", None, ("context", "dp")),
            P("expert", ("context", "dp"), None),
        ),
        check_vma=False,
    )
```

```python
import functools
import itertools
import types

import jax
import jax.numpy as jnp
from jax import lax
from jax.experimental import pallas as pl
from jax.experimental.pallas import tpu as pltpu
from jax.sharding import PartitionSpec as P

HEADS = 12
EPS = 1e-06
F32 = jnp.float32
BF16 = jnp.bfloat16
MESH = pl.DeviceIdType.MESH
NN = (((1,), (0,)), ((), ()))
NT = (((1,), (1,)), ((), ()))
TN = (((0,), (0,)), ((), ()))
VMEM_LIMIT = 60 * 2**20
LOGIT_LANE = 4


def mm(left, right, dims=NN):
    return lax.dot_general(left, right, dims, preferred_element_type=F32)


def lane_of(shape):
    return lax.broadcasted_iota(jnp.int32, shape, 1)


def row_of(shape):
    return lax.broadcasted_iota(jnp.int32, shape, 0)


class Links:
    def __init__(self, send, recv):
        self.send, self.recv, self.ids = send, recv, itertools.count()

    def new(self):
        return next(self.ids)

    def make(self, at, src, dst, device):
        return pltpu.make_async_remote_copy(
            src_ref=src,
            dst_ref=dst,
            send_sem=self.send.at[at],
            recv_sem=self.recv.at[at],
            device_id=device,
            device_id_type=MESH,
        )


def greet(devices):
    barrier = pltpu.get_barrier_semaphore()
    for device in devices:
        pl.semaphore_signal(barrier, inc=1, device_id=device, device_id_type=MESH)
    pl.semaphore_wait(barrier, len(devices))


def normalize(values):
    centred = values - jnp.mean(values, axis=-1, keepdims=True)
    inverse = lax.rsqrt(jnp.mean(centred * centred, axis=-1, keepdims=True) + EPS)
    return centred * inverse, inverse


def normalize_back(grad_out, unit_rows, inverse, gain):
    scaled = grad_out * gain
    centre_term = jnp.mean(scaled, axis=-1, keepdims=True)
    slope_term = jnp.mean(scaled * unit_rows, axis=-1, keepdims=True)
    return inverse * (scaled - centre_term - unit_rows * slope_term)


def to_column(row):
    size = row.shape[1]
    eye = row_of((size, size)) == lane_of((size, size))
    return jnp.sum(jnp.where(eye, row, 0.0), axis=1, keepdims=True)


def to_row(column):
    size = column.shape[0]
    eye = row_of((size, size)) == lane_of((size, size))
    return jnp.sum(jnp.where(eye, column, 0.0), axis=0, keepdims=True)


def key_bias(c, len_ref, image):
    at = row_of((c.S, 1))
    bias = jnp.full((c.S, 1), -1e30, F32)
    for block in range(c.C):
        start = block * c.B
        inside = jnp.logical_and(at >= start, at < start + len_ref[image, block])
        bias = jnp.where(inside, 0.0, bias)
    return bias


def two_heads(pair):
    first = lane_of(pair.shape) < pair.shape[1] // 2
    zero = jnp.zeros_like(pair)
    return jnp.concatenate([jnp.where(first, pair, zero), jnp.where(first, zero, pair)], axis=0)


def one_pair(stacked):
    half = stacked.shape[0] // 2
    first = lane_of((half, stacked.shape[1])) < stacked.shape[1] // 2
    return jnp.where(first, stacked[:half], stacked[half:])


class Gather:
    def __init__(self, c, links, w_ref, rows_of, z, y, own_part, other_part):
        self.c, self.links, self.w_ref, self.rows_of = c, links, w_ref, rows_of
        self.z, self.y, self.own_part, self.other_part = z, y, own_part, other_part
        span = range(c.E)
        self.up = [links.new() for _ in span]
        self.down = [links.new() for _ in span]
        self.y_up = [links.new() for _ in span]
        self.y_down = [links.new() for _ in span]
        self.core_up = [[links.new() for _ in span] for _ in range(2)]
        self.core_down = [[links.new() for _ in span] for _ in range(2)]
        self.sent = []

    def route(self, above, below, y_dev, core_dev):
        self.above, self.below, self.y_dev, self.core_dev = above, below, y_dev, core_dev

    def unit(self, at, z_at, y_at, device, part=None):
        ref = self.w_ref.at[self.own_part if part is None else part, self.rows_of(z_at, y_at), :]
        return self.links.make(at, ref, ref, device)

    def send(self, condition, *where):
        pl.when(condition)(lambda: self.unit(*where).start())
        self.sent.append((condition, where))

    def got(self, condition, at, z_at, y_at, part=None):
        pl.when(condition)(lambda: self.unit(at, z_at, y_at, self.core_dev, part).wait_recv())

    def open(self):
        z, y = self.z, self.y
        self.send(z < self.c.E - 1, self.up[1], z, y, self.above)
        self.send(z > 0, self.down[1], z, y, self.below)
        self.send(z >= 0, self.y_up[0], z, y, self.y_dev)

    def pass_y(self, j):
        z, y = self.z, 1 - self.y
        lower, upper = z >= j, z + j <= self.c.E - 1
        self.got(lower, self.y_up[j], z - j, y)
        self.send(lower, self.core_up[1][j], z - j, y, self.core_dev)
        if j:
            self.got(upper, self.y_down[j], z + j, y)
            self.send(upper, self.core_down[1][j], z + j, y, self.core_dev)

    def step(self, j):
        z, y, last = self.z, self.y, self.c.E - 1
        if j <= last:
            lower, upper = z >= j, z + j <= last
            self.got(lower, self.up[j], z - j, y)
            if j < last:
                self.send(jnp.logical_and(lower, z < last), self.up[j + 1], z - j, y, self.above)
            self.send(lower, self.y_up[j], z - j, y, self.y_dev)
            self.send(lower, self.core_up[0][j], z - j, y, self.core_dev)
            self.got(upper, self.down[j], z + j, y)
            if j < last:
                self.send(jnp.logical_and(upper, z > 0), self.down[j + 1], z + j, y, self.below)
            self.send(upper, self.y_down[j], z + j, y, self.y_dev)
            self.send(upper, self.core_down[0][j], z + j, y, self.core_dev)
        self.pass_y(j - 1)

    def finish(self):
        z, last = self.z, self.c.E - 1
        for side in range(2):
            y = self.y if side == 0 else 1 - self.y
            if side:
                self.got(z >= 0, self.core_up[1][0], z, y, self.other_part)
            for j in range(1, self.c.E):
                self.got(z >= j, self.core_up[side][j], z - j, y, self.other_part)
                self.got(z + j <= last, self.core_down[side][j], z + j, y, self.other_part)

    def close(self):
        for condition, where in self.sent:
            pl.when(condition)(lambda: self.unit(*where).wait_send())


def front_kernel(c, *refs):
    refs = list(refs)
    take = lambda count: [refs.pop(0) for _ in range(count)]
    len_ref, tok_ref, route_ref, keep_ref, cot_ref = take(5)
    if c.gather:
        wqkv_ref, wout_ref, small_ref = take(3)
        w_hbm, vec_ref = take(2)
    else:
        w_ref, vec_ref = take(2)
    q_ref, kv_hbm, lse_ref, att_ref, hid_ref, mix_ref, meta_ref, router_ref = take(8)
    send_ref, gsend_ref, dyarr_ref = take(3)
    if c.gather:
        smalls, w_ref = take(2)
    kv_ref, dysend, lsem, ssem, rsem = take(5)
    links = Links(ssem, rsem)
    z, x, y = lax.axis_index("expert"), lax.axis_index("context"), lax.axis_index("dp")
    core = lax.rem(x, 2)
    shard = z * c.Y + y
    core_dev, far_dev, y_dev = (z, x ^ 1, y), (z, x ^ 2, y), (z, x, 1 - y)
    plane = [(lax.div(shard ^ k, c.Y), x, lax.rem(shard ^ k, c.Y)) for k in range(1, c.E * c.Y)]
    experts = [(z ^ k, x, y) for k in range(1, c.E)]
    greet([core_dev, far_dev] + (plane if c.gather else experts))
    ends = []

    def go(at, src, dst, device):
        copy = links.make(at, src, dst, device)
        copy.start()
        ends.append(copy)

    if c.gather:
        small_ids = [links.new() for _ in plane]
        smalls[shard] = small_ref[...]
        for at, device in zip(small_ids, plane):
            go(at, smalls.at[shard], smalls.at[shard], device)

        def rows_of(z_at, y_at):
            return pl.ds(pl.multiple_of((z_at * c.Y + y_at) * c.sh, 32), c.sh)

        own_rows = rows_of(z, y)
        for part in range(3):
            w_ref[part, own_rows, :] = wqkv_ref[:, part * c.D : (part + 1) * c.D]
        w_ref[3, own_rows, :] = wout_ref[...]

        above, below = (lax.rem(z + 1, c.E), x, y), (lax.rem(z + c.E - 1, c.E), x, y)
        stages = [Gather(c, links, w_ref, rows_of, z, y, *parts) for parts in (
            (1 + core, 2 - core), (3 * core, 3 - 3 * core))]
        for stage in stages:
            stage.route(above, below, y_dev, core_dev)
        stages[0].open()

    unit_rows = [None] * c.N
    choices = []
    for image in range(c.N):
        rows = slice(image * c.B, (image + 1) * c.B)
        live = jnp.where(row_of((c.B, 1)) < len_ref[image, x], 1.0, 0.0)
        kept = [to_column(keep_ref[image, j : j + 1, :].astype(F32)) * live for j in range(2)]
        first, second = [
            to_column(route_ref[image, j : j + 1, :].astype(F32)).astype(jnp.int32) for j in range(2)
        ]
        lane = lane_of((c.B, 128))
        named = jnp.where(lane == first, kept[0], 0.0) + jnp.where(
            lane == second, kept[1], 0.0
        )
        earlier = jnp.where(lane_of((c.B, c.B)) < row_of((c.B, c.B)), 1.0, 0.0).astype(BF16)
        rank = mm(earlier, named.astype(BF16))
        rank_first = jnp.sum(jnp.where(lane == first, rank, 0.0), axis=1, keepdims=True)
        rank_second = jnp.sum(jnp.where(lane == second, rank, 0.0), axis=1, keepdims=True)
        slot_first = first * c.cap + rank_first.astype(jnp.int32)
        slot_second = second * c.cap + rank_second.astype(jnp.int32)
        at = lane_of((c.B, c.E * c.cap))
        place = jnp.where(at == slot_first, kept[0], 0.0) + jnp.where(
            at == slot_second, kept[1], 0.0
        )
        place = place.astype(BF16)
        choices.append((first, second, kept, slot_first, slot_second, place))
        dysend[image] = mm(place, cot_ref[rows, :], TN).astype(BF16).reshape(c.E, c.cap, c.D)

    if c.gather:
        for at, device in zip(small_ids, plane):
            other = lax.div(shard, 1)
            links.make(at, smalls.at[other], smalls.at[other], device).wait_recv()
        wide = jnp.concatenate([smalls[k] for k in range(c.E * c.Y)], axis=1).astype(BF16)
        span = c.E * c.Y * 128
        src, dst = row_of((span, c.D)), lane_of((span, c.D))
        inside = lax.rem(src, 128)
        pick = jnp.logical_and(inside < c.sh, lax.div(src, 128) * c.sh + inside == dst)
        vec_ref[...] = mm(wide, jnp.where(pick, 1.0, 0.0).astype(BF16))
    vec = vec_ref[...]
    own_at = pl.ds(pl.multiple_of(x * c.B, 32), c.B)
    norm_ids = [[links.new() for _ in range(3)] for _ in range(c.N)]
    for image in range(c.N):
        rows = slice(image * c.B, (image + 1) * c.B)
        unit_one, _ = normalize(tok_ref[rows, :].astype(F32))
        kv_ref[image, own_at, 2 * c.D : 3 * c.D] = (unit_one * vec[0:1] + vec[2:3]).astype(BF16)
        block = kv_ref.at[image, own_at, 2 * c.D : 3 * c.D]
        go(norm_ids[image][0], block, block, far_dev)
        go(norm_ids[image][1], block, block, core_dev)

    if c.gather:
        stages[0].step(1)
        stages[1].open()
        for j in range(2, c.E + 1):
            stages[0].step(j)
        stages[0].finish()

    normed = jnp.concatenate(
        [kv_ref[image, own_at, 2 * c.D : 3 * c.D] for image in range(c.N)], axis=0
    )
    kv_ids = [[links.new() for _ in range(3)] for _ in range(c.N)]
    keys = mm(normed, w_ref[1]).astype(BF16)
    values = mm(normed, w_ref[2]).astype(BF16)
    for image in range(c.N):
        rows = slice(image * c.B, (image + 1) * c.B)
        kv_ref[image, own_at, 0 : c.D] = keys[rows]
        kv_ref[image, own_at, c.D : 2 * c.D] = values[rows]
        block = kv_ref.at[image, own_at, 0 : 2 * c.D]
        go(kv_ids[image][0], block, block, far_dev)
        go(kv_ids[image][1], block, block, core_dev)
    if c.gather:
        for j in range(1, c.E + 1):
            stages[1].step(j)
    dy_ids = [links.new() for _ in experts]
    for k, (at, device) in enumerate(zip(dy_ids, experts), 1):
        go(at, dysend.at[:, z ^ k], dyarr_ref.at[z], device)
    own_dy = pltpu.make_async_copy(dysend.at[:, z], dyarr_ref.at[z], lsem.at[0])
    own_dy.start()
    leaving = [own_dy]
    if c.gather:
        stages[1].finish()
        leaving.append(pltpu.make_async_copy(w_ref, w_hbm, lsem.at[1]))
        leaving[-1].start()
    q_ref[...] = mm(normed, w_ref[0]).astype(BF16)

    def block_of(image, who, first=0, last=2):
        rows_at = pl.ds(pl.multiple_of(who * c.B, 32), c.B)
        return kv_ref.at[image, rows_at, first * c.D : last * c.D]

    for image in range(c.N):
        far_block = block_of(image, x ^ 2, 2, 3)
        links.make(norm_ids[image][0], far_block, far_block, far_dev).wait_recv()
        go(norm_ids[image][2], far_block, far_block, core_dev)

    for image in range(c.N):
        rows = pl.ds(image * c.B, c.B)
        far_block = block_of(image, x ^ 2)
        links.make(kv_ids[image][0], far_block, far_block, far_dev).wait_recv()
        go(kv_ids[image][2], far_block, far_block, core_dev)
        near_block = block_of(image, x ^ 1)
        links.make(kv_ids[image][1], near_block, near_block, core_dev).wait_recv()
        cross_block = block_of(image, x ^ 3)
        links.make(kv_ids[image][2], cross_block, cross_block, core_dev).wait_recv()
        for at, who in ((1, x ^ 1), (2, x ^ 3)):
            there = block_of(image, who, 2, 3)
            links.make(norm_ids[image][at], there, there, core_dev).wait_recv()
        leaving.append(pltpu.make_async_copy(kv_ref.at[image], kv_hbm.at[image], lsem.at[2 + image]))
        leaving[-1].start()
        bias = key_bias(c, len_ref, image)

        def pair_step(pair, carry):
            lanes = pl.ds(pl.multiple_of(pair * 128, 128), 128)
            value_lanes = pl.ds(pl.multiple_of(c.D + pair * 128, 128), 128)
            queries = two_heads(q_ref[rows, lanes]) * jnp.asarray(c.scale, BF16)
            scores = mm(kv_ref[image, :, lanes], queries, NT) + bias
            top = jnp.max(scores, axis=0, keepdims=True)
            exponent = jnp.exp(scores - top)
            total = jnp.sum(exponent, axis=0, keepdims=True)
            probs = (exponent * (1.0 / total)).astype(BF16)
            lse_ref[image, pair] = jnp.broadcast_to(top + jnp.log(total), (8, 2 * c.B))
            mixed_values = mm(kv_ref[image, :, value_lanes].T, probs)
            att_ref[rows, lanes] = one_pair(mixed_values.T).astype(BF16)
            return carry

        lax.fori_loop(0, c.D // 128, pair_step, 0)

    branch = mm(att_ref[...], w_ref[3])
    hidden = tok_ref[...].astype(F32) + branch
    hid_ref[...] = hidden
    unit_two, _ = normalize(hidden)
    mixed = (unit_two * vec[1:2] + vec[3:4]).astype(BF16)
    mix_ref[...] = mixed
    pad = jnp.zeros((128 - c.r8, c.D), BF16)
    logits = mm(mixed, jnp.concatenate([vec.astype(BF16), pad], axis=0), NT)
    lane = lane_of((c.N * c.B, 128))
    valid = jnp.logical_and(lane >= LOGIT_LANE, lane < LOGIT_LANE + c.E)
    logits = jnp.where(valid, logits, -1e30)
    weight = jnp.exp(logits - jnp.max(logits, axis=1, keepdims=True))
    router = weight / jnp.sum(weight, axis=1, keepdims=True)
    router_ref[...] = router
    gsend_ref[...] = jnp.zeros_like(gsend_ref)
    lane = lane_of((c.B, 128))
    for image in range(c.N):
        rows = slice(image * c.B, (image + 1) * c.B)
        first, second, kept, slot_first, slot_second, place = choices[image]
        here = router[rows]
        gate_first = kept[0] * jnp.sum(
            jnp.where(lane == LOGIT_LANE + first, here, 0.0), axis=1, keepdims=True
        )
        gate_second = kept[1] * jnp.sum(
            jnp.where(lane == LOGIT_LANE + second, here, 0.0), axis=1, keepdims=True
        )
        send_ref[image] = mm(place, mixed[rows], TN).astype(BF16).reshape(c.E, c.cap, c.D)
        at = lane_of((c.B, c.cap))
        for expert in range(c.E):
            gates = jnp.where(at == slot_first - expert * c.cap, gate_first, 0.0)
            gates = gates + jnp.where(at == slot_second - expert * c.cap, gate_second, 0.0)
            gsend_ref[expert, image : image + 1, :] = jnp.sum(gates, axis=0, keepdims=True)
        columns = (
            slot_first.astype(F32),
            slot_second.astype(F32),
            kept[0],
            kept[1],
            gate_first,
            gate_second,
            first.astype(F32),
            second.astype(F32),
        )
        meta = jnp.zeros((c.B, 128), F32)
        for index, column in enumerate(columns):
            meta = jnp.where(lane == index, column, meta)
        meta_ref[rows, :] = meta

    for k, (at, device) in enumerate(zip(dy_ids, experts), 1):
        links.make(at, dyarr_ref.at[z ^ k], dyarr_ref.at[z ^ k], device).wait_recv()
    for copy in leaving:
        copy.wait()
    for copy in ends:
        copy.wait_send()
    if c.gather:
        for stage in stages:
            stage.close()


def spec(space):
    return pl.BlockSpec(memory_space=space)


def run_front(c, lengths, tok, route, keep, cot, weights):
    shape = jax.ShapeDtypeStruct
    made = [shape((4, c.D, c.D), BF16), shape((c.r8, c.D), F32)] if c.gather else []
    made += [
        shape((c.T, c.D), BF16),
        shape((c.N, c.S, 3 * c.D), BF16),
        shape((c.N, c.D // 128, 8, 2 * c.B), F32),
        shape((c.T, c.D), BF16),
        shape((c.T, c.D), F32),
        shape((c.T, c.D), BF16),
        shape((c.T, 128), F32),
        shape((c.T, 128), F32),
        shape((c.N, c.E, c.cap, c.D), BF16),
        shape((c.E, 8, c.cap), F32),
        shape((c.E, c.N, c.cap, c.D), BF16),
    ]
    count = 112 if c.gather else 2 * c.E + 32
    places = [spec(pltpu.VMEM)] * len(made)
    places[-1] = places[-10] = spec(pl.ANY)
    gather_scratch = []
    if c.gather:
        places[0] = spec(pl.ANY)
        gather_scratch = [
            pltpu.VMEM((c.E * c.Y, c.r8, 128), F32),
            pltpu.VMEM((4, c.D, c.D), BF16),
        ]
    out = pl.pallas_call(
        functools.partial(front_kernel, c),
        out_shape=made,
        in_specs=[spec(pltpu.SMEM)] + [spec(pltpu.VMEM)] * (4 + len(weights)),
        out_specs=places,
        scratch_shapes=gather_scratch
        + [
            pltpu.VMEM((c.N, c.S, 3 * c.D), BF16),
            pltpu.VMEM((c.N, c.E, c.cap, c.D), BF16),
            pltpu.SemaphoreType.DMA((2 + c.N,)),
            pltpu.SemaphoreType.DMA((count,)),
            pltpu.SemaphoreType.DMA((count,)),
        ],
        compiler_params=pltpu.CompilerParams(
            collective_id=0, has_side_effects=True, vmem_limit_bytes=VMEM_LIMIT
        ),
        name="front",
    )(lengths, tok, route, keep, cot, *weights)
    return out if c.gather else list(weights) + list(out)


def gelu_both(pre):
    inner = 0.7978845608028654 * (pre + 0.044715 * pre * pre * pre)
    bend = jnp.tanh(inner)
    half = 0.5 * (1.0 + bend)
    slope = 0.7978845608028654 * (1.0 + 0.134145 * pre * pre)
    return pre * half, half + 0.5 * pre * (1.0 - bend * bend) * slope


def expert_kernel(
    c,
    send_ref,
    gsend_ref,
    dyarr_ref,
    win_hbm,
    wdown_hbm,
    xback_ref,
    gback_ref,
    yloc_ref,
    grad_hbm,
    gnext_hbm,
    win,
    wdown,
    arr,
    garr,
    act_all,
    dpre_all,
    dout_all,
    dxs,
    dgs,
    turned,
    gsend,
    grecv,
    gown,
    wsem,
    ssem,
    rsem,
):
    links = Links(ssem, rsem)
    z, x, y = lax.axis_index("expert"), lax.axis_index("context"), lax.axis_index("dp")
    experts = [(z ^ k, x, y) for k in range(1, c.E)]
    load_in = pltpu.make_async_copy(win_hbm, win, wsem.at[0])
    load_down = pltpu.make_async_copy(wdown_hbm, wdown, wsem.at[1])
    load_in.start()
    load_down.start()
    greet(experts + [(z, x ^ 1, y), (z, x ^ 2, y), (z, x, 1 - y)])
    ids = [[links.new() for _ in range(4)] for _ in range(c.E)]
    ends = []

    def go(at, src, dst, device):
        copy = links.make(at, src, dst, device)
        copy.start()
        ends.append(copy)

    group = c.E // c.chunks
    height = group * c.N * c.cap

    def dispatch(g):
        started = len(ends)
        for k in range(max(1, g * group), (g + 1) * group):
            go(ids[k][1], gsend_ref.at[z ^ k], garr.at[z], experts[k - 1])
            go(ids[k][0], send_ref.at[:, z ^ k], arr.at[z], experts[k - 1])
        return ends[started:]

    dispatch(0)
    early = dispatch(c.chunks - 2)
    for g in range(1, c.chunks - 2):
        dispatch(g)
    for image in range(c.N):
        arr[z, image] = send_ref[image, z]
    garr[z] = gsend_ref[z]
    load_in.wait()
    load_down.wait()
    dgs[...] = jnp.zeros_like(dgs)
    for g in range(c.chunks):
        if g == 1:
            for copy in early:
                copy.wait_send()
            ends[:] = [copy for copy in ends if all(copy is not other for other in early)]
            dispatch(c.chunks - 1)
        slab = lax.div(z, group) ^ g
        for k in range(g * group, (g + 1) * group):
            if k:
                there = z ^ k
                links.make(ids[k][0], arr.at[there], arr.at[there], experts[k - 1]).wait_recv()
                links.make(ids[k][1], garr.at[there], garr.at[there], experts[k - 1]).wait_recv()
        start = pl.multiple_of(slab * height, 32)
        rows = pl.ds(start, height)
        for member in range(group):
            source = slab * group + member
            for image in range(c.N):
                gates = to_column(garr[source, image : image + 1, :])
                offset = (member * c.N + image) * c.cap
                part = pl.ds(pl.multiple_of(start + offset, 16), c.cap)
                dout_all[part, :] = (gates * dyarr_ref[source, image].astype(F32)).astype(BF16)
        inputs = arr[pl.ds(slab * group, group)].reshape(height, c.D)
        douts = dout_all[rows, :]

        def ff_step(step, carry):
            lanes = pl.ds(pl.multiple_of(step * c.FB, 128), c.FB)
            pre = mm(inputs, win[:, lanes])
            act, slope = gelu_both(pre)
            act_all[rows, lanes] = act.astype(BF16)
            dact = mm(douts, wdown[lanes, :], NT)
            dpre_all[rows, lanes] = (dact * slope).astype(BF16)
            return carry

        lax.fori_loop(0, c.FF // c.FB, ff_step, 0)
        dx = mm(dpre_all[rows, :], win[...], NT).astype(BF16)
        dxs[pl.ds(slab * group, group)] = dx.reshape(group, c.N, c.cap, c.D)
        made = mm(act_all[rows, :], wdown[...]).astype(BF16)
        yloc_ref[pl.ds(slab * group, group)] = made.reshape(group, c.N, c.cap, c.D)
        for member in range(group):
            source = slab * group + member
            for image in range(c.N):
                offset = (member * c.N + image) * c.cap
                dots = made[offset : offset + c.cap].astype(F32) * dyarr_ref[source, image].astype(
                    F32
                )
                dgs[source, image : image + 1, :] = to_row(jnp.sum(dots, axis=1, keepdims=True))
        for k in range(g * group, (g + 1) * group):
            if k:
                there = z ^ k
                go(ids[k][2], dxs.at[there], xback_ref.at[:, z], experts[k - 1])
                go(ids[k][3], dgs.at[there], gback_ref.at[z], experts[k - 1])
    for image in range(c.N):
        xback_ref[image, z] = dxs[z, image]
    gback_ref[z] = dgs[z]

    total = c.E * c.N * c.cap
    turned[0] = arr[...].reshape(total, c.D).T
    turned[1] = dout_all[...].T

    core = lax.rem(x, 2)
    core_dev, far_dev, y_dev = (z, x ^ 1, y), (z, x ^ 2, y), (z, x, 1 - y)
    half = c.FF // 4
    grad_ids = [[links.new() for _ in range(2)] for _ in range(2)]
    sources = (dpre_all, act_all)

    def blocks(which, owner, into):
        def block_step(part, carry):
            lanes = pl.ds(pl.multiple_of((2 * part + owner) * half, 128), half)
            into[part, which] = mm(turned[which], sources[which][:, lanes]).astype(BF16)
            return carry

        lax.fori_loop(0, 2, block_step, 0)

    piece = half // 2
    side = lax.div(x, 2)
    other_piece = pl.ds(pl.multiple_of((1 - y) * piece, 128), piece)
    next_ids = [links.new() for _ in range(2)]
    leaving = []
    for which in range(2):
        blocks(which, 1 - core, gsend)
        for part in range(2):
            go(grad_ids[which][part], gsend.at[part, which], grecv.at[part, which], core_dev)
        blocks(which, core, gown)
        for part in range(2):
            there = grecv.at[part, which]
            links.make(grad_ids[which][part], there, there, core_dev).wait_recv()
            gown[part, which] = (
                gown[part, which].astype(F32) + grecv[part, which].astype(F32)
            ).astype(BF16)
        first = gown.at[1 - side, which, :, other_piece]
        go(next_ids[which], first, gnext_hbm.at[which], y_dev if which == 0 else far_dev)
        for part in range(2):
            leaving.append(
                pltpu.make_async_copy(
                    gown.at[part, which], grad_hbm.at[part, which], wsem.at[2 + 2 * which + part]
                )
            )
            leaving[-1].start()
    for which in range(2):
        there = gnext_hbm.at[which]
        links.make(next_ids[which], there, there, core_dev).wait_recv()
    for copy in leaving:
        copy.wait()
    for k in range(1, c.E):
        there = z ^ k
        links.make(ids[k][2], xback_ref.at[:, there], xback_ref.at[:, there], experts[k - 1]).wait_recv()
        links.make(ids[k][3], gback_ref.at[there], gback_ref.at[there], experts[k - 1]).wait_recv()
    for copy in ends:
        copy.wait_send()


def run_experts(c, send, gsend, dyarr, w_in, w_down):
    shape = jax.ShapeDtypeStruct
    total = c.E * c.N * c.cap
    count = 4 * c.E + 6
    return pl.pallas_call(
        functools.partial(expert_kernel, c),
        out_shape=[
            shape((c.N, c.E, c.cap, c.D), BF16),
            shape((c.E, 8, c.cap), F32),
            shape((c.E, c.N, c.cap, c.D), BF16),
            shape((2, 2, c.D, c.FF // 4), BF16),
            shape((2, c.D, c.FF // 8), BF16),
        ],
        in_specs=[spec(pltpu.VMEM)] * 3 + [spec(pl.ANY)] * 2,
        out_specs=[spec(pltpu.VMEM)] * 3 + [spec(pl.ANY)] * 2,
        scratch_shapes=[
            pltpu.VMEM((c.D, c.FF), BF16),
            pltpu.VMEM((c.FF, c.D), BF16),
            pltpu.VMEM((c.E, c.N, c.cap, c.D), BF16),
            pltpu.VMEM((c.E, 8, c.cap), F32),
            pltpu.VMEM((total, c.FF), BF16),
            pltpu.VMEM((total, c.FF), BF16),
            pltpu.VMEM((total, c.D), BF16),
            pltpu.VMEM((c.E, c.N, c.cap, c.D), BF16),
            pltpu.VMEM((c.E, 8, c.cap), F32),
            pltpu.VMEM((2, c.D, total), BF16),
            pltpu.VMEM((2, 2, c.D, c.FF // 4), BF16),
            pltpu.VMEM((2, 2, c.D, c.FF // 4), BF16),
            pltpu.VMEM((2, 2, c.D, c.FF // 4), BF16),
            pltpu.SemaphoreType.DMA((6,)),
            pltpu.SemaphoreType.DMA((count,)),
            pltpu.SemaphoreType.DMA((count,)),
        ],
        compiler_params=pltpu.CompilerParams(
            collective_id=1, has_side_effects=True, vmem_limit_bytes=VMEM_LIMIT
        ),
        name="experts",
    )(send, gsend, dyarr, w_in, w_down)


def in_parts(values, count):
    parts = []
    for _ in range(count):
        parts.append(values.astype(BF16))
        values = values - parts[-1].astype(F32)
    return parts


def back_kernel(c, *refs):
    refs = list(refs)
    take = lambda count: [refs.pop(0) for _ in range(count)]
    len_ref, tok_ref, cot_ref, vec_ref, q_ref, lse_ref, att_ref, hid_ref, mix_ref = take(9)
    meta_ref, router_ref, xback_ref, gback_ref = take(4)
    w_hbm, kv_hbm, yloc_hbm, grad_hbm, gnext_hbm = take(5)
    gtok_hbm, made, gy, gx = take(4)
    if c.gather:
        whole, gsmall_ref = take(2)
    else:
        dd, gsmall_ref = take(2)
    w_ref, kv_ref, gtok_ref, gpart, gnext = take(5)
    dkv, kvcore, kvfar, dproj, datt, dhid, norm_t, norm_all, router_sum = take(9)
    if c.gather:
        dd, dcore, done_x, done_y, done_z, small_four, small_y, small_z = take(8)
    lsem, ssem, rsem = take(3)
    links = Links(ssem, rsem)
    z, x, y = lax.axis_index("expert"), lax.axis_index("context"), lax.axis_index("dp")
    core, side = lax.rem(x, 2), lax.div(x, 2)
    core_dev, far_dev, y_dev = (z, x ^ 1, y), (z, x ^ 2, y), (z, x, 1 - y)
    experts = [(z ^ k, x, y) for k in range(1, c.E)]
    ends = []

    def go(at, src, dst, device):
        copy = links.make(at, src, dst, device)
        copy.start()
        ends.append(copy)

    def got(at, dst, device):
        links.make(at, dst, dst, device).wait_recv()

    half = c.FF // 4
    piece = half // 2
    loads = [
        pltpu.make_async_copy(w_hbm, w_ref, lsem.at[0]),
        pltpu.make_async_copy(kv_hbm, kv_ref, lsem.at[1]),
    ]
    own_piece = pl.ds(pl.multiple_of(y * piece, 128), piece)
    other_piece = pl.ds(pl.multiple_of((1 - y) * piece, 128), piece)
    parts = (grad_hbm.at[1 - side, 0, :, own_piece], grad_hbm.at[side, 1, :, other_piece])
    for which in range(2):
        loads.append(pltpu.make_async_copy(parts[which], gpart.at[which], lsem.at[2 + which]))
        loads.append(
            pltpu.make_async_copy(gnext_hbm.at[which], gnext.at[which], lsem.at[6 + which])
        )
    own_made = pltpu.make_async_copy(yloc_hbm.at[z], made.at[:, z], lsem.at[4])
    loads.append(own_made)
    for load in loads:
        load.start()
    cross_dev = [(z, x ^ 3, y)] if c.gather else []
    greet([core_dev, far_dev, y_dev] + experts + cross_dev)

    made_ids = [links.new() for _ in experts]
    for k, (at, device) in enumerate(zip(made_ids, experts), 1):
        go(at, yloc_hbm.at[z ^ k], made.at[:, z], device)
    gy_ids = [links.new() for _ in range(2)]
    gx_ids = [links.new() for _ in range(2)]
    go(gy_ids[0], grad_hbm.at[side, 0, :, other_piece], gy.at[0], y_dev)
    go(gx_ids[1], grad_hbm.at[1 - side, 1, :, own_piece], gx.at[1], far_dev)
    for which in range(2):
        loads[2 + 2 * which].wait()
        loads[3 + 2 * which].wait()
        gpart[which] = (gpart[which].astype(F32) + gnext[which].astype(F32)).astype(BF16)
        if which == 0:
            go(gx_ids[0], gpart.at[0], gx.at[0], far_dev)
        else:
            go(gy_ids[1], gpart.at[1], gy.at[1], y_dev)

    def grads_end():
        for which in range(2):
            got(gy_ids[which], gy.at[which], y_dev)
            got(gx_ids[which], gx.at[which], far_dev)

    if c.gather:
        n_dense = 4
        core_cols = c.D // 2
        keep_cols = pl.ds(pl.multiple_of(core * core_cols, 128), core_cols)
        give_cols = pl.ds(pl.multiple_of((1 - core) * core_cols, 128), core_cols)
        ids_core = [links.new() for _ in range(n_dense)]
        ids_x = [links.new() for _ in range(n_dense)]
        ids_y = [links.new() for _ in range(n_dense)]
        ids_z = [[links.new() for _ in experts] for _ in range(n_dense)]
        ids_own = [links.new() for _ in range(n_dense)]

        def dense_start(m, value):
            dd[m] = value.astype(BF16).reshape(c.E, c.Y, c.sh, c.D)
            go(ids_core[m], dd.at[m, :, :, :, give_cols], dcore.at[m], core_dev)

        def dense_y(m):
            got(ids_core[m], dcore.at[m], core_dev)
            dd[m, :, :, :, keep_cols] = (
                dd[m, :, :, :, keep_cols].astype(F32) + dcore[m].astype(F32)
            ).astype(BF16)
            go(ids_y[m], dd.at[m, :, 1 - y, :, keep_cols], done_y.at[m], y_dev)

        def dense_z(m):
            got(ids_y[m], done_y.at[m], y_dev)
            dd[m, :, y, :, keep_cols] = (
                dd[m, :, y, :, keep_cols].astype(F32) + done_y[m].astype(F32)
            ).astype(BF16)
            for k, device in enumerate(experts, 1):
                go(
                    ids_z[m][k - 1],
                    dd.at[m, z ^ k, y, :, keep_cols],
                    done_z.at[m, z],
                    device,
                )

        def dense_x(m):
            total = dd[m, z, y, :, keep_cols].astype(F32)
            for k, device in enumerate(experts, 1):
                got(ids_z[m][k - 1], done_z.at[m, z ^ k], device)
                total = total + done_z[m, z ^ k].astype(F32)
            done_x[m, 0] = total.astype(BF16)
            go(ids_x[m], done_x.at[m, 0], done_x.at[m, 1], far_dev)

        def dense_share(m):
            got(ids_x[m], done_x.at[m, 1], far_dev)
            whole[m, core] = done_x[m, 0].astype(F32) + done_x[m, 1].astype(F32)
            go(ids_own[m], whole.at[m, core], whole.at[m, core], core_dev)

        def dense_end(m):
            there = whole.at[m, 1 - core]
            got(ids_own[m], there, core_dev)

    else:

        def dense_start(m, value):
            dd[m] = value.astype(BF16)

    vec = vec_ref[...]
    lane = lane_of((c.B, 128))
    d_mixed, dy_rows = [], []
    d_logits = []
    for image in range(c.N):
        rows = slice(image * c.B, (image + 1) * c.B)
        meta = meta_ref[rows, :]
        slots = [meta[:, j : j + 1].astype(jnp.int32) for j in range(2)]
        kept = [meta[:, 2 + j : 3 + j] for j in range(2)]
        names = [meta[:, 6 + j : 7 + j].astype(jnp.int32) for j in range(2)]
        at = lane_of((c.B, c.E * c.cap))
        place = jnp.where(at == slots[0], kept[0], 0.0) + jnp.where(at == slots[1], kept[1], 0.0)
        copies = xback_ref[image].reshape(c.E * c.cap, c.D)
        d_mixed.append(mm(place.astype(BF16), copies))
        d_router = jnp.zeros((c.B, 128), F32)
        at = lane_of((c.B, c.cap))
        for j in range(2):
            d_gate = jnp.zeros((c.B, c.cap), F32)
            for expert in range(c.E):
                row = gback_ref[expert, image : image + 1, :]
                d_gate = d_gate + jnp.where(at == slots[j] - expert * c.cap, row, 0.0)
            d_gate = jnp.sum(d_gate, axis=1, keepdims=True) * kept[j]
            d_router = d_router + jnp.where(lane == LOGIT_LANE + names[j], d_gate, 0.0)
        router = router_ref[rows, :]
        dot = jnp.sum(router * d_router, axis=1, keepdims=True)
        d_logits.append(router * (d_router - dot))
        live = jnp.where(row_of((c.B, 1)) < len_ref[image, x], 1.0, 0.0)
        dy_rows.append(cot_ref[rows, :].astype(F32) * live)
    d_mixed = jnp.concatenate(d_mixed, axis=0)
    d_logits = jnp.concatenate(d_logits, axis=0)
    dy_rows = jnp.concatenate(dy_rows, axis=0)
    logit_rows = jnp.concatenate([vec, jnp.zeros((128 - c.r8, c.D), F32)], axis=0)
    lane_here = row_of((128, c.D))
    is_router = jnp.logical_and(lane_here >= LOGIT_LANE, lane_here < LOGIT_LANE + c.E)
    w_router = jnp.where(is_router, logit_rows, 0.0)
    high, low = in_parts(d_logits, 2)
    w_router = w_router.astype(BF16)
    d_mixed = d_mixed + mm(high, w_router) + mm(low, w_router)
    router_sum[...] = mm(high, mix_ref[...], TN) + mm(low, mix_ref[...], TN)
    unit_two, inverse_two = normalize(hid_ref[...])
    gains_two = jnp.sum(d_mixed * unit_two, axis=0, keepdims=True)
    biases_two = jnp.sum(d_mixed, axis=0, keepdims=True)
    d_hidden = dy_rows + normalize_back(d_mixed, unit_two, inverse_two, vec[1:2])
    dhid[...] = d_hidden
    d_branch = d_hidden.astype(BF16)
    dense_start(3, mm(att_ref[...], d_branch, TN))
    loads[0].wait()
    datt[...] = mm(d_branch, w_ref[3], NT).astype(BF16)
    unit_one, inverse_one = normalize(tok_ref[...].astype(F32))
    norm_t[...] = (unit_one * vec[0:1] + vec[2:3]).astype(BF16).T
    loads[1].wait()
    for image in range(c.N):
        norm_all[:, image * c.S : (image + 1) * c.S] = kv_ref[image, :, 2 * c.D : 3 * c.D].T

    kvcore_ids = [[links.new() for _ in range(2)] for _ in range(c.N)]
    kvfar_ids = [links.new() for _ in range(c.N)]

    def block_rows(who):
        return pl.ds(pl.multiple_of(who * c.B, 32), c.B)

    def attend_back(image, first_pair, last_pair):
        rows = pl.ds(image * c.B, c.B)
        bias = key_bias(c, len_ref, image)

        def pair_step(pair, carry):
            lanes = pl.ds(pl.multiple_of(pair * 128, 128), 128)
            value_lanes = pl.ds(pl.multiple_of(c.D + pair * 128, 128), 128)
            scale = jnp.asarray(c.scale, BF16)
            queries = two_heads(q_ref[rows, lanes]) * scale
            grads = two_heads(datt[rows, lanes])
            keys = kv_ref[image, :, lanes]
            probs = jnp.exp(mm(keys, queries, NT) + bias - lse_ref[image, pair][0:1])
            d_probs = mm(kv_ref[image, :, value_lanes], grads, NT)
            dot = jnp.sum(probs * d_probs, axis=0, keepdims=True)
            d_scores = (probs * (d_probs - dot)).astype(BF16)
            dkv[image, :, value_lanes] = mm(probs.astype(BF16), grads).astype(BF16)
            dkv[image, :, lanes] = mm(d_scores, queries).astype(BF16)
            d_queries = mm(keys.T, d_scores).T
            dproj[rows, lanes] = (one_pair(d_queries) * c.scale).astype(BF16)
            return carry

        lax.fori_loop(first_pair, last_pair, pair_step, 0)

    def kv_to_core(image):
        for s in range(2):
            block = dkv.at[image, block_rows(2 * s + 1 - core), :]
            go(kvcore_ids[image][s], block, kvcore.at[image, s], core_dev)

    def kv_to_far(image):
        for s in range(2):
            got(kvcore_ids[image][s], kvcore.at[image, s], core_dev)
        rows = block_rows(2 * (1 - side) + core)
        kvcore[image, 1 - side] = (
            dkv[image, rows, :].astype(F32) + kvcore[image, 1 - side].astype(F32)
        ).astype(BF16)
        go(kvfar_ids[image], kvcore.at[image, 1 - side], kvfar.at[image], far_dev)

    def kv_end(image):
        got(kvfar_ids[image], kvfar.at[image], far_dev)
        total = dkv[image, block_rows(2 * side + core), :].astype(F32)
        total = total + kvcore[image, side].astype(F32) + kvfar[image].astype(F32)
        rows = pl.ds(image * c.B, c.B)
        dproj[rows, c.D : 3 * c.D] = total.astype(BF16)

    pairs = c.D // 128
    attend_back(0, 0, pairs)
    kv_to_core(0)
    if c.gather:
        dense_y(3)
    attend_back(1, 0, pairs // 2)
    kv_to_far(0)
    attend_back(1, pairs // 2, pairs)
    kv_to_core(1)
    dense_start(0, mm(norm_t[...], dproj[:, 0 : c.D]))
    for m in (1, 2):
        columns = slice((m - 1) * c.D, m * c.D)
        dense_start(m, mm(norm_all[...], dkv[:, :, columns].reshape(c.N * c.S, c.D)))
    kv_to_far(1)
    if c.gather:
        dense_y(0)
        dense_y(1)
        dense_y(2)
        dense_z(3)
        kv_end(0)
        dense_z(0)
        dense_x(3)
        dense_z(1)
    else:
        kv_end(0)
    kv_end(1)
    d_normed = mm(dproj[:, 0 : c.D], w_ref[0], NT)
    d_normed = d_normed + mm(dproj[:, c.D : 2 * c.D], w_ref[1], NT)
    d_normed = d_normed + mm(dproj[:, 2 * c.D : 3 * c.D], w_ref[2], NT)
    unit_one, inverse_one = normalize(tok_ref[...].astype(F32))
    gains_one = jnp.sum(d_normed * unit_one, axis=0, keepdims=True)
    biases_one = jnp.sum(d_normed, axis=0, keepdims=True)
    small_here = jnp.concatenate([gains_one, gains_two, biases_one, biases_two], axis=0)
    small_here = jnp.concatenate(
        [small_here, router_sum[LOGIT_LANE : LOGIT_LANE + c.r8 - 4]], axis=0
    )
    if c.gather:
        small_ids = [links.new() for _ in range(3)]
        small_y_id = links.new()
        small_z_ids = [links.new() for _ in experts]
        small_four[x] = small_here
        for k, at in enumerate(small_ids, 1):
            go(at, small_four.at[x], small_four.at[x], (z, x ^ k, y))
    gtok_ref[...] = dhid[...] + normalize_back(d_normed, unit_one, inverse_one, vec[0:1])
    leave = pltpu.make_async_copy(gtok_ref, gtok_hbm, lsem.at[5])
    leave.start()
    if c.gather:

        dense_x(0)
        dense_share(3)
        dense_z(2)
        for k, at in enumerate(small_ids, 1):
            got(at, small_four.at[x ^ k], (z, x ^ k, y))
        small_y[0] = (small_four[0] + small_four[1]) + (small_four[2] + small_four[3])
        go(small_y_id, small_y.at[0], small_y.at[1], y_dev)
        dense_x(1)
        dense_share(0)
        got(small_y_id, small_y.at[1], y_dev)
        small_z[z] = small_y[0] + small_y[1]
        for at, device in zip(small_z_ids, experts):
            go(at, small_z.at[z], small_z.at[z], device)
        dense_end(3)
        dense_x(2)
        dense_share(1)
        dense_end(0)
        for k, (at, device) in enumerate(zip(small_z_ids, experts), 1):
            got(at, small_z.at[z ^ k], device)
        gsmall_ref[...] = sum((small_z[k] for k in range(1, c.E)), small_z[0])
        dense_share(2)
        dense_end(1)
        dense_end(2)
    else:
        gsmall_ref[...] = small_here
    for k, (at, device) in enumerate(zip(made_ids, experts), 1):
        got(at, made.at[:, z ^ k], device)
    grads_end()
    leave.wait()
    own_made.wait()
    for copy in ends:
        copy.wait_send()


def last_kernel(c, *refs):
    refs = list(refs)
    take = lambda count: [refs.pop(0) for _ in range(count)]
    len_ref, hid_ref, meta_ref, gtok_in, made_in, grad_in, gy_in, gx_in = take(8)
    if c.gather:
        whole_ref, small_ref = take(2)
    out_ref, gtok_out, gin_ref, gdown_ref = take(4)
    if c.gather:
        gqkv_ref, gout_ref, gains_ref, biases_ref, grouter_ref = take(5)
    made, gown, gy, gx, sem = take(5)
    z, x, y = lax.axis_index("expert"), lax.axis_index("context"), lax.axis_index("dp")
    side = lax.div(x, 2)
    piece = c.FF // 8
    own_piece = pl.ds(pl.multiple_of(y * piece, 128), piece)
    loads = []
    for which in range(2):
        for index, (src, dst) in enumerate((
            (grad_in.at[side, which, :, own_piece], gown.at[which]),
            (gy_in.at[which], gy.at[which]),
            (gx_in.at[which], gx.at[which]),
        )):
            loads.append(pltpu.make_async_copy(src, dst, sem.at[3 * which + index]))
    loads.append(pltpu.make_async_copy(made_in, made, sem.at[6]))
    for load in loads:
        load.start()
    gtok_out[...] = gtok_in[...]
    if c.gather:
        core_cols = c.D // 2
        for m in range(4):
            for k in range(2):
                if m == 3:
                    gout_ref[:, k * core_cols : (k + 1) * core_cols] = whole_ref[m, k]
                else:
                    start = m * c.D + k * core_cols
                    gqkv_ref[:, start : start + core_cols] = whole_ref[m, k]
        src, dst = row_of((c.D, 128)), lane_of((c.D, 128))
        pick = jnp.logical_and(dst < c.sh, src == dst + (z * c.Y + y) * c.sh)
        pick = jnp.where(pick, 1.0, 0.0).astype(BF16)
        small = sum(mm(part, pick) for part in in_parts(small_ref[...], 3))
        gains_ref[...] = small[0:2, 0 : c.sh]
        biases_ref[...] = small[2:4, 0 : c.sh]
        grouter_ref[...] = small[LOGIT_LANE : LOGIT_LANE + c.E, 0 : c.sh]
    for which in range(2):
        for load in loads[3 * which : 3 * which + 3]:
            load.wait()
        total = gown[which].astype(F32) + gy[which].astype(F32) + gx[which].astype(F32)
        if which == 0:
            gin_ref[...] = total
        else:
            gdown_ref[...] = total.T
    loads[6].wait()
    for image in range(c.N):
        rows = slice(image * c.B, (image + 1) * c.B)
        meta = meta_ref[rows, :]
        slots = [meta[:, j : j + 1].astype(jnp.int32) for j in range(2)]
        at = lane_of((c.B, c.E * c.cap))
        gates = jnp.where(at == slots[0], meta[:, 4:5], 0.0)
        gates = gates + jnp.where(at == slots[1], meta[:, 5:6], 0.0)
        high, low = in_parts(gates, 2)
        rows_made = made[image].reshape(c.E * c.cap, c.D)
        mixture = mm(high, rows_made) + mm(low, rows_made)
        live = jnp.where(row_of((c.B, 1)) < len_ref[image, x], 1.0, 0.0)
        out_ref[rows, :] = (live * (hid_ref[rows, :] + mixture)).astype(BF16)


def run_back(c, tok, cot, lengths, weights, vec, q, kv, lse, att, hid, mix, meta, router, xback, gback, yloc, grads, gnext):
    shape = jax.ShapeDtypeStruct
    piece = c.FF // 8
    made = [
        shape((c.T, c.D), F32),
        shape((c.N, c.E, c.cap, c.D), BF16),
        shape((2, c.D, piece), BF16),
        shape((2, c.D, piece), BF16),
    ]
    dense_scratch = []
    if c.gather:
        half_cols = c.D // 2
        made += [shape((4, 2, c.sh, half_cols), F32), shape((c.r8, c.D), F32)]
        dense_scratch = [
            pltpu.VMEM((4, c.E, c.Y, c.sh, c.D), BF16),
            pltpu.VMEM((4, c.E, c.Y, c.sh, half_cols), BF16),
            pltpu.VMEM((4, 2, c.sh, half_cols), BF16),
            pltpu.VMEM((4, c.E, c.sh, half_cols), BF16),
            pltpu.VMEM((4, c.E, c.sh, half_cols), BF16),
            pltpu.VMEM((c.C, c.r8, c.D), F32),
            pltpu.VMEM((2, c.r8, c.D), F32),
            pltpu.VMEM((c.E, c.r8, c.D), F32),
        ]
    else:
        made += [shape((4, c.D, c.D), BF16), shape((c.r8, c.D), F32)]
    count = 5 * c.E + 64
    results = pl.pallas_call(
        functools.partial(back_kernel, c),
        out_shape=made,
        in_specs=[spec(pltpu.SMEM)] + [spec(pltpu.VMEM)] * 12 + [spec(pl.ANY)] * 5,
        out_specs=[spec(pl.ANY)] * 4 + [spec(pltpu.VMEM)] * 2,
        scratch_shapes=[
            pltpu.VMEM((4, c.D, c.D), BF16),
            pltpu.VMEM((c.N, c.S, 3 * c.D), BF16),
            pltpu.VMEM((c.T, c.D), F32),
            pltpu.VMEM((2, c.D, piece), BF16),
            pltpu.VMEM((2, c.D, piece), BF16),
            pltpu.VMEM((c.N, c.S, 2 * c.D), BF16),
            pltpu.VMEM((c.N, 2, c.B, 2 * c.D), BF16),
            pltpu.VMEM((c.N, c.B, 2 * c.D), BF16),
            pltpu.VMEM((c.T, 3 * c.D), BF16),
            pltpu.VMEM((c.T, c.D), BF16),
            pltpu.VMEM((c.T, c.D), F32),
            pltpu.VMEM((c.D, c.T), BF16),
            pltpu.VMEM((c.D, c.N * c.S), BF16),
            pltpu.VMEM((128, c.D), F32),
            *dense_scratch,
            pltpu.SemaphoreType.DMA((8,)),
            pltpu.SemaphoreType.DMA((count,)),
            pltpu.SemaphoreType.DMA((count,)),
        ],
        compiler_params=pltpu.CompilerParams(
            collective_id=2, has_side_effects=True, vmem_limit_bytes=VMEM_LIMIT
        ),
        name="back",
    )(lengths, tok, cot, vec, q, lse, att, hid, mix, meta, router, xback, gback, weights, kv, yloc, grads, gnext)
    g_tok, made_home, gy, gx, dense, small = results
    last = [shape((c.T, c.D), BF16), shape((c.T, c.D), F32)]
    last += [shape((c.D, piece), F32), shape((piece, c.D), F32)]
    if c.gather:
        last += [shape((c.sh, 3 * c.D), F32), shape((c.sh, c.D), F32)]
        last += [shape((2, c.sh), F32), shape((2, c.sh), F32), shape((c.E, c.sh), F32)]
    more = (dense, small) if c.gather else ()
    results = pl.pallas_call(
        functools.partial(last_kernel, c),
        out_shape=last,
        in_specs=[spec(pltpu.SMEM)]
        + [spec(pltpu.VMEM)] * 3
        + [spec(pl.ANY)] * 4
        + [spec(pltpu.VMEM)] * len(more),
        out_specs=[spec(pltpu.VMEM)] * len(last),
        scratch_shapes=[
            pltpu.VMEM((c.N, c.E, c.cap, c.D), BF16),
            pltpu.VMEM((2, c.D, piece), BF16),
            pltpu.VMEM((2, c.D, piece), BF16),
            pltpu.VMEM((2, c.D, piece), BF16),
            pltpu.SemaphoreType.DMA((7,)),
        ],
        compiler_params=pltpu.CompilerParams(vmem_limit_bytes=VMEM_LIMIT),
        name="last",
    )(lengths, hid, meta, g_tok, made_home, grads, gy, gx, *more)
    out, g_tok, g_in, g_down = results[:4]
    if c.gather:
        g_qkv, g_out, g_gains, g_biases, g_router = results[4:]
    else:
        both = ("expert", "dp")
        flat = dense.astype(F32).transpose(1, 0, 2).reshape(c.D, 4 * c.D)
        flat = lax.psum_scatter(flat, both, scatter_dimension=0, tiled=True)
        small = lax.psum_scatter(small, both, scatter_dimension=1, tiled=True)
        flat, small = lax.psum((flat, small), "context")
        g_qkv, g_out = flat[:, : 3 * c.D], flat[:, 3 * c.D :]
        g_gains, g_biases = small[0:2], small[2:4]
        g_router = small[LOGIT_LANE : LOGIT_LANE + c.E]
    rows = (c.N, c.B, c.D)
    return (
        out.reshape(rows),
        g_tok.reshape(rows),
        g_qkv,
        g_out,
        g_router.T,
        g_gains,
        g_biases,
        g_in[None],
        g_down[None],
    )


def pack_small(c, w_router, norm_gains, norm_biases):
    rows = jnp.concatenate([norm_gains, norm_biases, w_router.T], axis=0).astype(F32)
    return jnp.pad(rows, ((0, c.r8 - rows.shape[0]), (0, 128 - rows.shape[1])))


def per_device(
    mesh_shape,
    tokens,
    lengths,
    route_ids,
    keep_mask,
    w_qkv,
    w_attn_out,
    w_router,
    norm_gains,
    norm_biases,
    w_expert_in,
    w_expert_down,
    cotangent,
):
    images, block, width = tokens.shape
    experts = mesh_shape["expert"] * w_expert_in.shape[0]
    c = types.SimpleNamespace(
        E=experts,
        Y=mesh_shape["dp"],
        C=mesh_shape["context"],
        N=images,
        B=block,
        D=width,
        T=images * block,
        S=mesh_shape["context"] * block,
        FF=w_expert_in.shape[2],
        FB=512,
        cap=max(2, 16 * block // (5 * experts)),
        sh=w_qkv.shape[0],
        r8=-(-(LOGIT_LANE + experts) // 8) * 8,
        scale=(width // HEADS) ** -0.5,
        chunks=4,
    )
    c.gather = c.sh % 32 == 0
    tok = tokens.reshape(c.T, width)
    cot = cotangent.reshape(c.T, width)
    route = route_ids.transpose(0, 2, 1)
    keep = keep_mask.transpose(0, 2, 1)
    both = ("expert", "dp")
    if c.gather:
        given = (w_qkv, w_attn_out, pack_small(c, w_router, norm_gains, norm_biases))
    else:
        qkv = lax.all_gather(w_qkv, both, axis=0, tiled=True)
        out = lax.all_gather(w_attn_out, both, axis=0, tiled=True)
        small = pack_small(c, w_router, norm_gains, norm_biases)[:, : c.sh]
        vec = lax.all_gather(small, both, axis=1, tiled=True)
        stacked = jnp.concatenate([qkv, out], axis=1).reshape(width, 4, width).transpose(1, 0, 2)
        given = (stacked, vec)
    front = run_front(c, lengths, tok, route, keep, cot, given)
    weights, vec, q, kv, lse, att, hid, mix, meta, router, send, gsend, dyarr = front
    back = run_experts(c, send, gsend, dyarr, w_expert_in[0], w_expert_down[0])
    return run_back(
        c, tok, cot, lengths, weights, vec, q, kv, lse, att, hid, mix, meta, router, *back
    )


def solution(mesh):
    rows = P(("expert", "dp"), "context", None)
    shard = P(("expert", "dp"), None)
    column = P(None, ("expert", "dp"))
    expert = P("expert", None, None)
    return jax.shard_map(
        functools.partial(per_device, dict(mesh.shape)),
        mesh=mesh,
        in_specs=(rows, shard, rows, rows, shard, shard, shard, column, column, expert, expert, rows),
        out_specs=(
            rows,
            rows,
            shard,
            shard,
            shard,
            column,
            column,
            P("expert", None, ("context", "dp")),
            P("expert", ("context", "dp"), None),
        ),
        check_vma=False,
    )
```

```python
import functools
import itertools
import types

import jax
import jax.numpy as jnp
from jax import lax
from jax.experimental import pallas as pl
from jax.experimental.pallas import tpu as pltpu
from jax.sharding import PartitionSpec as P

HEADS = 12
EPS = 1e-06
F32 = jnp.float32
BF16 = jnp.bfloat16
MESH = pl.DeviceIdType.MESH
NN = (((1,), (0,)), ((), ()))
NT = (((1,), (1,)), ((), ()))
TN = (((0,), (0,)), ((), ()))
VMEM_LIMIT = 60 * 2**20
LOGIT_LANE = 4


def mm(left, right, dims=NN):
    return lax.dot_general(left, right, dims, preferred_element_type=F32)


def lane_of(shape):
    return lax.broadcasted_iota(jnp.int32, shape, 1)


def row_of(shape):
    return lax.broadcasted_iota(jnp.int32, shape, 0)


class Links:
    def __init__(self, send, recv):
        self.send, self.recv, self.ids = send, recv, itertools.count()

    def new(self):
        return next(self.ids)

    def make(self, at, src, dst, device):
        return pltpu.make_async_remote_copy(
            src_ref=src,
            dst_ref=dst,
            send_sem=self.send.at[at],
            recv_sem=self.recv.at[at],
            device_id=device,
            device_id_type=MESH,
        )


def greet(devices):
    barrier = pltpu.get_barrier_semaphore()
    for device in devices:
        pl.semaphore_signal(barrier, inc=1, device_id=device, device_id_type=MESH)
    pl.semaphore_wait(barrier, len(devices))


def normalize(values):
    centred = values - jnp.mean(values, axis=-1, keepdims=True)
    inverse = lax.rsqrt(jnp.mean(centred * centred, axis=-1, keepdims=True) + EPS)
    return centred * inverse, inverse


def normalize_back(grad_out, unit_rows, inverse, gain):
    scaled = grad_out * gain
    centre_term = jnp.mean(scaled, axis=-1, keepdims=True)
    slope_term = jnp.mean(scaled * unit_rows, axis=-1, keepdims=True)
    return inverse * (scaled - centre_term - unit_rows * slope_term)


def to_column(row):
    size = row.shape[1]
    eye = row_of((size, size)) == lane_of((size, size))
    return jnp.sum(jnp.where(eye, row, 0.0), axis=1, keepdims=True)


def to_row(column):
    size = column.shape[0]
    eye = row_of((size, size)) == lane_of((size, size))
    return jnp.sum(jnp.where(eye, column, 0.0), axis=0, keepdims=True)


def key_bias(c, len_ref, image):
    at = row_of((c.S, 1))
    bias = jnp.full((c.S, 1), -1e30, F32)
    for block in range(c.C):
        start = block * c.B
        inside = jnp.logical_and(at >= start, at < start + len_ref[image, block])
        bias = jnp.where(inside, 0.0, bias)
    return bias


def two_heads(pair):
    first = lane_of(pair.shape) < pair.shape[1] // 2
    zero = jnp.zeros_like(pair)
    return jnp.concatenate([jnp.where(first, pair, zero), jnp.where(first, zero, pair)], axis=0)


def one_pair(stacked):
    half = stacked.shape[0] // 2
    first = lane_of((half, stacked.shape[1])) < stacked.shape[1] // 2
    return jnp.where(first, stacked[:half], stacked[half:])


class Gather:
    def __init__(self, c, links, w_ref, rows_of, z, y, own_part, other_part):
        self.c, self.links, self.w_ref, self.rows_of = c, links, w_ref, rows_of
        self.z, self.y, self.own_part, self.other_part = z, y, own_part, other_part
        span = range(c.E)
        self.up = [links.new() for _ in span]
        self.down = [links.new() for _ in span]
        self.y_up = [links.new() for _ in span]
        self.y_down = [links.new() for _ in span]
        self.core_up = [[links.new() for _ in span] for _ in range(2)]
        self.core_down = [[links.new() for _ in span] for _ in range(2)]
        self.sent = []

    def route(self, above, below, y_dev, core_dev):
        self.above, self.below, self.y_dev, self.core_dev = above, below, y_dev, core_dev

    def unit(self, at, z_at, y_at, device, part=None):
        ref = self.w_ref.at[self.own_part if part is None else part, self.rows_of(z_at, y_at), :]
        return self.links.make(at, ref, ref, device)

    def send(self, condition, *where):
        pl.when(condition)(lambda: self.unit(*where).start())
        self.sent.append((condition, where))

    def got(self, condition, at, z_at, y_at, part=None):
        pl.when(condition)(lambda: self.unit(at, z_at, y_at, self.core_dev, part).wait_recv())

    def open(self):
        z, y = self.z, self.y
        self.send(z < self.c.E - 1, self.up[1], z, y, self.above)
        self.send(z > 0, self.down[1], z, y, self.below)
        self.send(z >= 0, self.y_up[0], z, y, self.y_dev)

    def pass_y(self, j):
        z, y = self.z, 1 - self.y
        lower, upper = z >= j, z + j <= self.c.E - 1
        self.got(lower, self.y_up[j], z - j, y)
        self.send(lower, self.core_up[1][j], z - j, y, self.core_dev)
        if j:
            self.got(upper, self.y_down[j], z + j, y)
            self.send(upper, self.core_down[1][j], z + j, y, self.core_dev)

    def step(self, j):
        z, y, last = self.z, self.y, self.c.E - 1
        if j <= last:
            lower, upper = z >= j, z + j <= last
            self.got(lower, self.up[j], z - j, y)
            if j < last:
                self.send(jnp.logical_and(lower, z < last), self.up[j + 1], z - j, y, self.above)
            self.send(lower, self.y_up[j], z - j, y, self.y_dev)
            self.send(lower, self.core_up[0][j], z - j, y, self.core_dev)
            self.got(upper, self.down[j], z + j, y)
            if j < last:
                self.send(jnp.logical_and(upper, z > 0), self.down[j + 1], z + j, y, self.below)
            self.send(upper, self.y_down[j], z + j, y, self.y_dev)
            self.send(upper, self.core_down[0][j], z + j, y, self.core_dev)
        self.pass_y(j - 1)

    def finish(self):
        z, last = self.z, self.c.E - 1
        for side in range(2):
            y = self.y if side == 0 else 1 - self.y
            if side:
                self.got(z >= 0, self.core_up[1][0], z, y, self.other_part)
            for j in range(1, self.c.E):
                self.got(z >= j, self.core_up[side][j], z - j, y, self.other_part)
                self.got(z + j <= last, self.core_down[side][j], z + j, y, self.other_part)

    def close(self):
        for condition, where in self.sent:
            pl.when(condition)(lambda: self.unit(*where).wait_send())


def front_kernel(c, *refs):
    refs = list(refs)
    take = lambda count: [refs.pop(0) for _ in range(count)]
    len_ref, tok_ref, route_ref, keep_ref, cot_ref = take(5)
    if c.gather:
        wqkv_ref, wout_ref, small_ref = take(3)
        w_hbm, vec_ref = take(2)
    else:
        w_ref, vec_ref = take(2)
    q_ref, kv_hbm, lse_ref, att_ref, hid_ref, mix_ref, meta_ref, router_ref = take(8)
    send_ref, gsend_ref, dyarr_ref = take(3)
    if c.gather:
        smalls, w_ref = take(2)
    kv_ref, dysend, lsem, ssem, rsem = take(5)
    if c.relay:
        dy_info, far_info, far_rows, dypack = take(4)
    links = Links(ssem, rsem)
    z, x, y = lax.axis_index("expert"), lax.axis_index("context"), lax.axis_index("dp")
    core = lax.rem(x, 2)
    shard = z * c.Y + y
    core_dev, far_dev, y_dev = (z, x ^ 1, y), (z, x ^ 2, y), (z, x, 1 - y)
    plane = [(lax.div(shard ^ k, c.Y), x, lax.rem(shard ^ k, c.Y)) for k in range(1, c.E * c.Y)]
    experts = [(z ^ k, x, y) for k in range(1, c.E)]
    greet([core_dev, far_dev] + (plane if c.gather else experts))
    ends = []

    def go(at, src, dst, device):
        copy = links.make(at, src, dst, device)
        copy.start()
        ends.append(copy)

    if c.gather:
        small_ids = [links.new() for _ in plane]
        smalls[shard] = small_ref[...]
        for at, device in zip(small_ids, plane):
            go(at, smalls.at[shard], smalls.at[shard], device)

        def rows_of(z_at, y_at):
            return pl.ds(pl.multiple_of((z_at * c.Y + y_at) * c.sh, 32), c.sh)

        own_rows = rows_of(z, y)
        for part in range(3):
            w_ref[part, own_rows, :] = wqkv_ref[:, part * c.D : (part + 1) * c.D]
        w_ref[3, own_rows, :] = wout_ref[...]

        above, below = (lax.rem(z + 1, c.E), x, y), (lax.rem(z + c.E - 1, c.E), x, y)
        stages = [Gather(c, links, w_ref, rows_of, z, y, *parts) for parts in (
            (1 + core, 2 - core), (3 * core, 3 - 3 * core))]
        for stage in stages:
            stage.route(above, below, y_dev, core_dev)
        stages[0].open()

    if c.relay:
        dy_info_id = links.new()
        dy_far_ids = [links.new() for _ in range(c.N)]
        dy_relay_ids = [links.new() for _ in range(c.N)]

    unit_rows = [None] * c.N
    choices = []
    for image in range(c.N):
        rows = slice(image * c.B, (image + 1) * c.B)
        live = jnp.where(row_of((c.B, 1)) < len_ref[image, x], 1.0, 0.0)
        kept = [to_column(keep_ref[image, j : j + 1, :].astype(F32)) * live for j in range(2)]
        first, second = [
            to_column(route_ref[image, j : j + 1, :].astype(F32)).astype(jnp.int32) for j in range(2)
        ]
        lane = lane_of((c.B, 128))
        named = jnp.where(lane == first, kept[0], 0.0) + jnp.where(
            lane == second, kept[1], 0.0
        )
        earlier = jnp.where(lane_of((c.B, c.B)) < row_of((c.B, c.B)), 1.0, 0.0).astype(BF16)
        rank = mm(earlier, named.astype(BF16))
        rank_first = jnp.sum(jnp.where(lane == first, rank, 0.0), axis=1, keepdims=True)
        rank_second = jnp.sum(jnp.where(lane == second, rank, 0.0), axis=1, keepdims=True)
        slot_first = first * c.cap + rank_first.astype(jnp.int32)
        slot_second = second * c.cap + rank_second.astype(jnp.int32)
        at = lane_of((c.B, c.E * c.cap))
        place = jnp.where(at == slot_first, kept[0], 0.0) + jnp.where(
            at == slot_second, kept[1], 0.0
        )
        place = place.astype(BF16)
        choices.append((first, second, kept, slot_first, slot_second, place))
        if c.relay:
            info = [to_row(column) for column in (slot_first.astype(F32), slot_second.astype(F32), *kept)]
            dy_info[image] = jnp.concatenate(info + [jnp.zeros((4, c.B), F32)], axis=0)
        dysend[image] = mm(place, cot_ref[rows, :], TN).astype(BF16).reshape(c.E, c.cap, c.D)

    if c.gather:
        for at, device in zip(small_ids, plane):
            other = lax.div(shard, 1)
            links.make(at, smalls.at[other], smalls.at[other], device).wait_recv()
        wide = jnp.concatenate([smalls[k] for k in range(c.E * c.Y)], axis=1).astype(BF16)
        span = c.E * c.Y * 128
        src, dst = row_of((span, c.D)), lane_of((span, c.D))
        inside = lax.rem(src, 128)
        pick = jnp.logical_and(inside < c.sh, lax.div(src, 128) * c.sh + inside == dst)
        vec_ref[...] = mm(wide, jnp.where(pick, 1.0, 0.0).astype(BF16))
    vec = vec_ref[...]
    own_at = pl.ds(pl.multiple_of(x * c.B, 32), c.B)
    norm_ids = [[links.new() for _ in range(3)] for _ in range(c.N)]
    for image in range(c.N):
        rows = slice(image * c.B, (image + 1) * c.B)
        unit_one, _ = normalize(tok_ref[rows, :].astype(F32))
        kv_ref[image, own_at, 2 * c.D : 3 * c.D] = (unit_one * vec[0:1] + vec[2:3]).astype(BF16)
        block = kv_ref.at[image, own_at, 2 * c.D : 3 * c.D]
        go(norm_ids[image][0], block, block, far_dev)
        go(norm_ids[image][1], block, block, core_dev)

    if c.gather:
        stages[0].step(1)
        stages[1].open()
        for j in range(2, c.E + 1):
            stages[0].step(j)
        stages[0].finish()

    normed = jnp.concatenate(
        [kv_ref[image, own_at, 2 * c.D : 3 * c.D] for image in range(c.N)], axis=0
    )
    kv_ids = [[links.new() for _ in range(3)] for _ in range(c.N)]
    keys = mm(normed, w_ref[1]).astype(BF16)
    values = mm(normed, w_ref[2]).astype(BF16)
    for image in range(c.N):
        rows = slice(image * c.B, (image + 1) * c.B)
        kv_ref[image, own_at, 0 : c.D] = keys[rows]
        kv_ref[image, own_at, c.D : 2 * c.D] = values[rows]
        block = kv_ref.at[image, own_at, 0 : 2 * c.D]
        go(kv_ids[image][0], block, block, far_dev)
        go(kv_ids[image][1], block, block, core_dev)
    if c.gather:
        for j in range(1, c.E + 1):
            stages[1].step(j)
    dy_ids = [links.new() for _ in experts]
    for k, (at, device) in enumerate(zip(dy_ids, experts), 1):
        if k == 1 or not c.relay:
            go(at, dysend.at[:, z ^ k], dyarr_ref.at[z], device)
    own_dy = pltpu.make_async_copy(dysend.at[:, z], dyarr_ref.at[z], lsem.at[0])
    own_dy.start()
    if c.relay:
        go(dy_info_id, dy_info, far_info, experts[1])

    def dy_to_far(image):
        rows = pl.ds(image * c.B, c.B)
        go(dy_far_ids[image], cot_ref.at[rows, :], far_rows.at[image], experts[1])

    def dy_pass_on(image):
        if image == 0:
            links.make(dy_info_id, far_info, far_info, experts[1]).wait_recv()
        here = far_rows.at[image]
        links.make(dy_far_ids[image], here, here, experts[1]).wait_recv()
        info = far_info[image]
        at = row_of((c.cap, c.B)).astype(F32)
        for index in range(2):
            first = ((z ^ index) * c.cap).astype(F32)
            kept = jnp.where(at == info[0:1] - first, info[2:3], 0.0)
            kept = kept + jnp.where(at == info[1:2] - first, info[3:4], 0.0)
            dypack[index, image] = mm(kept.astype(BF16), far_rows[image]).astype(BF16)
        go(dy_relay_ids[image], dypack.at[1, image], dyarr_ref.at[z ^ 2, image], experts[0])
        leaving.append(
            pltpu.make_async_copy(
                dypack.at[0, image], dyarr_ref.at[z ^ 2, image], lsem.at[2 + c.N + image]
            )
        )
        leaving[-1].start()

    leaving = [own_dy]
    if c.relay:
        dy_to_far(0)
    if c.gather:
        stages[1].finish()
        leaving.append(pltpu.make_async_copy(w_ref, w_hbm, lsem.at[1]))
        leaving[-1].start()
    q_ref[...] = mm(normed, w_ref[0]).astype(BF16)

    def block_of(image, who, first=0, last=2):
        rows_at = pl.ds(pl.multiple_of(who * c.B, 32), c.B)
        return kv_ref.at[image, rows_at, first * c.D : last * c.D]

    for image in range(c.N):
        far_block = block_of(image, x ^ 2, 2, 3)
        links.make(norm_ids[image][0], far_block, far_block, far_dev).wait_recv()
        go(norm_ids[image][2], far_block, far_block, core_dev)

    for image in range(c.N):
        rows = pl.ds(image * c.B, c.B)
        far_block = block_of(image, x ^ 2)
        links.make(kv_ids[image][0], far_block, far_block, far_dev).wait_recv()
        go(kv_ids[image][2], far_block, far_block, core_dev)
        near_block = block_of(image, x ^ 1)
        links.make(kv_ids[image][1], near_block, near_block, core_dev).wait_recv()
        cross_block = block_of(image, x ^ 3)
        links.make(kv_ids[image][2], cross_block, cross_block, core_dev).wait_recv()
        for at, who in ((1, x ^ 1), (2, x ^ 3)):
            there = block_of(image, who, 2, 3)
            links.make(norm_ids[image][at], there, there, core_dev).wait_recv()
        leaving.append(pltpu.make_async_copy(kv_ref.at[image], kv_hbm.at[image], lsem.at[2 + image]))
        leaving[-1].start()
        if c.relay and image == 0:
            dy_to_far(1)
        bias = key_bias(c, len_ref, image)

        def pair_step(pair, carry):
            lanes = pl.ds(pl.multiple_of(pair * 128, 128), 128)
            value_lanes = pl.ds(pl.multiple_of(c.D + pair * 128, 128), 128)
            queries = two_heads(q_ref[rows, lanes]) * jnp.asarray(c.scale, BF16)
            scores = mm(kv_ref[image, :, lanes], queries, NT) + bias
            top = jnp.max(scores, axis=0, keepdims=True)
            exponent = jnp.exp(scores - top)
            total = jnp.sum(exponent, axis=0, keepdims=True)
            probs = (exponent * (1.0 / total)).astype(BF16)
            lse_ref[image, pair] = jnp.broadcast_to(top + jnp.log(total), (8, 2 * c.B))
            mixed_values = mm(kv_ref[image, :, value_lanes].T, probs)
            att_ref[rows, lanes] = one_pair(mixed_values.T).astype(BF16)
            return carry

        lax.fori_loop(0, c.D // 128, pair_step, 0)
        if c.relay:
            dy_pass_on(image)

    branch = mm(att_ref[...], w_ref[3])
    hidden = tok_ref[...].astype(F32) + branch
    hid_ref[...] = hidden
    unit_two, _ = normalize(hidden)
    mixed = (unit_two * vec[1:2] + vec[3:4]).astype(BF16)
    mix_ref[...] = mixed
    pad = jnp.zeros((128 - c.r8, c.D), BF16)
    logits = mm(mixed, jnp.concatenate([vec.astype(BF16), pad], axis=0), NT)
    lane = lane_of((c.N * c.B, 128))
    valid = jnp.logical_and(lane >= LOGIT_LANE, lane < LOGIT_LANE + c.E)
    logits = jnp.where(valid, logits, -1e30)
    weight = jnp.exp(logits - jnp.max(logits, axis=1, keepdims=True))
    router = weight / jnp.sum(weight, axis=1, keepdims=True)
    router_ref[...] = router
    gsend_ref[...] = jnp.zeros_like(gsend_ref)
    lane = lane_of((c.B, 128))
    for image in range(c.N):
        rows = slice(image * c.B, (image + 1) * c.B)
        first, second, kept, slot_first, slot_second, place = choices[image]
        here = router[rows]
        gate_first = kept[0] * jnp.sum(
            jnp.where(lane == LOGIT_LANE + first, here, 0.0), axis=1, keepdims=True
        )
        gate_second = kept[1] * jnp.sum(
            jnp.where(lane == LOGIT_LANE + second, here, 0.0), axis=1, keepdims=True
        )
        send_ref[image] = mm(place, mixed[rows], TN).astype(BF16).reshape(c.E, c.cap, c.D)
        at = lane_of((c.B, c.cap))
        for expert in range(c.E):
            gates = jnp.where(at == slot_first - expert * c.cap, gate_first, 0.0)
            gates = gates + jnp.where(at == slot_second - expert * c.cap, gate_second, 0.0)
            gsend_ref[expert, image : image + 1, :] = jnp.sum(gates, axis=0, keepdims=True)
        columns = (
            slot_first.astype(F32),
            slot_second.astype(F32),
            kept[0],
            kept[1],
            gate_first,
            gate_second,
            first.astype(F32),
            second.astype(F32),
        )
        meta = jnp.zeros((c.B, 128), F32)
        for index, column in enumerate(columns):
            meta = jnp.where(lane == index, column, meta)
        meta_ref[rows, :] = meta

    for k, (at, device) in enumerate(zip(dy_ids, experts), 1):
        if k == 1 or not c.relay:
            links.make(at, dyarr_ref.at[z ^ k], dyarr_ref.at[z ^ k], device).wait_recv()
    if c.relay:
        for image in range(c.N):
            there = dyarr_ref.at[z ^ 3, image]
            links.make(dy_relay_ids[image], there, there, experts[0]).wait_recv()
    for copy in leaving:
        copy.wait()
    for copy in ends:
        copy.wait_send()
    if c.gather:
        for stage in stages:
            stage.close()


def spec(space):
    return pl.BlockSpec(memory_space=space)


def run_front(c, lengths, tok, route, keep, cot, weights):
    shape = jax.ShapeDtypeStruct
    made = [shape((4, c.D, c.D), BF16), shape((c.r8, c.D), F32)] if c.gather else []
    made += [
        shape((c.T, c.D), BF16),
        shape((c.N, c.S, 3 * c.D), BF16),
        shape((c.N, c.D // 128, 8, 2 * c.B), F32),
        shape((c.T, c.D), BF16),
        shape((c.T, c.D), F32),
        shape((c.T, c.D), BF16),
        shape((c.T, 128), F32),
        shape((c.T, 128), F32),
        shape((c.N, c.E, c.cap, c.D), BF16),
        shape((c.E, 8, c.cap), F32),
        shape((c.E, c.N, c.cap, c.D), BF16),
    ]
    count = 112 if c.gather else 2 * c.E + 32
    places = [spec(pltpu.VMEM)] * len(made)
    places[-1] = places[-10] = spec(pl.ANY)
    gather_scratch = []
    if c.gather:
        places[0] = spec(pl.ANY)
        gather_scratch = [
            pltpu.VMEM((c.E * c.Y, c.r8, 128), F32),
            pltpu.VMEM((4, c.D, c.D), BF16),
        ]
    relay_scratch = []
    if c.relay:
        relay_scratch = [
            pltpu.VMEM((c.N, 8, c.B), F32),
            pltpu.VMEM((c.N, 8, c.B), F32),
            pltpu.VMEM((c.N, c.B, c.D), BF16),
            pltpu.VMEM((2, c.N, c.cap, c.D), BF16),
        ]
    out = pl.pallas_call(
        functools.partial(front_kernel, c),
        out_shape=made,
        in_specs=[spec(pltpu.SMEM)] + [spec(pltpu.VMEM)] * (4 + len(weights)),
        out_specs=places,
        scratch_shapes=gather_scratch
        + [
            pltpu.VMEM((c.N, c.S, 3 * c.D), BF16),
            pltpu.VMEM((c.N, c.E, c.cap, c.D), BF16),
            pltpu.SemaphoreType.DMA((2 + 2 * c.N,)),
            pltpu.SemaphoreType.DMA((count,)),
            pltpu.SemaphoreType.DMA((count,)),
        ]
        + relay_scratch,
        compiler_params=pltpu.CompilerParams(
            collective_id=0, has_side_effects=True, vmem_limit_bytes=VMEM_LIMIT
        ),
        name="front",
    )(lengths, tok, route, keep, cot, *weights)
    return out if c.gather else list(weights) + list(out)


def gelu_both(pre):
    inner = 0.7978845608028654 * (pre + 0.044715 * pre * pre * pre)
    bend = jnp.tanh(inner)
    half = 0.5 * (1.0 + bend)
    slope = 0.7978845608028654 * (1.0 + 0.134145 * pre * pre)
    return pre * half, half + 0.5 * pre * (1.0 - bend * bend) * slope


def expert_kernel(
    c,
    send_ref,
    gsend_ref,
    dyarr_ref,
    win_hbm,
    wdown_hbm,
    xback_ref,
    gback_ref,
    yloc_ref,
    grad_hbm,
    gnext_hbm,
    win,
    wdown,
    arr,
    garr,
    act_all,
    dpre_all,
    dout_all,
    dxs,
    dgs,
    turned,
    gsend,
    grecv,
    gown,
    wsem,
    ssem,
    rsem,
):
    links = Links(ssem, rsem)
    z, x, y = lax.axis_index("expert"), lax.axis_index("context"), lax.axis_index("dp")
    experts = [(z ^ k, x, y) for k in range(1, c.E)]
    load_in = pltpu.make_async_copy(win_hbm, win, wsem.at[0])
    load_down = pltpu.make_async_copy(wdown_hbm, wdown, wsem.at[1])
    load_in.start()
    load_down.start()
    greet(experts + [(z, x ^ 1, y), (z, x ^ 2, y), (z, x, 1 - y)])
    ids = [[links.new() for _ in range(4)] for _ in range(c.E)]
    ends = []

    def go(at, src, dst, device):
        copy = links.make(at, src, dst, device)
        copy.start()
        ends.append(copy)

    group = c.E // c.chunks
    height = group * c.N * c.cap

    def dispatch(g):
        started = len(ends)
        for k in range(max(1, g * group), (g + 1) * group):
            go(ids[k][1], gsend_ref.at[z ^ k], garr.at[z], experts[k - 1])
            go(ids[k][0], send_ref.at[:, z ^ k], arr.at[z], experts[k - 1])
        return ends[started:]

    dispatch(0)
    early = dispatch(c.chunks - 2)
    for g in range(1, c.chunks - 2):
        dispatch(g)
    for image in range(c.N):
        arr[z, image] = send_ref[image, z]
    garr[z] = gsend_ref[z]
    load_in.wait()
    load_down.wait()
    dgs[...] = jnp.zeros_like(dgs)
    for g in range(c.chunks):
        if g == 1:
            for copy in early:
                copy.wait_send()
            ends[:] = [copy for copy in ends if all(copy is not other for other in early)]
            dispatch(c.chunks - 1)
        slab = lax.div(z, group) ^ g
        for k in range(g * group, (g + 1) * group):
            if k:
                there = z ^ k
                links.make(ids[k][0], arr.at[there], arr.at[there], experts[k - 1]).wait_recv()
                links.make(ids[k][1], garr.at[there], garr.at[there], experts[k - 1]).wait_recv()
        start = pl.multiple_of(slab * height, 32)
        rows = pl.ds(start, height)
        for member in range(group):
            source = slab * group + member
            for image in range(c.N):
                gates = to_column(garr[source, image : image + 1, :])
                offset = (member * c.N + image) * c.cap
                part = pl.ds(pl.multiple_of(start + offset, 16), c.cap)
                dout_all[part, :] = (gates * dyarr_ref[source, image].astype(F32)).astype(BF16)
        inputs = arr[pl.ds(slab * group, group)].reshape(height, c.D)
        douts = dout_all[rows, :]

        def ff_step(step, carry):
            lanes = pl.ds(pl.multiple_of(step * c.FB, 128), c.FB)
            pre = mm(inputs, win[:, lanes])
            act, slope = gelu_both(pre)
            act_all[rows, lanes] = act.astype(BF16)
            dact = mm(douts, wdown[lanes, :], NT)
            dpre_all[rows, lanes] = (dact * slope).astype(BF16)
            return carry

        lax.fori_loop(0, c.FF // c.FB, ff_step, 0)
        dx = mm(dpre_all[rows, :], win[...], NT).astype(BF16)
        dxs[pl.ds(slab * group, group)] = dx.reshape(group, c.N, c.cap, c.D)
        made = mm(act_all[rows, :], wdown[...]).astype(BF16)
        yloc_ref[pl.ds(slab * group, group)] = made.reshape(group, c.N, c.cap, c.D)
        for member in range(group):
            source = slab * group + member
            for image in range(c.N):
                offset = (member * c.N + image) * c.cap
                dots = made[offset : offset + c.cap].astype(F32) * dyarr_ref[source, image].astype(
                    F32
                )
                dgs[source, image : image + 1, :] = to_row(jnp.sum(dots, axis=1, keepdims=True))
        for k in range(g * group, (g + 1) * group):
            if k:
                there = z ^ k
                go(ids[k][2], dxs.at[there], xback_ref.at[:, z], experts[k - 1])
                go(ids[k][3], dgs.at[there], gback_ref.at[z], experts[k - 1])
    for image in range(c.N):
        xback_ref[image, z] = dxs[z, image]
    gback_ref[z] = dgs[z]

    total = c.E * c.N * c.cap
    turned[0] = arr[...].reshape(total, c.D).T
    turned[1] = dout_all[...].T

    core = lax.rem(x, 2)
    core_dev, far_dev, y_dev = (z, x ^ 1, y), (z, x ^ 2, y), (z, x, 1 - y)
    half = c.FF // 4
    grad_ids = [[links.new() for _ in range(2)] for _ in range(2)]
    sources = (dpre_all, act_all)

    def blocks(which, owner, into):
        def block_step(part, carry):
            lanes = pl.ds(pl.multiple_of((2 * part + owner) * half, 128), half)
            into[part, which] = mm(turned[which], sources[which][:, lanes]).astype(BF16)
            return carry

        lax.fori_loop(0, 2, block_step, 0)

    piece = half // 2
    side = lax.div(x, 2)
    other_piece = pl.ds(pl.multiple_of((1 - y) * piece, 128), piece)
    next_ids = [links.new() for _ in range(2)]
    leaving = []
    for which in range(2):
        blocks(which, 1 - core, gsend)
        for part in range(2):
            go(grad_ids[which][part], gsend.at[part, which], grecv.at[part, which], core_dev)
        blocks(which, core, gown)
        for part in range(2):
            there = grecv.at[part, which]
            links.make(grad_ids[which][part], there, there, core_dev).wait_recv()
            gown[part, which] = (
                gown[part, which].astype(F32) + grecv[part, which].astype(F32)
            ).astype(BF16)
        first = gown.at[1 - side, which, :, other_piece]
        go(next_ids[which], first, gnext_hbm.at[which], y_dev if which == 0 else far_dev)
        for part in range(2):
            leaving.append(
                pltpu.make_async_copy(
                    gown.at[part, which], grad_hbm.at[part, which], wsem.at[2 + 2 * which + part]
                )
            )
            leaving[-1].start()
    for which in range(2):
        there = gnext_hbm.at[which]
        links.make(next_ids[which], there, there, core_dev).wait_recv()
    for copy in leaving:
        copy.wait()
    for k in range(1, c.E):
        there = z ^ k
        links.make(ids[k][2], xback_ref.at[:, there], xback_ref.at[:, there], experts[k - 1]).wait_recv()
        links.make(ids[k][3], gback_ref.at[there], gback_ref.at[there], experts[k - 1]).wait_recv()
    for copy in ends:
        copy.wait_send()


def run_experts(c, send, gsend, dyarr, w_in, w_down):
    shape = jax.ShapeDtypeStruct
    total = c.E * c.N * c.cap
    count = 4 * c.E + 6
    return pl.pallas_call(
        functools.partial(expert_kernel, c),
        out_shape=[
            shape((c.N, c.E, c.cap, c.D), BF16),
            shape((c.E, 8, c.cap), F32),
            shape((c.E, c.N, c.cap, c.D), BF16),
            shape((2, 2, c.D, c.FF // 4), BF16),
            shape((2, c.D, c.FF // 8), BF16),
        ],
        in_specs=[spec(pltpu.VMEM)] * 3 + [spec(pl.ANY)] * 2,
        out_specs=[spec(pltpu.VMEM)] * 3 + [spec(pl.ANY)] * 2,
        scratch_shapes=[
            pltpu.VMEM((c.D, c.FF), BF16),
            pltpu.VMEM((c.FF, c.D), BF16),
            pltpu.VMEM((c.E, c.N, c.cap, c.D), BF16),
            pltpu.VMEM((c.E, 8, c.cap), F32),
            pltpu.VMEM((total, c.FF), BF16),
            pltpu.VMEM((total, c.FF), BF16),
            pltpu.VMEM((total, c.D), BF16),
            pltpu.VMEM((c.E, c.N, c.cap, c.D), BF16),
            pltpu.VMEM((c.E, 8, c.cap), F32),
            pltpu.VMEM((2, c.D, total), BF16),
            pltpu.VMEM((2, 2, c.D, c.FF // 4), BF16),
            pltpu.VMEM((2, 2, c.D, c.FF // 4), BF16),
            pltpu.VMEM((2, 2, c.D, c.FF // 4), BF16),
            pltpu.SemaphoreType.DMA((6,)),
            pltpu.SemaphoreType.DMA((count,)),
            pltpu.SemaphoreType.DMA((count,)),
        ],
        compiler_params=pltpu.CompilerParams(
            collective_id=1, has_side_effects=True, vmem_limit_bytes=VMEM_LIMIT
        ),
        name="experts",
    )(send, gsend, dyarr, w_in, w_down)


def in_parts(values, count):
    parts = []
    for _ in range(count):
        parts.append(values.astype(BF16))
        values = values - parts[-1].astype(F32)
    return parts


def back_kernel(c, *refs):
    refs = list(refs)
    take = lambda count: [refs.pop(0) for _ in range(count)]
    len_ref, tok_ref, cot_ref, vec_ref, q_ref, lse_ref, att_ref, hid_ref, mix_ref = take(9)
    meta_ref, router_ref, xback_ref, gback_ref = take(4)
    w_hbm, kv_hbm, yloc_hbm, grad_hbm, gnext_hbm = take(5)
    gtok_hbm, made, gy, gx = take(4)
    if c.gather:
        whole, gsmall_ref = take(2)
    else:
        dd, gsmall_ref = take(2)
    w_ref, kv_ref, gtok_ref, gpart, gnext = take(5)
    dkv, kvcore, kvfar, dproj, datt, dhid, norm_t, norm_all, router_sum = take(9)
    if c.gather:
        dd, dcore, done_x, done_y, done_z, small_four, small_y, small_z = take(8)
    lsem, ssem, rsem = take(3)
    links = Links(ssem, rsem)
    z, x, y = lax.axis_index("expert"), lax.axis_index("context"), lax.axis_index("dp")
    core, side = lax.rem(x, 2), lax.div(x, 2)
    core_dev, far_dev, y_dev = (z, x ^ 1, y), (z, x ^ 2, y), (z, x, 1 - y)
    experts = [(z ^ k, x, y) for k in range(1, c.E)]
    ends = []

    def go(at, src, dst, device):
        copy = links.make(at, src, dst, device)
        copy.start()
        ends.append(copy)

    def got(at, dst, device):
        links.make(at, dst, dst, device).wait_recv()

    half = c.FF // 4
    piece = half // 2
    loads = [
        pltpu.make_async_copy(w_hbm, w_ref, lsem.at[0]),
        pltpu.make_async_copy(kv_hbm, kv_ref, lsem.at[1]),
    ]
    own_piece = pl.ds(pl.multiple_of(y * piece, 128), piece)
    other_piece = pl.ds(pl.multiple_of((1 - y) * piece, 128), piece)
    parts = (grad_hbm.at[1 - side, 0, :, own_piece], grad_hbm.at[side, 1, :, other_piece])
    for which in range(2):
        loads.append(pltpu.make_async_copy(parts[which], gpart.at[which], lsem.at[2 + which]))
        loads.append(
            pltpu.make_async_copy(gnext_hbm.at[which], gnext.at[which], lsem.at[6 + which])
        )
    own_made = pltpu.make_async_copy(yloc_hbm.at[z], made.at[:, z], lsem.at[4])
    loads.append(own_made)
    for load in loads:
        load.start()
    cross_dev = [(z, x ^ 3, y)] if c.gather else []
    greet([core_dev, far_dev, y_dev] + experts + cross_dev)

    made_ids = [links.new() for _ in experts]
    for k, (at, device) in enumerate(zip(made_ids, experts), 1):
        go(at, yloc_hbm.at[z ^ k], made.at[:, z], device)
    gy_ids = [links.new() for _ in range(2)]
    gx_ids = [links.new() for _ in range(2)]
    go(gy_ids[0], grad_hbm.at[side, 0, :, other_piece], gy.at[0], y_dev)
    go(gx_ids[1], grad_hbm.at[1 - side, 1, :, own_piece], gx.at[1], far_dev)
    for which in range(2):
        loads[2 + 2 * which].wait()
        loads[3 + 2 * which].wait()
        gpart[which] = (gpart[which].astype(F32) + gnext[which].astype(F32)).astype(BF16)
        if which == 0:
            go(gx_ids[0], gpart.at[0], gx.at[0], far_dev)
        else:
            go(gy_ids[1], gpart.at[1], gy.at[1], y_dev)

    def grads_end():
        for which in range(2):
            got(gy_ids[which], gy.at[which], y_dev)
            got(gx_ids[which], gx.at[which], far_dev)

    if c.gather:
        n_dense = 4
        core_cols = c.D // 2
        keep_cols = pl.ds(pl.multiple_of(core * core_cols, 128), core_cols)
        give_cols = pl.ds(pl.multiple_of((1 - core) * core_cols, 128), core_cols)
        ids_core = [links.new() for _ in range(n_dense)]
        ids_x = [links.new() for _ in range(n_dense)]
        ids_y = [links.new() for _ in range(n_dense)]
        ids_z = [[links.new() for _ in experts] for _ in range(n_dense)]
        ids_own = [links.new() for _ in range(n_dense)]

        def dense_start(m, value):
            dd[m] = value.astype(BF16).reshape(c.E, c.Y, c.sh, c.D)
            go(ids_core[m], dd.at[m, :, :, :, give_cols], dcore.at[m], core_dev)

        def dense_y(m):
            got(ids_core[m], dcore.at[m], core_dev)
            dd[m, :, :, :, keep_cols] = (
                dd[m, :, :, :, keep_cols].astype(F32) + dcore[m].astype(F32)
            ).astype(BF16)
            go(ids_y[m], dd.at[m, :, 1 - y, :, keep_cols], done_y.at[m], y_dev)

        def dense_z(m):
            got(ids_y[m], done_y.at[m], y_dev)
            dd[m, :, y, :, keep_cols] = (
                dd[m, :, y, :, keep_cols].astype(F32) + done_y[m].astype(F32)
            ).astype(BF16)
            for k, device in enumerate(experts, 1):
                go(
                    ids_z[m][k - 1],
                    dd.at[m, z ^ k, y, :, keep_cols],
                    done_z.at[m, z],
                    device,
                )

        def dense_x(m):
            total = dd[m, z, y, :, keep_cols].astype(F32)
            for k, device in enumerate(experts, 1):
                got(ids_z[m][k - 1], done_z.at[m, z ^ k], device)
                total = total + done_z[m, z ^ k].astype(F32)
            done_x[m, 0] = total.astype(BF16)
            go(ids_x[m], done_x.at[m, 0], done_x.at[m, 1], far_dev)

        def dense_share(m):
            got(ids_x[m], done_x.at[m, 1], far_dev)
            whole[m, core] = done_x[m, 0].astype(F32) + done_x[m, 1].astype(F32)
            go(ids_own[m], whole.at[m, core], whole.at[m, core], core_dev)

        def dense_end(m):
            there = whole.at[m, 1 - core]
            got(ids_own[m], there, core_dev)

    else:

        def dense_start(m, value):
            dd[m] = value.astype(BF16)

    vec = vec_ref[...]
    lane = lane_of((c.B, 128))
    d_mixed, dy_rows = [], []
    d_logits = []
    for image in range(c.N):
        rows = slice(image * c.B, (image + 1) * c.B)
        meta = meta_ref[rows, :]
        slots = [meta[:, j : j + 1].astype(jnp.int32) for j in range(2)]
        kept = [meta[:, 2 + j : 3 + j] for j in range(2)]
        names = [meta[:, 6 + j : 7 + j].astype(jnp.int32) for j in range(2)]
        at = lane_of((c.B, c.E * c.cap))
        place = jnp.where(at == slots[0], kept[0], 0.0) + jnp.where(at == slots[1], kept[1], 0.0)
        copies = xback_ref[image].reshape(c.E * c.cap, c.D)
        d_mixed.append(mm(place.astype(BF16), copies))
        d_router = jnp.zeros((c.B, 128), F32)
        at = lane_of((c.B, c.cap))
        for j in range(2):
            d_gate = jnp.zeros((c.B, c.cap), F32)
            for expert in range(c.E):
                row = gback_ref[expert, image : image + 1, :]
                d_gate = d_gate + jnp.where(at == slots[j] - expert * c.cap, row, 0.0)
            d_gate = jnp.sum(d_gate, axis=1, keepdims=True) * kept[j]
            d_router = d_router + jnp.where(lane == LOGIT_LANE + names[j], d_gate, 0.0)
        router = router_ref[rows, :]
        dot = jnp.sum(router * d_router, axis=1, keepdims=True)
        d_logits.append(router * (d_router - dot))
        live = jnp.where(row_of((c.B, 1)) < len_ref[image, x], 1.0, 0.0)
        dy_rows.append(cot_ref[rows, :].astype(F32) * live)
    d_mixed = jnp.concatenate(d_mixed, axis=0)
    d_logits = jnp.concatenate(d_logits, axis=0)
    dy_rows = jnp.concatenate(dy_rows, axis=0)
    logit_rows = jnp.concatenate([vec, jnp.zeros((128 - c.r8, c.D), F32)], axis=0)
    lane_here = row_of((128, c.D))
    is_router = jnp.logical_and(lane_here >= LOGIT_LANE, lane_here < LOGIT_LANE + c.E)
    w_router = jnp.where(is_router, logit_rows, 0.0)
    high, low = in_parts(d_logits, 2)
    w_router = w_router.astype(BF16)
    d_mixed = d_mixed + mm(high, w_router) + mm(low, w_router)
    router_sum[...] = mm(high, mix_ref[...], TN) + mm(low, mix_ref[...], TN)
    unit_two, inverse_two = normalize(hid_ref[...])
    gains_two = jnp.sum(d_mixed * unit_two, axis=0, keepdims=True)
    biases_two = jnp.sum(d_mixed, axis=0, keepdims=True)
    d_hidden = dy_rows + normalize_back(d_mixed, unit_two, inverse_two, vec[1:2])
    dhid[...] = d_hidden
    d_branch = d_hidden.astype(BF16)
    dense_start(3, mm(att_ref[...], d_branch, TN))
    loads[0].wait()
    datt[...] = mm(d_branch, w_ref[3], NT).astype(BF16)
    unit_one, inverse_one = normalize(tok_ref[...].astype(F32))
    norm_t[...] = (unit_one * vec[0:1] + vec[2:3]).astype(BF16).T
    loads[1].wait()
    for image in range(c.N):
        norm_all[:, image * c.S : (image + 1) * c.S] = kv_ref[image, :, 2 * c.D : 3 * c.D].T

    kvcore_ids = [[links.new() for _ in range(2)] for _ in range(c.N)]
    kvfar_ids = [links.new() for _ in range(c.N)]

    def block_rows(who):
        return pl.ds(pl.multiple_of(who * c.B, 32), c.B)

    def attend_back(image, first_pair, last_pair):
        rows = pl.ds(image * c.B, c.B)
        bias = key_bias(c, len_ref, image)

        def pair_step(pair, carry):
            lanes = pl.ds(pl.multiple_of(pair * 128, 128), 128)
            value_lanes = pl.ds(pl.multiple_of(c.D + pair * 128, 128), 128)
            scale = jnp.asarray(c.scale, BF16)
            queries = two_heads(q_ref[rows, lanes]) * scale
            grads = two_heads(datt[rows, lanes])
            keys = kv_ref[image, :, lanes]
            probs = jnp.exp(mm(keys, queries, NT) + bias - lse_ref[image, pair][0:1])
            d_probs = mm(kv_ref[image, :, value_lanes], grads, NT)
            dot = jnp.sum(probs * d_probs, axis=0, keepdims=True)
            d_scores = (probs * (d_probs - dot)).astype(BF16)
            dkv[image, :, value_lanes] = mm(probs.astype(BF16), grads).astype(BF16)
            dkv[image, :, lanes] = mm(d_scores, queries).astype(BF16)
            d_queries = mm(keys.T, d_scores).T
            dproj[rows, lanes] = (one_pair(d_queries) * c.scale).astype(BF16)
            return carry

        lax.fori_loop(first_pair, last_pair, pair_step, 0)

    def kv_to_core(image):
        for s in range(2):
            block = dkv.at[image, block_rows(2 * s + 1 - core), :]
            go(kvcore_ids[image][s], block, kvcore.at[image, s], core_dev)

    def kv_to_far(image):
        for s in range(2):
            got(kvcore_ids[image][s], kvcore.at[image, s], core_dev)
        rows = block_rows(2 * (1 - side) + core)
        kvcore[image, 1 - side] = (
            dkv[image, rows, :].astype(F32) + kvcore[image, 1 - side].astype(F32)
        ).astype(BF16)
        go(kvfar_ids[image], kvcore.at[image, 1 - side], kvfar.at[image], far_dev)

    def kv_end(image):
        got(kvfar_ids[image], kvfar.at[image], far_dev)
        total = dkv[image, block_rows(2 * side + core), :].astype(F32)
        total = total + kvcore[image, side].astype(F32) + kvfar[image].astype(F32)
        rows = pl.ds(image * c.B, c.B)
        dproj[rows, c.D : 3 * c.D] = total.astype(BF16)

    pairs = c.D // 128
    attend_back(0, 0, pairs)
    kv_to_core(0)
    if c.gather:
        dense_y(3)
    attend_back(1, 0, pairs // 2)
    kv_to_far(0)
    attend_back(1, pairs // 2, pairs)
    kv_to_core(1)
    dense_start(0, mm(norm_t[...], dproj[:, 0 : c.D]))
    for m in (1, 2):
        columns = slice((m - 1) * c.D, m * c.D)
        dense_start(m, mm(norm_all[...], dkv[:, :, columns].reshape(c.N * c.S, c.D)))
    kv_to_far(1)
    if c.gather:
        dense_y(0)
        dense_y(1)
        dense_y(2)
        dense_z(3)
        kv_end(0)
        dense_z(0)
        dense_x(3)
        dense_z(1)
    else:
        kv_end(0)
    kv_end(1)
    d_normed = mm(dproj[:, 0 : c.D], w_ref[0], NT)
    d_normed = d_normed + mm(dproj[:, c.D : 2 * c.D], w_ref[1], NT)
    d_normed = d_normed + mm(dproj[:, 2 * c.D : 3 * c.D], w_ref[2], NT)
    unit_one, inverse_one = normalize(tok_ref[...].astype(F32))
    gains_one = jnp.sum(d_normed * unit_one, axis=0, keepdims=True)
    biases_one = jnp.sum(d_normed, axis=0, keepdims=True)
    small_here = jnp.concatenate([gains_one, gains_two, biases_one, biases_two], axis=0)
    small_here = jnp.concatenate(
        [small_here, router_sum[LOGIT_LANE : LOGIT_LANE + c.r8 - 4]], axis=0
    )
    if c.gather:
        small_ids = [links.new() for _ in range(3)]
        small_y_id = links.new()
        small_z_ids = [links.new() for _ in experts]
        small_four[x] = small_here
        for k, at in enumerate(small_ids, 1):
            go(at, small_four.at[x], small_four.at[x], (z, x ^ k, y))
    gtok_ref[...] = dhid[...] + normalize_back(d_normed, unit_one, inverse_one, vec[0:1])
    leave = pltpu.make_async_copy(gtok_ref, gtok_hbm, lsem.at[5])
    leave.start()
    if c.gather:

        dense_x(0)
        dense_share(3)
        dense_z(2)
        for k, at in enumerate(small_ids, 1):
            got(at, small_four.at[x ^ k], (z, x ^ k, y))
        small_y[0] = (small_four[0] + small_four[1]) + (small_four[2] + small_four[3])
        go(small_y_id, small_y.at[0], small_y.at[1], y_dev)
        dense_x(1)
        dense_share(0)
        got(small_y_id, small_y.at[1], y_dev)
        small_z[z] = small_y[0] + small_y[1]
        for at, device in zip(small_z_ids, experts):
            go(at, small_z.at[z], small_z.at[z], device)
        dense_end(3)
        dense_x(2)
        dense_share(1)
        dense_end(0)
        for k, (at, device) in enumerate(zip(small_z_ids, experts), 1):
            got(at, small_z.at[z ^ k], device)
        gsmall_ref[...] = sum((small_z[k] for k in range(1, c.E)), small_z[0])
        dense_share(2)
        dense_end(1)
        dense_end(2)
    else:
        gsmall_ref[...] = small_here
    for k, (at, device) in enumerate(zip(made_ids, experts), 1):
        got(at, made.at[:, z ^ k], device)
    grads_end()
    leave.wait()
    own_made.wait()
    for copy in ends:
        copy.wait_send()


def last_kernel(c, *refs):
    refs = list(refs)
    take = lambda count: [refs.pop(0) for _ in range(count)]
    len_ref, hid_ref, meta_ref, gtok_in, made_in, grad_in, gy_in, gx_in = take(8)
    if c.gather:
        whole_ref, small_ref = take(2)
    out_ref, gtok_out, gin_ref, gdown_ref = take(4)
    if c.gather:
        gqkv_ref, gout_ref, gains_ref, biases_ref, grouter_ref = take(5)
    made, gown, gy, gx, sem = take(5)
    z, x, y = lax.axis_index("expert"), lax.axis_index("context"), lax.axis_index("dp")
    side = lax.div(x, 2)
    piece = c.FF // 8
    own_piece = pl.ds(pl.multiple_of(y * piece, 128), piece)
    loads = []
    for which in range(2):
        for index, (src, dst) in enumerate((
            (grad_in.at[side, which, :, own_piece], gown.at[which]),
            (gy_in.at[which], gy.at[which]),
            (gx_in.at[which], gx.at[which]),
        )):
            loads.append(pltpu.make_async_copy(src, dst, sem.at[3 * which + index]))
    loads.append(pltpu.make_async_copy(made_in, made, sem.at[6]))
    for load in loads:
        load.start()
    gtok_out[...] = gtok_in[...]
    if c.gather:
        core_cols = c.D // 2
        for m in range(4):
            for k in range(2):
                if m == 3:
                    gout_ref[:, k * core_cols : (k + 1) * core_cols] = whole_ref[m, k]
                else:
                    start = m * c.D + k * core_cols
                    gqkv_ref[:, start : start + core_cols] = whole_ref[m, k]
        src, dst = row_of((c.D, 128)), lane_of((c.D, 128))
        pick = jnp.logical_and(dst < c.sh, src == dst + (z * c.Y + y) * c.sh)
        pick = jnp.where(pick, 1.0, 0.0).astype(BF16)
        small = sum(mm(part, pick) for part in in_parts(small_ref[...], 3))
        gains_ref[...] = small[0:2, 0 : c.sh]
        biases_ref[...] = small[2:4, 0 : c.sh]
        grouter_ref[...] = small[LOGIT_LANE : LOGIT_LANE + c.E, 0 : c.sh]
    for which in range(2):
        for load in loads[3 * which : 3 * which + 3]:
            load.wait()
        total = gown[which].astype(F32) + gy[which].astype(F32) + gx[which].astype(F32)
        if which == 0:
            gin_ref[...] = total
        else:
            gdown_ref[...] = total.T
    loads[6].wait()
    for image in range(c.N):
        rows = slice(image * c.B, (image + 1) * c.B)
        meta = meta_ref[rows, :]
        slots = [meta[:, j : j + 1].astype(jnp.int32) for j in range(2)]
        at = lane_of((c.B, c.E * c.cap))
        gates = jnp.where(at == slots[0], meta[:, 4:5], 0.0)
        gates = gates + jnp.where(at == slots[1], meta[:, 5:6], 0.0)
        high, low = in_parts(gates, 2)
        rows_made = made[image].reshape(c.E * c.cap, c.D)
        mixture = mm(high, rows_made) + mm(low, rows_made)
        live = jnp.where(row_of((c.B, 1)) < len_ref[image, x], 1.0, 0.0)
        out_ref[rows, :] = (live * (hid_ref[rows, :] + mixture)).astype(BF16)


def run_back(c, tok, cot, lengths, weights, vec, q, kv, lse, att, hid, mix, meta, router, xback, gback, yloc, grads, gnext):
    shape = jax.ShapeDtypeStruct
    piece = c.FF // 8
    made = [
        shape((c.T, c.D), F32),
        shape((c.N, c.E, c.cap, c.D), BF16),
        shape((2, c.D, piece), BF16),
        shape((2, c.D, piece), BF16),
    ]
    dense_scratch = []
    if c.gather:
        half_cols = c.D // 2
        made += [shape((4, 2, c.sh, half_cols), F32), shape((c.r8, c.D), F32)]
        dense_scratch = [
            pltpu.VMEM((4, c.E, c.Y, c.sh, c.D), BF16),
            pltpu.VMEM((4, c.E, c.Y, c.sh, half_cols), BF16),
            pltpu.VMEM((4, 2, c.sh, half_cols), BF16),
            pltpu.VMEM((4, c.E, c.sh, half_cols), BF16),
            pltpu.VMEM((4, c.E, c.sh, half_cols), BF16),
            pltpu.VMEM((c.C, c.r8, c.D), F32),
            pltpu.VMEM((2, c.r8, c.D), F32),
            pltpu.VMEM((c.E, c.r8, c.D), F32),
        ]
    else:
        made += [shape((4, c.D, c.D), BF16), shape((c.r8, c.D), F32)]
    count = 5 * c.E + 64
    results = pl.pallas_call(
        functools.partial(back_kernel, c),
        out_shape=made,
        in_specs=[spec(pltpu.SMEM)] + [spec(pltpu.VMEM)] * 12 + [spec(pl.ANY)] * 5,
        out_specs=[spec(pl.ANY)] * 4 + [spec(pltpu.VMEM)] * 2,
        scratch_shapes=[
            pltpu.VMEM((4, c.D, c.D), BF16),
            pltpu.VMEM((c.N, c.S, 3 * c.D), BF16),
            pltpu.VMEM((c.T, c.D), F32),
            pltpu.VMEM((2, c.D, piece), BF16),
            pltpu.VMEM((2, c.D, piece), BF16),
            pltpu.VMEM((c.N, c.S, 2 * c.D), BF16),
            pltpu.VMEM((c.N, 2, c.B, 2 * c.D), BF16),
            pltpu.VMEM((c.N, c.B, 2 * c.D), BF16),
            pltpu.VMEM((c.T, 3 * c.D), BF16),
            pltpu.VMEM((c.T, c.D), BF16),
            pltpu.VMEM((c.T, c.D), F32),
            pltpu.VMEM((c.D, c.T), BF16),
            pltpu.VMEM((c.D, c.N * c.S), BF16),
            pltpu.VMEM((128, c.D), F32),
            *dense_scratch,
            pltpu.SemaphoreType.DMA((8,)),
            pltpu.SemaphoreType.DMA((count,)),
            pltpu.SemaphoreType.DMA((count,)),
        ],
        compiler_params=pltpu.CompilerParams(
            collective_id=2, has_side_effects=True, vmem_limit_bytes=VMEM_LIMIT
        ),
        name="back",
    )(lengths, tok, cot, vec, q, lse, att, hid, mix, meta, router, xback, gback, weights, kv, yloc, grads, gnext)
    g_tok, made_home, gy, gx, dense, small = results
    last = [shape((c.T, c.D), BF16), shape((c.T, c.D), F32)]
    last += [shape((c.D, piece), F32), shape((piece, c.D), F32)]
    if c.gather:
        last += [shape((c.sh, 3 * c.D), F32), shape((c.sh, c.D), F32)]
        last += [shape((2, c.sh), F32), shape((2, c.sh), F32), shape((c.E, c.sh), F32)]
    more = (dense, small) if c.gather else ()
    results = pl.pallas_call(
        functools.partial(last_kernel, c),
        out_shape=last,
        in_specs=[spec(pltpu.SMEM)]
        + [spec(pltpu.VMEM)] * 3
        + [spec(pl.ANY)] * 4
        + [spec(pltpu.VMEM)] * len(more),
        out_specs=[spec(pltpu.VMEM)] * len(last),
        scratch_shapes=[
            pltpu.VMEM((c.N, c.E, c.cap, c.D), BF16),
            pltpu.VMEM((2, c.D, piece), BF16),
            pltpu.VMEM((2, c.D, piece), BF16),
            pltpu.VMEM((2, c.D, piece), BF16),
            pltpu.SemaphoreType.DMA((7,)),
        ],
        compiler_params=pltpu.CompilerParams(vmem_limit_bytes=VMEM_LIMIT),
        name="last",
    )(lengths, hid, meta, g_tok, made_home, grads, gy, gx, *more)
    out, g_tok, g_in, g_down = results[:4]
    if c.gather:
        g_qkv, g_out, g_gains, g_biases, g_router = results[4:]
    else:
        both = ("expert", "dp")
        flat = dense.astype(F32).transpose(1, 0, 2).reshape(c.D, 4 * c.D)
        flat = lax.psum_scatter(flat, both, scatter_dimension=0, tiled=True)
        small = lax.psum_scatter(small, both, scatter_dimension=1, tiled=True)
        flat, small = lax.psum((flat, small), "context")
        g_qkv, g_out = flat[:, : 3 * c.D], flat[:, 3 * c.D :]
        g_gains, g_biases = small[0:2], small[2:4]
        g_router = small[LOGIT_LANE : LOGIT_LANE + c.E]
    rows = (c.N, c.B, c.D)
    return (
        out.reshape(rows),
        g_tok.reshape(rows),
        g_qkv,
        g_out,
        g_router.T,
        g_gains,
        g_biases,
        g_in[None],
        g_down[None],
    )


def pack_small(c, w_router, norm_gains, norm_biases):
    rows = jnp.concatenate([norm_gains, norm_biases, w_router.T], axis=0).astype(F32)
    return jnp.pad(rows, ((0, c.r8 - rows.shape[0]), (0, 128 - rows.shape[1])))


def per_device(
    mesh_shape,
    tokens,
    lengths,
    route_ids,
    keep_mask,
    w_qkv,
    w_attn_out,
    w_router,
    norm_gains,
    norm_biases,
    w_expert_in,
    w_expert_down,
    cotangent,
):
    images, block, width = tokens.shape
    experts = mesh_shape["expert"] * w_expert_in.shape[0]
    c = types.SimpleNamespace(
        E=experts,
        Y=mesh_shape["dp"],
        C=mesh_shape["context"],
        N=images,
        B=block,
        D=width,
        T=images * block,
        S=mesh_shape["context"] * block,
        FF=w_expert_in.shape[2],
        FB=512,
        cap=max(2, 16 * block // (5 * experts)),
        sh=w_qkv.shape[0],
        r8=-(-(LOGIT_LANE + experts) // 8) * 8,
        scale=(width // HEADS) ** -0.5,
        chunks=4,
    )
    c.gather = c.sh % 32 == 0
    c.relay = experts == 4 and c.cap % 128 == 0
    tok = tokens.reshape(c.T, width)
    cot = cotangent.reshape(c.T, width)
    route = route_ids.transpose(0, 2, 1)
    keep = keep_mask.transpose(0, 2, 1)
    both = ("expert", "dp")
    if c.gather:
        given = (w_qkv, w_attn_out, pack_small(c, w_router, norm_gains, norm_biases))
    else:
        qkv = lax.all_gather(w_qkv, both, axis=0, tiled=True)
        out = lax.all_gather(w_attn_out, both, axis=0, tiled=True)
        small = pack_small(c, w_router, norm_gains, norm_biases)[:, : c.sh]
        vec = lax.all_gather(small, both, axis=1, tiled=True)
        stacked = jnp.concatenate([qkv, out], axis=1).reshape(width, 4, width).transpose(1, 0, 2)
        given = (stacked, vec)
    front = run_front(c, lengths, tok, route, keep, cot, given)
    weights, vec, q, kv, lse, att, hid, mix, meta, router, send, gsend, dyarr = front
    back = run_experts(c, send, gsend, dyarr, w_expert_in[0], w_expert_down[0])
    return run_back(
        c, tok, cot, lengths, weights, vec, q, kv, lse, att, hid, mix, meta, router, *back
    )


def solution(mesh):
    rows = P(("expert", "dp"), "context", None)
    shard = P(("expert", "dp"), None)
    column = P(None, ("expert", "dp"))
    expert = P("expert", None, None)
    return jax.shard_map(
        functools.partial(per_device, dict(mesh.shape)),
        mesh=mesh,
        in_specs=(rows, shard, rows, rows, shard, shard, shard, column, column, expert, expert, rows),
        out_specs=(
            rows,
            rows,
            shard,
            shard,
            shard,
            column,
            column,
            P("expert", None, ("context", "dp")),
            P("expert", ("context", "dp"), None),
        ),
        check_vma=False,
    )
```

```python
import functools
import itertools
import types

import jax
import jax.numpy as jnp
from jax import lax
from jax.experimental import pallas as pl
from jax.experimental.pallas import tpu as pltpu
from jax.sharding import PartitionSpec as P

HEADS = 12
EPS = 1e-06
F32 = jnp.float32
BF16 = jnp.bfloat16
MESH = pl.DeviceIdType.MESH
NN = (((1,), (0,)), ((), ()))
NT = (((1,), (1,)), ((), ()))
TN = (((0,), (0,)), ((), ()))
VMEM_LIMIT = 60 * 2**20
LOGIT_LANE = 4


def mm(left, right, dims=NN):
    return lax.dot_general(left, right, dims, preferred_element_type=F32)


def lane_of(shape):
    return lax.broadcasted_iota(jnp.int32, shape, 1)


def row_of(shape):
    return lax.broadcasted_iota(jnp.int32, shape, 0)


class Links:
    def __init__(self, send, recv):
        self.send, self.recv, self.ids = send, recv, itertools.count()

    def new(self):
        return next(self.ids)

    def make(self, at, src, dst, device):
        return pltpu.make_async_remote_copy(
            src_ref=src,
            dst_ref=dst,
            send_sem=self.send.at[at],
            recv_sem=self.recv.at[at],
            device_id=device,
            device_id_type=MESH,
        )


def greet(devices):
    barrier = pltpu.get_barrier_semaphore()
    for device in devices:
        pl.semaphore_signal(barrier, inc=1, device_id=device, device_id_type=MESH)
    pl.semaphore_wait(barrier, len(devices))


def normalize(values):
    centred = values - jnp.mean(values, axis=-1, keepdims=True)
    inverse = lax.rsqrt(jnp.mean(centred * centred, axis=-1, keepdims=True) + EPS)
    return centred * inverse, inverse


def normalize_back(grad_out, unit_rows, inverse, gain):
    scaled = grad_out * gain
    centre_term = jnp.mean(scaled, axis=-1, keepdims=True)
    slope_term = jnp.mean(scaled * unit_rows, axis=-1, keepdims=True)
    return inverse * (scaled - centre_term - unit_rows * slope_term)


def to_column(row):
    size = row.shape[1]
    eye = row_of((size, size)) == lane_of((size, size))
    return jnp.sum(jnp.where(eye, row, 0.0), axis=1, keepdims=True)


def to_row(column):
    size = column.shape[0]
    eye = row_of((size, size)) == lane_of((size, size))
    return jnp.sum(jnp.where(eye, column, 0.0), axis=0, keepdims=True)


def key_bias(c, len_ref, image):
    at = row_of((c.S, 1))
    bias = jnp.full((c.S, 1), -1e30, F32)
    for block in range(c.C):
        start = block * c.B
        inside = jnp.logical_and(at >= start, at < start + len_ref[image, block])
        bias = jnp.where(inside, 0.0, bias)
    return bias


def two_heads(pair):
    first = lane_of(pair.shape) < pair.shape[1] // 2
    zero = jnp.zeros_like(pair)
    return jnp.concatenate([jnp.where(first, pair, zero), jnp.where(first, zero, pair)], axis=0)


def one_pair(stacked):
    half = stacked.shape[0] // 2
    first = lane_of((half, stacked.shape[1])) < stacked.shape[1] // 2
    return jnp.where(first, stacked[:half], stacked[half:])


class Gather:
    def __init__(self, c, links, w_ref, rows_of, z, y, own_part, other_part):
        self.c, self.links, self.w_ref, self.rows_of = c, links, w_ref, rows_of
        self.z, self.y, self.own_part, self.other_part = z, y, own_part, other_part
        span = range(c.E)
        self.up = [links.new() for _ in span]
        self.down = [links.new() for _ in span]
        self.y_up = [links.new() for _ in span]
        self.y_down = [links.new() for _ in span]
        self.core_up = [[links.new() for _ in span] for _ in range(2)]
        self.core_down = [[links.new() for _ in span] for _ in range(2)]
        self.sent = []

    def route(self, above, below, y_dev, core_dev):
        self.above, self.below, self.y_dev, self.core_dev = above, below, y_dev, core_dev

    def unit(self, at, z_at, y_at, device, part=None):
        ref = self.w_ref.at[self.own_part if part is None else part, self.rows_of(z_at, y_at), :]
        return self.links.make(at, ref, ref, device)

    def send(self, condition, *where):
        pl.when(condition)(lambda: self.unit(*where).start())
        self.sent.append((condition, where))

    def got(self, condition, at, z_at, y_at, part=None):
        pl.when(condition)(lambda: self.unit(at, z_at, y_at, self.core_dev, part).wait_recv())

    def open(self):
        z, y = self.z, self.y
        self.send(z < self.c.E - 1, self.up[1], z, y, self.above)
        self.send(z > 0, self.down[1], z, y, self.below)
        self.send(z >= 0, self.y_up[0], z, y, self.y_dev)

    def pass_y(self, j):
        z, y = self.z, 1 - self.y
        lower, upper = z >= j, z + j <= self.c.E - 1
        self.got(lower, self.y_up[j], z - j, y)
        self.send(lower, self.core_up[1][j], z - j, y, self.core_dev)
        if j:
            self.got(upper, self.y_down[j], z + j, y)
            self.send(upper, self.core_down[1][j], z + j, y, self.core_dev)

    def step(self, j):
        z, y, last = self.z, self.y, self.c.E - 1
        if j <= last:
            lower, upper = z >= j, z + j <= last
            self.got(lower, self.up[j], z - j, y)
            if j < last:
                self.send(jnp.logical_and(lower, z < last), self.up[j + 1], z - j, y, self.above)
            self.send(lower, self.y_up[j], z - j, y, self.y_dev)
            self.send(lower, self.core_up[0][j], z - j, y, self.core_dev)
            self.got(upper, self.down[j], z + j, y)
            if j < last:
                self.send(jnp.logical_and(upper, z > 0), self.down[j + 1], z + j, y, self.below)
            self.send(upper, self.y_down[j], z + j, y, self.y_dev)
            self.send(upper, self.core_down[0][j], z + j, y, self.core_dev)
        self.pass_y(j - 1)

    def finish(self):
        z, last = self.z, self.c.E - 1
        for side in range(2):
            y = self.y if side == 0 else 1 - self.y
            if side:
                self.got(z >= 0, self.core_up[1][0], z, y, self.other_part)
            for j in range(1, self.c.E):
                self.got(z >= j, self.core_up[side][j], z - j, y, self.other_part)
                self.got(z + j <= last, self.core_down[side][j], z + j, y, self.other_part)

    def close(self):
        for condition, where in self.sent:
            pl.when(condition)(lambda: self.unit(*where).wait_send())


def front_kernel(c, *refs):
    refs = list(refs)
    take = lambda count: [refs.pop(0) for _ in range(count)]
    len_ref, tok_ref, route_ref, keep_ref, cot_ref = take(5)
    if c.gather:
        wqkv_ref, wout_ref, small_ref = take(3)
        w_hbm, vec_ref = take(2)
    else:
        w_ref, vec_ref = take(2)
    q_ref, kv_hbm, lse_ref, att_ref, hid_ref, mix_ref, meta_ref, router_ref = take(8)
    send_ref, gsend_ref, dyarr_ref = take(3)
    if c.gather:
        smalls, w_ref = take(2)
    kv_ref, dysend, lsem, ssem, rsem = take(5)
    if c.relay:
        dy_info, far_info, far_rows, dypack = take(4)
    links = Links(ssem, rsem)
    z, x, y = lax.axis_index("expert"), lax.axis_index("context"), lax.axis_index("dp")
    core = lax.rem(x, 2)
    shard = z * c.Y + y
    core_dev, far_dev, y_dev = (z, x ^ 1, y), (z, x ^ 2, y), (z, x, 1 - y)
    plane = [(lax.div(shard ^ k, c.Y), x, lax.rem(shard ^ k, c.Y)) for k in range(1, c.E * c.Y)]
    experts = [(z ^ k, x, y) for k in range(1, c.E)]
    greet([core_dev, far_dev] + (plane if c.gather else experts))
    ends = []

    def go(at, src, dst, device):
        copy = links.make(at, src, dst, device)
        copy.start()
        ends.append(copy)

    if c.gather:
        small_ids = [links.new() for _ in plane]
        smalls[shard] = small_ref[...]
        for at, device in zip(small_ids, plane):
            go(at, smalls.at[shard], smalls.at[shard], device)

        def rows_of(z_at, y_at):
            return pl.ds(pl.multiple_of((z_at * c.Y + y_at) * c.sh, 32), c.sh)

        own_rows = rows_of(z, y)
        for part in range(3):
            w_ref[part, own_rows, :] = wqkv_ref[:, part * c.D : (part + 1) * c.D]
        w_ref[3, own_rows, :] = wout_ref[...]

        above, below = (lax.rem(z + 1, c.E), x, y), (lax.rem(z + c.E - 1, c.E), x, y)
        stages = [Gather(c, links, w_ref, rows_of, z, y, *parts) for parts in (
            (1 + core, 2 - core), (3 * core, 3 - 3 * core))]
        for stage in stages:
            stage.route(above, below, y_dev, core_dev)
        stages[0].open()

    if c.relay:
        dy_info_id = links.new()
        dy_far_ids = [links.new() for _ in range(c.N)]
        dy_relay_ids = [links.new() for _ in range(c.N)]

    unit_rows = [None] * c.N
    choices = []
    for image in range(c.N):
        rows = slice(image * c.B, (image + 1) * c.B)
        live = jnp.where(row_of((c.B, 1)) < len_ref[image, x], 1.0, 0.0)
        kept = [to_column(keep_ref[image, j : j + 1, :].astype(F32)) * live for j in range(2)]
        first, second = [
            to_column(route_ref[image, j : j + 1, :].astype(F32)).astype(jnp.int32) for j in range(2)
        ]
        lane = lane_of((c.B, 128))
        named = jnp.where(lane == first, kept[0], 0.0) + jnp.where(
            lane == second, kept[1], 0.0
        )
        earlier = jnp.where(lane_of((c.B, c.B)) < row_of((c.B, c.B)), 1.0, 0.0).astype(BF16)
        rank = mm(earlier, named.astype(BF16))
        rank_first = jnp.sum(jnp.where(lane == first, rank, 0.0), axis=1, keepdims=True)
        rank_second = jnp.sum(jnp.where(lane == second, rank, 0.0), axis=1, keepdims=True)
        slot_first = first * c.cap + rank_first.astype(jnp.int32)
        slot_second = second * c.cap + rank_second.astype(jnp.int32)
        at = lane_of((c.B, c.E * c.cap))
        place = jnp.where(at == slot_first, kept[0], 0.0) + jnp.where(
            at == slot_second, kept[1], 0.0
        )
        place = place.astype(BF16)
        choices.append((first, second, kept, slot_first, slot_second, place))
        if c.relay:
            info = [to_row(column) for column in (slot_first.astype(F32), slot_second.astype(F32), *kept)]
            dy_info[image] = jnp.concatenate(info + [jnp.zeros((4, c.B), F32)], axis=0)
        dysend[image] = mm(place, cot_ref[rows, :], TN).astype(BF16).reshape(c.E, c.cap, c.D)

    if c.gather:
        for at, device in zip(small_ids, plane):
            other = lax.div(shard, 1)
            links.make(at, smalls.at[other], smalls.at[other], device).wait_recv()
        wide = jnp.concatenate([smalls[k] for k in range(c.E * c.Y)], axis=1).astype(BF16)
        span = c.E * c.Y * 128
        src, dst = row_of((span, c.D)), lane_of((span, c.D))
        inside = lax.rem(src, 128)
        pick = jnp.logical_and(inside < c.sh, lax.div(src, 128) * c.sh + inside == dst)
        vec_ref[...] = mm(wide, jnp.where(pick, 1.0, 0.0).astype(BF16))
    vec = vec_ref[...]
    own_at = pl.ds(pl.multiple_of(x * c.B, 32), c.B)
    norm_ids = [[links.new() for _ in range(3)] for _ in range(c.N)]
    for image in range(c.N):
        rows = slice(image * c.B, (image + 1) * c.B)
        unit_one, _ = normalize(tok_ref[rows, :].astype(F32))
        kv_ref[image, own_at, 2 * c.D : 3 * c.D] = (unit_one * vec[0:1] + vec[2:3]).astype(BF16)
        block = kv_ref.at[image, own_at, 2 * c.D : 3 * c.D]
        go(norm_ids[image][0], block, block, far_dev)
        go(norm_ids[image][1], block, block, core_dev)

    if c.gather:
        stages[0].step(1)
        stages[1].open()
        for j in range(2, c.E + 1):
            stages[0].step(j)
        stages[0].finish()

    normed = jnp.concatenate(
        [kv_ref[image, own_at, 2 * c.D : 3 * c.D] for image in range(c.N)], axis=0
    )
    kv_ids = [[links.new() for _ in range(3)] for _ in range(c.N)]
    keys = mm(normed, w_ref[1]).astype(BF16)
    values = mm(normed, w_ref[2]).astype(BF16)
    for image in range(c.N):
        rows = slice(image * c.B, (image + 1) * c.B)
        kv_ref[image, own_at, 0 : c.D] = keys[rows]
        kv_ref[image, own_at, c.D : 2 * c.D] = values[rows]
        block = kv_ref.at[image, own_at, 0 : 2 * c.D]
        go(kv_ids[image][0], block, block, far_dev)
        go(kv_ids[image][1], block, block, core_dev)
    if c.gather:
        for j in range(1, c.E + 1):
            stages[1].step(j)
    dy_ids = [links.new() for _ in experts]
    for k, (at, device) in enumerate(zip(dy_ids, experts), 1):
        if k == 1 or not c.relay:
            go(at, dysend.at[:, z ^ k], dyarr_ref.at[z], device)
    own_dy = pltpu.make_async_copy(dysend.at[:, z], dyarr_ref.at[z], lsem.at[0])
    own_dy.start()
    if c.relay:
        go(dy_info_id, dy_info, far_info, experts[1])

    def dy_to_far(image):
        rows = pl.ds(image * c.B, c.B)
        go(dy_far_ids[image], cot_ref.at[rows, :], far_rows.at[image], experts[1])

    def dy_pass_on(image):
        if image == 0:
            links.make(dy_info_id, far_info, far_info, experts[1]).wait_recv()
        here = far_rows.at[image]
        links.make(dy_far_ids[image], here, here, experts[1]).wait_recv()
        info = far_info[image]
        at = row_of((c.cap, c.B)).astype(F32)
        for index in range(2):
            first = ((z ^ index) * c.cap).astype(F32)
            kept = jnp.where(at == info[0:1] - first, info[2:3], 0.0)
            kept = kept + jnp.where(at == info[1:2] - first, info[3:4], 0.0)
            dypack[index, image] = mm(kept.astype(BF16), far_rows[image]).astype(BF16)
        go(dy_relay_ids[image], dypack.at[1, image], dyarr_ref.at[z ^ 2, image], experts[0])
        leaving.append(
            pltpu.make_async_copy(
                dypack.at[0, image], dyarr_ref.at[z ^ 2, image], lsem.at[2 + c.N + image]
            )
        )
        leaving[-1].start()

    leaving = [own_dy]
    if c.relay:
        dy_to_far(0)
    if c.gather:
        stages[1].finish()
        leaving.append(pltpu.make_async_copy(w_ref, w_hbm, lsem.at[1]))
        leaving[-1].start()
    q_ref[...] = mm(normed, w_ref[0]).astype(BF16)

    def block_of(image, who, first=0, last=2):
        rows_at = pl.ds(pl.multiple_of(who * c.B, 32), c.B)
        return kv_ref.at[image, rows_at, first * c.D : last * c.D]

    for image in range(c.N):
        far_block = block_of(image, x ^ 2, 2, 3)
        links.make(norm_ids[image][0], far_block, far_block, far_dev).wait_recv()
        go(norm_ids[image][2], far_block, far_block, core_dev)

    for image in range(c.N):
        rows = pl.ds(image * c.B, c.B)
        far_block = block_of(image, x ^ 2)
        links.make(kv_ids[image][0], far_block, far_block, far_dev).wait_recv()
        go(kv_ids[image][2], far_block, far_block, core_dev)
        near_block = block_of(image, x ^ 1)
        links.make(kv_ids[image][1], near_block, near_block, core_dev).wait_recv()
        cross_block = block_of(image, x ^ 3)
        links.make(kv_ids[image][2], cross_block, cross_block, core_dev).wait_recv()
        for at, who in ((1, x ^ 1), (2, x ^ 3)):
            there = block_of(image, who, 2, 3)
            links.make(norm_ids[image][at], there, there, core_dev).wait_recv()
        leaving.append(pltpu.make_async_copy(kv_ref.at[image], kv_hbm.at[image], lsem.at[2 + image]))
        leaving[-1].start()
        if c.relay and image == 0:
            dy_to_far(1)
        bias = key_bias(c, len_ref, image)

        def pair_step(pair, carry):
            lanes = pl.ds(pl.multiple_of(pair * 128, 128), 128)
            value_lanes = pl.ds(pl.multiple_of(c.D + pair * 128, 128), 128)
            queries = two_heads(q_ref[rows, lanes]) * jnp.asarray(c.scale, BF16)
            scores = mm(kv_ref[image, :, lanes], queries, NT) + bias
            top = jnp.max(scores, axis=0, keepdims=True)
            exponent = jnp.exp(scores - top)
            total = jnp.sum(exponent, axis=0, keepdims=True)
            probs = (exponent * (1.0 / total)).astype(BF16)
            lse_ref[image, pair] = jnp.broadcast_to(top + jnp.log(total), (8, 2 * c.B))
            mixed_values = mm(kv_ref[image, :, value_lanes].T, probs)
            att_ref[rows, lanes] = one_pair(mixed_values.T).astype(BF16)
            return carry

        lax.fori_loop(0, c.D // 128, pair_step, 0)
        if c.relay:
            dy_pass_on(image)

    branch = mm(att_ref[...], w_ref[3])
    hidden = tok_ref[...].astype(F32) + branch
    hid_ref[...] = hidden
    unit_two, _ = normalize(hidden)
    mixed = (unit_two * vec[1:2] + vec[3:4]).astype(BF16)
    mix_ref[...] = mixed
    pad = jnp.zeros((128 - c.r8, c.D), BF16)
    logits = mm(mixed, jnp.concatenate([vec.astype(BF16), pad], axis=0), NT)
    lane = lane_of((c.N * c.B, 128))
    valid = jnp.logical_and(lane >= LOGIT_LANE, lane < LOGIT_LANE + c.E)
    logits = jnp.where(valid, logits, -1e30)
    weight = jnp.exp(logits - jnp.max(logits, axis=1, keepdims=True))
    router = weight / jnp.sum(weight, axis=1, keepdims=True)
    router_ref[...] = router
    gsend_ref[...] = jnp.zeros_like(gsend_ref)
    lane = lane_of((c.B, 128))
    for image in range(c.N):
        rows = slice(image * c.B, (image + 1) * c.B)
        first, second, kept, slot_first, slot_second, place = choices[image]
        here = router[rows]
        gate_first = kept[0] * jnp.sum(
            jnp.where(lane == LOGIT_LANE + first, here, 0.0), axis=1, keepdims=True
        )
        gate_second = kept[1] * jnp.sum(
            jnp.where(lane == LOGIT_LANE + second, here, 0.0), axis=1, keepdims=True
        )
        send_ref[image] = mm(place, mixed[rows], TN).astype(BF16).reshape(c.E, c.cap, c.D)
        at = lane_of((c.B, c.cap))
        for expert in range(c.E):
            gates = jnp.where(at == slot_first - expert * c.cap, gate_first, 0.0)
            gates = gates + jnp.where(at == slot_second - expert * c.cap, gate_second, 0.0)
            gsend_ref[expert, image : image + 1, :] = jnp.sum(gates, axis=0, keepdims=True)
        columns = (
            slot_first.astype(F32),
            slot_second.astype(F32),
            kept[0],
            kept[1],
            gate_first,
            gate_second,
            first.astype(F32),
            second.astype(F32),
        )
        meta = jnp.zeros((c.B, 128), F32)
        for index, column in enumerate(columns):
            meta = jnp.where(lane == index, column, meta)
        meta_ref[rows, :] = meta

    for k, (at, device) in enumerate(zip(dy_ids, experts), 1):
        if k == 1 or not c.relay:
            links.make(at, dyarr_ref.at[z ^ k], dyarr_ref.at[z ^ k], device).wait_recv()
    if c.relay:
        for image in range(c.N):
            there = dyarr_ref.at[z ^ 3, image]
            links.make(dy_relay_ids[image], there, there, experts[0]).wait_recv()
    for copy in leaving:
        copy.wait()
    for copy in ends:
        copy.wait_send()
    if c.gather:
        for stage in stages:
            stage.close()


def spec(space):
    return pl.BlockSpec(memory_space=space)


def run_front(c, lengths, tok, route, keep, cot, weights):
    shape = jax.ShapeDtypeStruct
    made = [shape((4, c.D, c.D), BF16), shape((c.r8, c.D), F32)] if c.gather else []
    made += [
        shape((c.T, c.D), BF16),
        shape((c.N, c.S, 3 * c.D), BF16),
        shape((c.N, c.D // 128, 8, 2 * c.B), F32),
        shape((c.T, c.D), BF16),
        shape((c.T, c.D), F32),
        shape((c.T, c.D), BF16),
        shape((c.T, 128), F32),
        shape((c.T, 128), F32),
        shape((c.N, c.E, c.cap, c.D), BF16),
        shape((c.E, 8, c.cap), F32),
        shape((c.E, c.N, c.cap, c.D), BF16),
    ]
    count = 112 if c.gather else 2 * c.E + 32
    places = [spec(pltpu.VMEM)] * len(made)
    places[-1] = places[-10] = spec(pl.ANY)
    gather_scratch = []
    if c.gather:
        places[0] = spec(pl.ANY)
        gather_scratch = [
            pltpu.VMEM((c.E * c.Y, c.r8, 128), F32),
            pltpu.VMEM((4, c.D, c.D), BF16),
        ]
    relay_scratch = []
    if c.relay:
        relay_scratch = [
            pltpu.VMEM((c.N, 8, c.B), F32),
            pltpu.VMEM((c.N, 8, c.B), F32),
            pltpu.VMEM((c.N, c.B, c.D), BF16),
            pltpu.VMEM((2, c.N, c.cap, c.D), BF16),
        ]
    out = pl.pallas_call(
        functools.partial(front_kernel, c),
        out_shape=made,
        in_specs=[spec(pltpu.SMEM)] + [spec(pltpu.VMEM)] * (4 + len(weights)),
        out_specs=places,
        scratch_shapes=gather_scratch
        + [
            pltpu.VMEM((c.N, c.S, 3 * c.D), BF16),
            pltpu.VMEM((c.N, c.E, c.cap, c.D), BF16),
            pltpu.SemaphoreType.DMA((2 + 2 * c.N,)),
            pltpu.SemaphoreType.DMA((count,)),
            pltpu.SemaphoreType.DMA((count,)),
        ]
        + relay_scratch,
        compiler_params=pltpu.CompilerParams(
            collective_id=0, has_side_effects=True, vmem_limit_bytes=VMEM_LIMIT
        ),
        name="front",
    )(lengths, tok, route, keep, cot, *weights)
    return out if c.gather else list(weights) + list(out)


def gelu_both(pre):
    inner = 0.7978845608028654 * (pre + 0.044715 * pre * pre * pre)
    bend = jnp.tanh(inner)
    half = 0.5 * (1.0 + bend)
    slope = 0.7978845608028654 * (1.0 + 0.134145 * pre * pre)
    return pre * half, half + 0.5 * pre * (1.0 - bend * bend) * slope


def expert_kernel(
    c,
    send_ref,
    gsend_ref,
    dyarr_ref,
    win_hbm,
    wdown_hbm,
    xback_ref,
    gback_ref,
    yloc_ref,
    grad_hbm,
    gnext_hbm,
    win,
    wdown,
    arr,
    garr,
    act_all,
    dpre_all,
    dout_all,
    dxs,
    dgs,
    turned,
    gsend,
    grecv,
    gown,
    wsem,
    ssem,
    rsem,
):
    links = Links(ssem, rsem)
    z, x, y = lax.axis_index("expert"), lax.axis_index("context"), lax.axis_index("dp")
    experts = [(z ^ k, x, y) for k in range(1, c.E)]
    load_in = pltpu.make_async_copy(win_hbm, win, wsem.at[0])
    load_down = pltpu.make_async_copy(wdown_hbm, wdown, wsem.at[1])
    load_in.start()
    load_down.start()
    greet(experts + [(z, x ^ 1, y), (z, x ^ 2, y), (z, x, 1 - y)])
    ids = [[links.new() for _ in range(4)] for _ in range(c.E)]
    ends = []

    def go(at, src, dst, device):
        copy = links.make(at, src, dst, device)
        copy.start()
        ends.append(copy)

    group = c.E // c.chunks
    height = group * c.N * c.cap

    def dispatch(g):
        started = len(ends)
        for k in range(max(1, g * group), (g + 1) * group):
            go(ids[k][1], gsend_ref.at[z ^ k], garr.at[z], experts[k - 1])
            go(ids[k][0], send_ref.at[:, z ^ k], arr.at[z], experts[k - 1])
        return ends[started:]

    dispatch(0)
    early = dispatch(c.chunks - 2)
    for g in range(1, c.chunks - 2):
        dispatch(g)
    for image in range(c.N):
        arr[z, image] = send_ref[image, z]
    garr[z] = gsend_ref[z]
    load_in.wait()
    load_down.wait()
    dgs[...] = jnp.zeros_like(dgs)
    for g in range(c.chunks):
        if g == 1:
            for copy in early:
                copy.wait_send()
            ends[:] = [copy for copy in ends if all(copy is not other for other in early)]
            dispatch(c.chunks - 1)
        slab = lax.div(z, group) ^ g
        for k in range(g * group, (g + 1) * group):
            if k:
                there = z ^ k
                links.make(ids[k][0], arr.at[there], arr.at[there], experts[k - 1]).wait_recv()
                links.make(ids[k][1], garr.at[there], garr.at[there], experts[k - 1]).wait_recv()
        start = pl.multiple_of(slab * height, 32)
        rows = pl.ds(start, height)
        for member in range(group):
            source = slab * group + member
            for image in range(c.N):
                gates = to_column(garr[source, image : image + 1, :])
                offset = (member * c.N + image) * c.cap
                part = pl.ds(pl.multiple_of(start + offset, 16), c.cap)
                dout_all[part, :] = (gates * dyarr_ref[source, image].astype(F32)).astype(BF16)
        inputs = arr[pl.ds(slab * group, group)].reshape(height, c.D)
        douts = dout_all[rows, :]

        def ff_step(step, carry):
            lanes = pl.ds(pl.multiple_of(step * c.FB, 128), c.FB)
            pre = mm(inputs, win[:, lanes])
            act, slope = gelu_both(pre)
            act_all[rows, lanes] = act.astype(BF16)
            dact = mm(douts, wdown[lanes, :], NT)
            dpre_all[rows, lanes] = (dact * slope).astype(BF16)
            return carry

        lax.fori_loop(0, c.FF // c.FB, ff_step, 0)
        dx = mm(dpre_all[rows, :], win[...], NT).astype(BF16)
        dxs[pl.ds(slab * group, group)] = dx.reshape(group, c.N, c.cap, c.D)
        made = mm(act_all[rows, :], wdown[...]).astype(BF16)
        yloc_ref[pl.ds(slab * group, group)] = made.reshape(group, c.N, c.cap, c.D)
        for member in range(group):
            source = slab * group + member
            for image in range(c.N):
                offset = (member * c.N + image) * c.cap
                dots = made[offset : offset + c.cap].astype(F32) * dyarr_ref[source, image].astype(
                    F32
                )
                dgs[source, image : image + 1, :] = to_row(jnp.sum(dots, axis=1, keepdims=True))
        for k in range(g * group, (g + 1) * group):
            if k:
                there = z ^ k
                go(ids[k][2], dxs.at[there], xback_ref.at[:, z], experts[k - 1])
                go(ids[k][3], dgs.at[there], gback_ref.at[z], experts[k - 1])
    for image in range(c.N):
        xback_ref[image, z] = dxs[z, image]
    gback_ref[z] = dgs[z]

    total = c.E * c.N * c.cap
    turned[0] = arr[...].reshape(total, c.D).T
    turned[1] = dout_all[...].T

    core = lax.rem(x, 2)
    core_dev, far_dev, y_dev = (z, x ^ 1, y), (z, x ^ 2, y), (z, x, 1 - y)
    half = c.FF // 4
    grad_ids = [[links.new() for _ in range(2)] for _ in range(2)]
    sources = (dpre_all, act_all)

    def blocks(which, owner, into):
        def block_step(part, carry):
            lanes = pl.ds(pl.multiple_of((2 * part + owner) * half, 128), half)
            into[part, which] = mm(turned[which], sources[which][:, lanes]).astype(BF16)
            return carry

        lax.fori_loop(0, 2, block_step, 0)

    piece = half // 2
    side = lax.div(x, 2)
    other_piece = pl.ds(pl.multiple_of((1 - y) * piece, 128), piece)
    next_ids = [links.new() for _ in range(2)]
    leaving = []
    for which in range(2):
        blocks(which, 1 - core, gsend)
        for part in range(2):
            go(grad_ids[which][part], gsend.at[part, which], grecv.at[part, which], core_dev)
        blocks(which, core, gown)
        for part in range(2):
            there = grecv.at[part, which]
            links.make(grad_ids[which][part], there, there, core_dev).wait_recv()
            gown[part, which] = (
                gown[part, which].astype(F32) + grecv[part, which].astype(F32)
            ).astype(BF16)
        first = gown.at[1 - side, which, :, other_piece]
        go(next_ids[which], first, gnext_hbm.at[which], y_dev if which == 0 else far_dev)
        for part in range(2):
            leaving.append(
                pltpu.make_async_copy(
                    gown.at[part, which], grad_hbm.at[part, which], wsem.at[2 + 2 * which + part]
                )
            )
            leaving[-1].start()
    for which in range(2):
        there = gnext_hbm.at[which]
        links.make(next_ids[which], there, there, core_dev).wait_recv()
    for copy in leaving:
        copy.wait()
    for k in range(1, c.E):
        there = z ^ k
        links.make(ids[k][2], xback_ref.at[:, there], xback_ref.at[:, there], experts[k - 1]).wait_recv()
        links.make(ids[k][3], gback_ref.at[there], gback_ref.at[there], experts[k - 1]).wait_recv()
    for copy in ends:
        copy.wait_send()


def run_experts(c, send, gsend, dyarr, w_in, w_down):
    shape = jax.ShapeDtypeStruct
    total = c.E * c.N * c.cap
    count = 4 * c.E + 6
    return pl.pallas_call(
        functools.partial(expert_kernel, c),
        out_shape=[
            shape((c.N, c.E, c.cap, c.D), BF16),
            shape((c.E, 8, c.cap), F32),
            shape((c.E, c.N, c.cap, c.D), BF16),
            shape((2, 2, c.D, c.FF // 4), BF16),
            shape((2, c.D, c.FF // 8), BF16),
        ],
        in_specs=[spec(pltpu.VMEM)] * 3 + [spec(pl.ANY)] * 2,
        out_specs=[spec(pltpu.VMEM)] * 3 + [spec(pl.ANY)] * 2,
        scratch_shapes=[
            pltpu.VMEM((c.D, c.FF), BF16),
            pltpu.VMEM((c.FF, c.D), BF16),
            pltpu.VMEM((c.E, c.N, c.cap, c.D), BF16),
            pltpu.VMEM((c.E, 8, c.cap), F32),
            pltpu.VMEM((total, c.FF), BF16),
            pltpu.VMEM((total, c.FF), BF16),
            pltpu.VMEM((total, c.D), BF16),
            pltpu.VMEM((c.E, c.N, c.cap, c.D), BF16),
            pltpu.VMEM((c.E, 8, c.cap), F32),
            pltpu.VMEM((2, c.D, total), BF16),
            pltpu.VMEM((2, 2, c.D, c.FF // 4), BF16),
            pltpu.VMEM((2, 2, c.D, c.FF // 4), BF16),
            pltpu.VMEM((2, 2, c.D, c.FF // 4), BF16),
            pltpu.SemaphoreType.DMA((6,)),
            pltpu.SemaphoreType.DMA((count,)),
            pltpu.SemaphoreType.DMA((count,)),
        ],
        compiler_params=pltpu.CompilerParams(
            collective_id=1, has_side_effects=True, vmem_limit_bytes=VMEM_LIMIT
        ),
        name="experts",
    )(send, gsend, dyarr, w_in, w_down)


def in_parts(values, count):
    parts = []
    for _ in range(count):
        parts.append(values.astype(BF16))
        values = values - parts[-1].astype(F32)
    return parts


def back_kernel(c, *refs):
    refs = list(refs)
    take = lambda count: [refs.pop(0) for _ in range(count)]
    len_ref, tok_ref, cot_ref, vec_ref, q_ref, lse_ref, att_ref, hid_ref, mix_ref = take(9)
    meta_ref, router_ref, xback_ref, gback_ref = take(4)
    w_hbm, kv_hbm, yloc_hbm, grad_hbm, gnext_hbm = take(5)
    gtok_hbm, made, gy, gx = take(4)
    if c.gather:
        whole, gsmall_ref = take(2)
    else:
        dd, gsmall_ref = take(2)
    w_ref, kv_ref, gtok_ref, gpart, gnext = take(5)
    dkv, kvcore, kvfar, dproj, datt, dhid, norm_t, norm_all, router_sum = take(9)
    if c.gather:
        dd, dcore, done_x, done_y, done_z, small_four, small_y, small_z = take(8)
    lsem, ssem, rsem = take(3)
    links = Links(ssem, rsem)
    z, x, y = lax.axis_index("expert"), lax.axis_index("context"), lax.axis_index("dp")
    core, side = lax.rem(x, 2), lax.div(x, 2)
    core_dev, far_dev, y_dev = (z, x ^ 1, y), (z, x ^ 2, y), (z, x, 1 - y)
    experts = [(z ^ k, x, y) for k in range(1, c.E)]
    ends = []

    def go(at, src, dst, device):
        copy = links.make(at, src, dst, device)
        copy.start()
        ends.append(copy)

    def got(at, dst, device):
        links.make(at, dst, dst, device).wait_recv()

    half = c.FF // 4
    piece = half // 2
    loads = [
        pltpu.make_async_copy(w_hbm, w_ref, lsem.at[0]),
        pltpu.make_async_copy(kv_hbm, kv_ref, lsem.at[1]),
    ]
    own_piece = pl.ds(pl.multiple_of(y * piece, 128), piece)
    other_piece = pl.ds(pl.multiple_of((1 - y) * piece, 128), piece)
    parts = (grad_hbm.at[1 - side, 0, :, own_piece], grad_hbm.at[side, 1, :, other_piece])
    for which in range(2):
        loads.append(pltpu.make_async_copy(parts[which], gpart.at[which], lsem.at[2 + which]))
        loads.append(
            pltpu.make_async_copy(gnext_hbm.at[which], gnext.at[which], lsem.at[6 + which])
        )
    own_made = pltpu.make_async_copy(yloc_hbm.at[z], made.at[:, z], lsem.at[4])
    loads.append(own_made)
    for load in loads:
        load.start()
    cross_dev = [(z, x ^ 3, y)] if c.gather else []
    greet([core_dev, far_dev, y_dev] + experts + cross_dev)

    made_ids = [links.new() for _ in experts]
    for k, (at, device) in enumerate(zip(made_ids, experts), 1):
        go(at, yloc_hbm.at[z ^ k], made.at[:, z], device)
    gy_ids = [links.new() for _ in range(2)]
    gx_ids = [links.new() for _ in range(2)]
    go(gy_ids[0], grad_hbm.at[side, 0, :, other_piece], gy.at[0], y_dev)
    go(gx_ids[1], grad_hbm.at[1 - side, 1, :, own_piece], gx.at[1], far_dev)
    for which in range(2):
        loads[2 + 2 * which].wait()
        loads[3 + 2 * which].wait()
        gpart[which] = (gpart[which].astype(F32) + gnext[which].astype(F32)).astype(BF16)
        if which == 0:
            go(gx_ids[0], gpart.at[0], gx.at[0], far_dev)
        else:
            go(gy_ids[1], gpart.at[1], gy.at[1], y_dev)

    def grads_end():
        for which in range(2):
            got(gy_ids[which], gy.at[which], y_dev)
            got(gx_ids[which], gx.at[which], far_dev)

    if c.gather:
        n_dense = 4
        core_cols = c.D // 2
        keep_cols = pl.ds(pl.multiple_of(core * core_cols, 128), core_cols)
        give_cols = pl.ds(pl.multiple_of((1 - core) * core_cols, 128), core_cols)
        ids_core = [links.new() for _ in range(n_dense)]
        ids_x = [links.new() for _ in range(n_dense)]
        ids_y = [links.new() for _ in range(n_dense)]
        ids_z = [[links.new() for _ in experts] for _ in range(n_dense)]
        ids_own = [links.new() for _ in range(n_dense)]

        def dense_start(m, value):
            dd[m] = value.astype(BF16).reshape(c.E, c.Y, c.sh, c.D)
            go(ids_core[m], dd.at[m, :, :, :, give_cols], dcore.at[m], core_dev)

        def dense_y(m):
            got(ids_core[m], dcore.at[m], core_dev)
            dd[m, :, :, :, keep_cols] = (
                dd[m, :, :, :, keep_cols].astype(F32) + dcore[m].astype(F32)
            ).astype(BF16)
            go(ids_y[m], dd.at[m, :, 1 - y, :, keep_cols], done_y.at[m], y_dev)

        def dense_z(m):
            got(ids_y[m], done_y.at[m], y_dev)
            dd[m, :, y, :, keep_cols] = (
                dd[m, :, y, :, keep_cols].astype(F32) + done_y[m].astype(F32)
            ).astype(BF16)
            for k, device in enumerate(experts, 1):
                go(
                    ids_z[m][k - 1],
                    dd.at[m, z ^ k, y, :, keep_cols],
                    done_z.at[m, z],
                    device,
                )

        def dense_x(m):
            total = dd[m, z, y, :, keep_cols].astype(F32)
            for k, device in enumerate(experts, 1):
                got(ids_z[m][k - 1], done_z.at[m, z ^ k], device)
                total = total + done_z[m, z ^ k].astype(F32)
            done_x[m, 0] = total.astype(BF16)
            go(ids_x[m], done_x.at[m, 0], done_x.at[m, 1], far_dev)

        def dense_share(m):
            got(ids_x[m], done_x.at[m, 1], far_dev)
            whole[m, core] = done_x[m, 0].astype(F32) + done_x[m, 1].astype(F32)
            go(ids_own[m], whole.at[m, core], whole.at[m, core], core_dev)

        def dense_end(m):
            there = whole.at[m, 1 - core]
            got(ids_own[m], there, core_dev)

    else:

        def dense_start(m, value):
            dd[m] = value.astype(BF16)

    vec = vec_ref[...]
    lane = lane_of((c.B, 128))
    d_mixed, dy_rows = [], []
    d_logits = []
    for image in range(c.N):
        rows = slice(image * c.B, (image + 1) * c.B)
        meta = meta_ref[rows, :]
        slots = [meta[:, j : j + 1].astype(jnp.int32) for j in range(2)]
        kept = [meta[:, 2 + j : 3 + j] for j in range(2)]
        names = [meta[:, 6 + j : 7 + j].astype(jnp.int32) for j in range(2)]
        at = lane_of((c.B, c.E * c.cap))
        place = jnp.where(at == slots[0], kept[0], 0.0) + jnp.where(at == slots[1], kept[1], 0.0)
        copies = xback_ref[image].reshape(c.E * c.cap, c.D)
        d_mixed.append(mm(place.astype(BF16), copies))
        d_router = jnp.zeros((c.B, 128), F32)
        at = lane_of((c.B, c.cap))
        for j in range(2):
            d_gate = jnp.zeros((c.B, c.cap), F32)
            for expert in range(c.E):
                row = gback_ref[expert, image : image + 1, :]
                d_gate = d_gate + jnp.where(at == slots[j] - expert * c.cap, row, 0.0)
            d_gate = jnp.sum(d_gate, axis=1, keepdims=True) * kept[j]
            d_router = d_router + jnp.where(lane == LOGIT_LANE + names[j], d_gate, 0.0)
        router = router_ref[rows, :]
        dot = jnp.sum(router * d_router, axis=1, keepdims=True)
        d_logits.append(router * (d_router - dot))
        live = jnp.where(row_of((c.B, 1)) < len_ref[image, x], 1.0, 0.0)
        dy_rows.append(cot_ref[rows, :].astype(F32) * live)
    d_mixed = jnp.concatenate(d_mixed, axis=0)
    d_logits = jnp.concatenate(d_logits, axis=0)
    dy_rows = jnp.concatenate(dy_rows, axis=0)
    logit_rows = jnp.concatenate([vec, jnp.zeros((128 - c.r8, c.D), F32)], axis=0)
    lane_here = row_of((128, c.D))
    is_router = jnp.logical_and(lane_here >= LOGIT_LANE, lane_here < LOGIT_LANE + c.E)
    w_router = jnp.where(is_router, logit_rows, 0.0)
    high, low = in_parts(d_logits, 2)
    w_router = w_router.astype(BF16)
    d_mixed = d_mixed + mm(high, w_router) + mm(low, w_router)
    router_sum[...] = mm(high, mix_ref[...], TN) + mm(low, mix_ref[...], TN)
    unit_two, inverse_two = normalize(hid_ref[...])
    gains_two = jnp.sum(d_mixed * unit_two, axis=0, keepdims=True)
    biases_two = jnp.sum(d_mixed, axis=0, keepdims=True)
    d_hidden = dy_rows + normalize_back(d_mixed, unit_two, inverse_two, vec[1:2])
    dhid[...] = d_hidden
    d_branch = d_hidden.astype(BF16)
    dense_start(3, mm(att_ref[...], d_branch, TN))
    loads[0].wait()
    datt[...] = mm(d_branch, w_ref[3], NT).astype(BF16)
    unit_one, inverse_one = normalize(tok_ref[...].astype(F32))
    norm_t[...] = (unit_one * vec[0:1] + vec[2:3]).astype(BF16).T
    loads[1].wait()
    for image in range(c.N):
        norm_all[:, image * c.S : (image + 1) * c.S] = kv_ref[image, :, 2 * c.D : 3 * c.D].T

    kvcore_ids = [[links.new() for _ in range(2)] for _ in range(c.N)]
    kvfar_ids = [links.new() for _ in range(c.N)]

    def block_rows(who):
        return pl.ds(pl.multiple_of(who * c.B, 32), c.B)

    def attend_back(image, first_pair, last_pair):
        rows = pl.ds(image * c.B, c.B)
        bias = key_bias(c, len_ref, image)

        def pair_step(pair, carry):
            lanes = pl.ds(pl.multiple_of(pair * 128, 128), 128)
            value_lanes = pl.ds(pl.multiple_of(c.D + pair * 128, 128), 128)
            scale = jnp.asarray(c.scale, BF16)
            queries = two_heads(q_ref[rows, lanes]) * scale
            grads = two_heads(datt[rows, lanes])
            keys = kv_ref[image, :, lanes]
            probs = jnp.exp(mm(keys, queries, NT) + bias - lse_ref[image, pair][0:1])
            d_probs = mm(kv_ref[image, :, value_lanes], grads, NT)
            dot = jnp.sum(probs * d_probs, axis=0, keepdims=True)
            d_scores = (probs * (d_probs - dot)).astype(BF16)
            dkv[image, :, value_lanes] = mm(probs.astype(BF16), grads).astype(BF16)
            dkv[image, :, lanes] = mm(d_scores, queries).astype(BF16)
            d_queries = mm(keys.T, d_scores).T
            dproj[rows, lanes] = (one_pair(d_queries) * c.scale).astype(BF16)
            return carry

        lax.fori_loop(first_pair, last_pair, pair_step, 0)

    def kv_to_core(image):
        for s in range(2):
            block = dkv.at[image, block_rows(2 * s + 1 - core), :]
            go(kvcore_ids[image][s], block, kvcore.at[image, s], core_dev)

    def kv_to_far(image):
        for s in range(2):
            got(kvcore_ids[image][s], kvcore.at[image, s], core_dev)
        rows = block_rows(2 * (1 - side) + core)
        kvcore[image, 1 - side] = (
            dkv[image, rows, :].astype(F32) + kvcore[image, 1 - side].astype(F32)
        ).astype(BF16)
        go(kvfar_ids[image], kvcore.at[image, 1 - side], kvfar.at[image], far_dev)

    def kv_end(image):
        got(kvfar_ids[image], kvfar.at[image], far_dev)
        total = dkv[image, block_rows(2 * side + core), :].astype(F32)
        total = total + kvcore[image, side].astype(F32) + kvfar[image].astype(F32)
        rows = pl.ds(image * c.B, c.B)
        dproj[rows, c.D : 3 * c.D] = total.astype(BF16)

    pairs = c.D // 128
    attend_back(0, 0, pairs)
    kv_to_core(0)
    if c.gather:
        dense_y(3)
    attend_back(1, 0, pairs // 2)
    kv_to_far(0)
    attend_back(1, pairs // 2, pairs)
    kv_to_core(1)
    dense_start(0, mm(norm_t[...], dproj[:, 0 : c.D]))
    for m in (1, 2):
        columns = slice((m - 1) * c.D, m * c.D)
        dense_start(m, mm(norm_all[...], dkv[:, :, columns].reshape(c.N * c.S, c.D)))
    kv_to_far(1)
    if c.gather:
        dense_y(0)
        dense_y(1)
        dense_y(2)
        dense_z(3)
        kv_end(0)
        dense_z(0)
        dense_x(3)
        dense_z(1)
    else:
        kv_end(0)
    kv_end(1)
    d_normed = mm(dproj[:, 0 : c.D], w_ref[0], NT)
    d_normed = d_normed + mm(dproj[:, c.D : 2 * c.D], w_ref[1], NT)
    d_normed = d_normed + mm(dproj[:, 2 * c.D : 3 * c.D], w_ref[2], NT)
    unit_one, inverse_one = normalize(tok_ref[...].astype(F32))
    gains_one = jnp.sum(d_normed * unit_one, axis=0, keepdims=True)
    biases_one = jnp.sum(d_normed, axis=0, keepdims=True)
    small_here = jnp.concatenate([gains_one, gains_two, biases_one, biases_two], axis=0)
    small_here = jnp.concatenate(
        [small_here, router_sum[LOGIT_LANE : LOGIT_LANE + c.r8 - 4]], axis=0
    )
    if c.gather:
        small_ids = [links.new() for _ in range(3)]
        small_y_id = links.new()
        small_z_ids = [links.new() for _ in experts]
        small_four[x] = small_here
        for k, at in enumerate(small_ids, 1):
            go(at, small_four.at[x], small_four.at[x], (z, x ^ k, y))
    gtok_ref[...] = dhid[...] + normalize_back(d_normed, unit_one, inverse_one, vec[0:1])
    leave = pltpu.make_async_copy(gtok_ref, gtok_hbm, lsem.at[5])
    leave.start()
    if c.gather:

        dense_x(0)
        dense_share(3)
        dense_z(2)
        for k, at in enumerate(small_ids, 1):
            got(at, small_four.at[x ^ k], (z, x ^ k, y))
        small_y[0] = (small_four[0] + small_four[1]) + (small_four[2] + small_four[3])
        go(small_y_id, small_y.at[0], small_y.at[1], y_dev)
        dense_x(1)
        dense_share(0)
        got(small_y_id, small_y.at[1], y_dev)
        small_z[z] = small_y[0] + small_y[1]
        for at, device in zip(small_z_ids, experts):
            go(at, small_z.at[z], small_z.at[z], device)
        dense_end(3)
        dense_x(2)
        dense_share(1)
        dense_end(0)
        for k, (at, device) in enumerate(zip(small_z_ids, experts), 1):
            got(at, small_z.at[z ^ k], device)
        gsmall_ref[...] = sum((small_z[k] for k in range(1, c.E)), small_z[0])
        dense_share(2)
        dense_end(1)
        dense_end(2)
    else:
        gsmall_ref[...] = small_here
    for k, (at, device) in enumerate(zip(made_ids, experts), 1):
        got(at, made.at[:, z ^ k], device)
    grads_end()
    leave.wait()
    own_made.wait()
    for copy in ends:
        copy.wait_send()


def last_kernel(c, *refs):
    refs = list(refs)
    take = lambda count: [refs.pop(0) for _ in range(count)]
    len_ref, hid_ref, meta_ref, gtok_in, made_in, grad_in, gy_in, gx_in = take(8)
    if c.gather:
        whole_ref, small_ref = take(2)
    out_ref, gtok_out, gin_out, gdown_out = take(4)
    if c.gather:
        gqkv_ref, gout_ref, gains_ref, biases_ref, grouter_ref = take(5)
    made, gown, gy, gx, gin_ref, gdown_ref, sem = take(7)
    z, x, y = lax.axis_index("expert"), lax.axis_index("context"), lax.axis_index("dp")
    side = lax.div(x, 2)
    piece = c.FF // 8
    own_piece = pl.ds(pl.multiple_of(y * piece, 128), piece)
    loads = []
    for which in range(2):
        for index, (src, dst) in enumerate((
            (grad_in.at[side, which, :, own_piece], gown.at[which]),
            (gy_in.at[which], gy.at[which]),
            (gx_in.at[which], gx.at[which]),
        )):
            loads.append(pltpu.make_async_copy(src, dst, sem.at[3 * which + index]))
    loads.append(pltpu.make_async_copy(made_in, made, sem.at[6]))
    for load in loads:
        load.start()
    leaving = [pltpu.make_async_copy(gtok_in, gtok_out, sem.at[7])]
    leaving[0].start()
    if c.gather:
        core_cols = c.D // 2
        for m in range(4):
            for k in range(2):
                if m == 3:
                    gout_ref[:, k * core_cols : (k + 1) * core_cols] = whole_ref[m, k]
                else:
                    start = m * c.D + k * core_cols
                    gqkv_ref[:, start : start + core_cols] = whole_ref[m, k]
        src, dst = row_of((c.D, 128)), lane_of((c.D, 128))
        pick = jnp.logical_and(dst < c.sh, src == dst + (z * c.Y + y) * c.sh)
        pick = jnp.where(pick, 1.0, 0.0).astype(BF16)
        small = sum(mm(part, pick) for part in in_parts(small_ref[...], 3))
        gains_ref[...] = small[0:2, 0 : c.sh]
        biases_ref[...] = small[2:4, 0 : c.sh]
        grouter_ref[...] = small[LOGIT_LANE : LOGIT_LANE + c.E, 0 : c.sh]
    for which in range(2):
        for load in loads[3 * which : 3 * which + 3]:
            load.wait()
        total = gown[which].astype(F32) + gy[which].astype(F32) + gx[which].astype(F32)
        if which == 0:
            gin_ref[...] = total
        else:
            gdown_ref[...] = total.T
        src, dst = ((gin_ref, gin_out), (gdown_ref, gdown_out))[which]
        leaving.append(pltpu.make_async_copy(src, dst, sem.at[8 + which]))
        leaving[-1].start()
    loads[6].wait()
    for image in range(c.N):
        rows = slice(image * c.B, (image + 1) * c.B)
        meta = meta_ref[rows, :]
        slots = [meta[:, j : j + 1].astype(jnp.int32) for j in range(2)]
        at = lane_of((c.B, c.E * c.cap))
        gates = jnp.where(at == slots[0], meta[:, 4:5], 0.0)
        gates = gates + jnp.where(at == slots[1], meta[:, 5:6], 0.0)
        high, low = in_parts(gates, 2)
        rows_made = made[image].reshape(c.E * c.cap, c.D)
        mixture = mm(high, rows_made) + mm(low, rows_made)
        live = jnp.where(row_of((c.B, 1)) < len_ref[image, x], 1.0, 0.0)
        out_ref[rows, :] = (live * (hid_ref[rows, :] + mixture)).astype(BF16)
    for copy in leaving:
        copy.wait()


def run_back(c, tok, cot, lengths, weights, vec, q, kv, lse, att, hid, mix, meta, router, xback, gback, yloc, grads, gnext):
    shape = jax.ShapeDtypeStruct
    piece = c.FF // 8
    made = [
        shape((c.T, c.D), F32),
        shape((c.N, c.E, c.cap, c.D), BF16),
        shape((2, c.D, piece), BF16),
        shape((2, c.D, piece), BF16),
    ]
    dense_scratch = []
    if c.gather:
        half_cols = c.D // 2
        made += [shape((4, 2, c.sh, half_cols), F32), shape((c.r8, c.D), F32)]
        dense_scratch = [
            pltpu.VMEM((4, c.E, c.Y, c.sh, c.D), BF16),
            pltpu.VMEM((4, c.E, c.Y, c.sh, half_cols), BF16),
            pltpu.VMEM((4, 2, c.sh, half_cols), BF16),
            pltpu.VMEM((4, c.E, c.sh, half_cols), BF16),
            pltpu.VMEM((4, c.E, c.sh, half_cols), BF16),
            pltpu.VMEM((c.C, c.r8, c.D), F32),
            pltpu.VMEM((2, c.r8, c.D), F32),
            pltpu.VMEM((c.E, c.r8, c.D), F32),
        ]
    else:
        made += [shape((4, c.D, c.D), BF16), shape((c.r8, c.D), F32)]
    count = 5 * c.E + 64
    results = pl.pallas_call(
        functools.partial(back_kernel, c),
        out_shape=made,
        in_specs=[spec(pltpu.SMEM)] + [spec(pltpu.VMEM)] * 12 + [spec(pl.ANY)] * 5,
        out_specs=[spec(pl.ANY)] * 4 + [spec(pltpu.VMEM)] * 2,
        scratch_shapes=[
            pltpu.VMEM((4, c.D, c.D), BF16),
            pltpu.VMEM((c.N, c.S, 3 * c.D), BF16),
            pltpu.VMEM((c.T, c.D), F32),
            pltpu.VMEM((2, c.D, piece), BF16),
            pltpu.VMEM((2, c.D, piece), BF16),
            pltpu.VMEM((c.N, c.S, 2 * c.D), BF16),
            pltpu.VMEM((c.N, 2, c.B, 2 * c.D), BF16),
            pltpu.VMEM((c.N, c.B, 2 * c.D), BF16),
            pltpu.VMEM((c.T, 3 * c.D), BF16),
            pltpu.VMEM((c.T, c.D), BF16),
            pltpu.VMEM((c.T, c.D), F32),
            pltpu.VMEM((c.D, c.T), BF16),
            pltpu.VMEM((c.D, c.N * c.S), BF16),
            pltpu.VMEM((128, c.D), F32),
            *dense_scratch,
            pltpu.SemaphoreType.DMA((8,)),
            pltpu.SemaphoreType.DMA((count,)),
            pltpu.SemaphoreType.DMA((count,)),
        ],
        compiler_params=pltpu.CompilerParams(
            collective_id=2, has_side_effects=True, vmem_limit_bytes=VMEM_LIMIT
        ),
        name="back",
    )(lengths, tok, cot, vec, q, lse, att, hid, mix, meta, router, xback, gback, weights, kv, yloc, grads, gnext)
    g_tok, made_home, gy, gx, dense, small = results
    last = [shape((c.T, c.D), BF16), shape((c.T, c.D), F32)]
    last += [shape((c.D, piece), F32), shape((piece, c.D), F32)]
    if c.gather:
        last += [shape((c.sh, 3 * c.D), F32), shape((c.sh, c.D), F32)]
        last += [shape((2, c.sh), F32), shape((2, c.sh), F32), shape((c.E, c.sh), F32)]
    more = (dense, small) if c.gather else ()
    results = pl.pallas_call(
        functools.partial(last_kernel, c),
        out_shape=last,
        in_specs=[spec(pltpu.SMEM)]
        + [spec(pltpu.VMEM)] * 3
        + [spec(pl.ANY)] * 4
        + [spec(pltpu.VMEM)] * len(more),
        out_specs=[spec(pltpu.VMEM)] + [spec(pl.ANY)] * 3 + [spec(pltpu.VMEM)] * (len(last) - 4),
        scratch_shapes=[
            pltpu.VMEM((c.N, c.E, c.cap, c.D), BF16),
            pltpu.VMEM((2, c.D, piece), BF16),
            pltpu.VMEM((2, c.D, piece), BF16),
            pltpu.VMEM((2, c.D, piece), BF16),
            pltpu.VMEM((c.D, piece), F32),
            pltpu.VMEM((piece, c.D), F32),
            pltpu.SemaphoreType.DMA((10,)),
        ],
        compiler_params=pltpu.CompilerParams(vmem_limit_bytes=VMEM_LIMIT),
        name="last",
    )(lengths, hid, meta, g_tok, made_home, grads, gy, gx, *more)
    out, g_tok, g_in, g_down = results[:4]
    if c.gather:
        g_qkv, g_out, g_gains, g_biases, g_router = results[4:]
    else:
        both = ("expert", "dp")
        flat = dense.astype(F32).transpose(1, 0, 2).reshape(c.D, 4 * c.D)
        flat = lax.psum_scatter(flat, both, scatter_dimension=0, tiled=True)
        small = lax.psum_scatter(small, both, scatter_dimension=1, tiled=True)
        flat, small = lax.psum((flat, small), "context")
        g_qkv, g_out = flat[:, : 3 * c.D], flat[:, 3 * c.D :]
        g_gains, g_biases = small[0:2], small[2:4]
        g_router = small[LOGIT_LANE : LOGIT_LANE + c.E]
    rows = (c.N, c.B, c.D)
    return (
        out.reshape(rows),
        g_tok.reshape(rows),
        g_qkv,
        g_out,
        g_router.T,
        g_gains,
        g_biases,
        g_in[None],
        g_down[None],
    )


def pack_small(c, w_router, norm_gains, norm_biases):
    rows = jnp.concatenate([norm_gains, norm_biases, w_router.T], axis=0).astype(F32)
    return jnp.pad(rows, ((0, c.r8 - rows.shape[0]), (0, 128 - rows.shape[1])))


def per_device(
    mesh_shape,
    tokens,
    lengths,
    route_ids,
    keep_mask,
    w_qkv,
    w_attn_out,
    w_router,
    norm_gains,
    norm_biases,
    w_expert_in,
    w_expert_down,
    cotangent,
):
    images, block, width = tokens.shape
    experts = mesh_shape["expert"] * w_expert_in.shape[0]
    c = types.SimpleNamespace(
        E=experts,
        Y=mesh_shape["dp"],
        C=mesh_shape["context"],
        N=images,
        B=block,
        D=width,
        T=images * block,
        S=mesh_shape["context"] * block,
        FF=w_expert_in.shape[2],
        FB=512,
        cap=max(2, 16 * block // (5 * experts)),
        sh=w_qkv.shape[0],
        r8=-(-(LOGIT_LANE + experts) // 8) * 8,
        scale=(width // HEADS) ** -0.5,
        chunks=4,
    )
    c.gather = c.sh % 32 == 0
    c.relay = experts == 4 and c.cap % 128 == 0
    tok = tokens.reshape(c.T, width)
    cot = cotangent.reshape(c.T, width)
    route = route_ids.transpose(0, 2, 1)
    keep = keep_mask.transpose(0, 2, 1)
    both = ("expert", "dp")
    if c.gather:
        given = (w_qkv, w_attn_out, pack_small(c, w_router, norm_gains, norm_biases))
    else:
        qkv = lax.all_gather(w_qkv, both, axis=0, tiled=True)
        out = lax.all_gather(w_attn_out, both, axis=0, tiled=True)
        small = pack_small(c, w_router, norm_gains, norm_biases)[:, : c.sh]
        vec = lax.all_gather(small, both, axis=1, tiled=True)
        stacked = jnp.concatenate([qkv, out], axis=1).reshape(width, 4, width).transpose(1, 0, 2)
        given = (stacked, vec)
    front = run_front(c, lengths, tok, route, keep, cot, given)
    weights, vec, q, kv, lse, att, hid, mix, meta, router, send, gsend, dyarr = front
    back = run_experts(c, send, gsend, dyarr, w_expert_in[0], w_expert_down[0])
    return run_back(
        c, tok, cot, lengths, weights, vec, q, kv, lse, att, hid, mix, meta, router, *back
    )


def solution(mesh):
    rows = P(("expert", "dp"), "context", None)
    shard = P(("expert", "dp"), None)
    column = P(None, ("expert", "dp"))
    expert = P("expert", None, None)
    return jax.shard_map(
        functools.partial(per_device, dict(mesh.shape)),
        mesh=mesh,
        in_specs=(rows, shard, rows, rows, shard, shard, shard, column, column, expert, expert, rows),
        out_specs=(
            rows,
            rows,
            shard,
            shard,
            shard,
            column,
            column,
            P("expert", None, ("context", "dp")),
            P("expert", ("context", "dp"), None),
        ),
        check_vma=False,
    )
```
